32 devices in a mesh: apa: 2 (over y), gz: 4 (over x, core), drift: 4 (over z).
Axes of the slice: x: 2, y: 2, z: 4, core: 2. Of those that a mesh axis runs over, the one named last changes fastest.
Arguments:
- charge: bfloat16 [16384, 384], P(('apa', 'gz', 'drift')), parts along dimension 0, may hold values from 0.049804688 to 2
- intersection: bfloat16 [128, 3, 2, 32, 128], P(('apa', 'gz', 'drift')), parts along dimension 0, may hold values from 0 to 0.03125
- ovl_block: int32 [128, 3, 2], P(('apa', 'gz', 'drift')), parts along dimension 0, may hold values from 0 to 15, as said below
- ovl_count: int32 [128, 3], P(('apa', 'gz', 'drift')), parts along dimension 0, may hold values from 1 to 2
- diff_class: int32 [768], P('apa'), parts along dimension 0, may hold values from 0 to 5
- response: bfloat16 [3, 21, 200], replicated, may hold values from -0.029907227 to 0.029907227
- cotangent: bfloat16 [6, 512, 3072], P('apa', 'gz', 'drift'), parts along dimension 0, may hold values from -120 to 120
Outputs:
- signal: bfloat16 [6, 512, 3072], P('apa', 'gz', 'drift'), parts along dimension 0
- charge_grad: bfloat16 [16384, 384], P(('apa', 'gz', 'drift')), parts along dimension 0
The draws below stay inside these ranges and needn't reach their ends.
There are 2 independent parts, one for each index of `apa`. The reference program is written for one: setup_inputs(seed, part) draws one part's arguments, and reference() takes and returns one part's arrays. A program takes and returns all parts, laid end to end along the dimension named above; an argument that names none is the same for every part. Nothing has to cross between parts.
Inputs may be any that keep to these rules, and one draw needn't show every extreme that they name: `ovl_block`: planes are U, V, W in this order. Cell block b lies in z-block b // 16; its W entries name wire blocks of that z-block, z-block g owning wire blocks g * 4 to (g + 1) * 4 - 1 of every plane. Entry 0 of each list is live. Among the live U and V entries of one group of 4 consecutive cell blocks (starting at a multiple of 4), at most 8 name wire blocks of one z-block, and every such group reaches 8 for some z-block. `ovl_count`: entry k of a list is live where k < count; the others are ignored.
All inputs are finite; a program needn't handle non-finite values.
Results may differ from the reference program's by a relative error of at most 0.0058.
Values may be sent and summed in bfloat16 or wider, within the bound.
No kernel may reach another device: no remote copies, remote signals or barrier semaphores. Data moves between devices by JAX's collectives and lax.ppermute only.
A program may use at most 128 MiB of HBM per device.

```python
import math
import jax
import jax.numpy as jnp
from jax import lax

WIRES = 512
TICKS = 3072
RESP_W = 21
RESP_T = 200
WB = 32
TPB = 8
HB = 2
K = 2
VB = 128
NDIFF = 6
NVB = 4
WBLK = 16
X = 384
VBLK = 64
CELLS = 8192
N_GZ = 4
N_DRIFT = 4


def draw_ovl_block(key, part):
    devices = N_GZ * N_DRIFT
    per_owner = WIRES // WB // N_GZ
    cap_limit = 8 * NVB // N_GZ
    other_count = N_GZ - 1
    key_hot, key_order, key_shift, key_cross, key_local = jax.random.split(jax.random.fold_in(key, 17), 5)
    hot_rows = jax.random.randint(key_hot, (N_DRIFT,), 0, N_GZ)
    device_ids = jnp.arange(devices, dtype=jnp.int32)
    z_block = device_ids // N_DRIFT
    hot_owner = hot_rows[device_ids % N_DRIFT][:, None]
    slot_order = jax.vmap(lambda single: jax.random.permutation(single, 2 * NVB))(jax.random.split(key_order, devices))
    slot_rank = jnp.argsort(slot_order, axis=1).astype(jnp.int32)
    owner_shift = jax.random.randint(key_shift, (devices, 1), 0, other_count)
    first_owner = jnp.where(slot_rank < cap_limit, hot_owner, (hot_owner + 1 + (slot_rank - cap_limit + owner_shift) % other_count) % N_GZ)
    later_index = 2 * NVB - cap_limit + jnp.arange(2 * NVB, dtype=jnp.int32)[None, :]
    second_owner = (hot_owner + 1 + (later_index + owner_shift) % other_count) % N_GZ
    owners = jnp.stack([first_owner, second_owner], axis=-1)
    cross_blocks = owners * per_owner + jax.random.randint(key_cross, owners.shape, 0, per_owner)
    cross_blocks = cross_blocks.reshape(devices, NVB, 2, 2)
    local_blocks = z_block[:, None, None, None] * per_owner + jax.random.randint(key_local, (devices, NVB, 1, 2), 0, per_owner)
    return jnp.concatenate([cross_blocks, local_blocks], axis=2).reshape(devices * NVB, 3, 2).astype(jnp.int32)


def place_ends(result, rng, smallest, largest):
    extent = result.shape
    place = [jax.random.randint(jax.random.fold_in(rng, axis), (), 0, extent[axis]) for axis in range(len(extent))]
    result = result.at[tuple(place)].set(smallest)
    longest = extent.index(max(extent))
    place[longest] = (place[longest] + 1) % extent[longest]
    return result.at[tuple(place)].set(largest)


def level_of(key, extent, cuts, least, largest):
    loudness = 1.0
    for position, blocks in cuts:
        draws = jax.random.uniform(jax.random.fold_in(jax.random.fold_in(key, 6), position), (blocks,), jnp.float32, least / len(cuts), largest / len(cuts))
        loudness = loudness * jnp.repeat(jnp.exp(draws), extent[position] // blocks).reshape((-1,) + (1,) * (len(extent) - 1 - position))
    return loudness


def gaussian(own_key, extent, scale, reach, cuts=(), kind=jnp.bfloat16):
    array = jax.random.normal(own_key, extent, jnp.float32) * scale
    if len(cuts) > 0:
        array = level_of(own_key, extent, cuts, -0.22, 0.18) * array
    return jnp.clip(array, min=-reach, max=reach).astype(kind)


def setup_inputs(seed: int = 0, part: int = 0) -> dict:
    arg_keys = jax.random.split(jax.random.key(seed), 8)
    own_keys = jax.random.split(jax.random.fold_in(arg_keys[7], part), 8)
    return {
        "charge": jnp.clip(jnp.exp(math.log(2.0) - 3.6927934 * jax.random.uniform(own_keys[0], (CELLS, X), jnp.float32) ** level_of(own_keys[0], (CELLS, X), ((0, 16),), -0.2, 0.2)), 0.049804688, 2.0).astype(jnp.bfloat16),
        "intersection": jnp.clip(0.03125 * jax.random.uniform(own_keys[1], (VBLK, 3, K, WB, VB), jnp.float32) ** level_of(own_keys[1], (VBLK, 3, K, WB, VB), ((0, 16),), -0.2, 0.2), 0.0, 0.03125).astype(jnp.bfloat16),
        "ovl_block": draw_ovl_block(jax.random.fold_in(jax.random.fold_in(arg_keys[7], part), 71), part),
        "ovl_count": place_ends(jax.random.randint(own_keys[3], (VBLK, 3), 1, K + 1), jax.random.fold_in(own_keys[3], 1), 1, K).astype(jnp.int32),
        "diff_class": place_ends(jax.random.randint(own_keys[4], (X,), 0, NDIFF), jax.random.fold_in(own_keys[4], 1), 0, NDIFF - 1).astype(jnp.int32),
        "response": gaussian(arg_keys[5], (3, RESP_W, RESP_T), 0.005, 0.029907227),
        "cotangent": gaussian(own_keys[6], (3, WIRES, TICKS), 20.0, 120.0, ((1, 4), (2, 4))),
    }


def smear_weights(offset, classes):
    spread_width = TPB * (0.2 + 0.15 * classes)
    reach_ticks = HB * TPB
    samples = jnp.arange(-reach_ticks, reach_ticks).astype(jnp.float32) + 0.5
    normalizer = jnp.sum(jnp.exp(-(samples * samples) / (2.0 * spread_width[..., None] * spread_width[..., None])), axis=-1)
    inside = jnp.abs(offset) < reach_ticks
    bump = jnp.exp(-(offset * offset) / (2.0 * spread_width * spread_width))
    return jnp.where(inside, bump, jnp.zeros_like(bump)) / normalizer


def planes_conv(field, kernel, padding):
    return lax.conv_general_dilated(field[None], kernel[:, None], (1, 1), padding, dimension_numbers=("NCHW", "OIHW", "NCHW"), feature_group_count=3, precision=lax.Precision.HIGHEST)[0]


def reference(charge, intersection, ovl_block, ovl_count, diff_class, response, cotangent):
    highest = lax.Precision.HIGHEST
    entry_live = jnp.arange(K, dtype=jnp.int32)[None, None, :] < ovl_count[:, :, None]
    weights = intersection.astype(jnp.float32)
    charge_blocks = charge.reshape(VBLK, VB, X).astype(jnp.float32)
    pieces = jnp.einsum("bpkwc,bcx->bpkwx", weights, charge_blocks, precision=highest).astype(jnp.bfloat16)
    pieces = jnp.where(entry_live[:, :, :, None, None], pieces, jnp.zeros((), jnp.bfloat16))
    plane_of = jnp.broadcast_to(jnp.arange(3, dtype=jnp.int32)[None, :, None], ovl_block.shape)
    target = (plane_of * WBLK + ovl_block).reshape(-1).astype(jnp.int32)
    currents = jax.ops.segment_sum(pieces.reshape(VBLK * 3 * K, WB, X).astype(jnp.float32), target, num_segments=3 * WBLK)
    currents = currents.reshape(3, WIRES, X)
    bin_index = jnp.arange(X).astype(jnp.float32)
    tick_index = jnp.arange(TICKS).astype(jnp.float32)
    offset = tick_index[None, :] - TPB * bin_index[:, None] - (TPB - 1) / 2.0
    smear_table = smear_weights(offset, diff_class.astype(jnp.float32)[:, None])
    drifted = jnp.einsum("pwx,xt->pwt", currents, smear_table, precision=highest).astype(jnp.bfloat16)
    half_width = (RESP_W - 1) // 2
    response_wide = response.astype(jnp.float32)
    signal = planes_conv(drifted.astype(jnp.float32), response_wide[:, :, ::-1], [(half_width, half_width), (RESP_T - 1, 0)]).astype(jnp.bfloat16)
    tick_grads = planes_conv(cotangent.astype(jnp.float32), response_wide[:, ::-1, :], [(half_width, half_width), (0, RESP_T - 1)]).astype(jnp.bfloat16)
    bin_grads = jnp.einsum("pwt,xt->pwx", tick_grads.astype(jnp.float32), smear_table, precision=highest).astype(jnp.bfloat16)
    blocks = bin_grads.reshape(3 * WBLK, WB, X)
    chosen = jnp.take(blocks, target, axis=0).reshape(VBLK, 3, K, WB, X)
    chosen = jnp.where(entry_live[:, :, :, None, None], chosen, jnp.zeros((), jnp.bfloat16))
    charge_grad = jnp.einsum("bpkwc,bpkwx->bcx", weights, chosen.astype(jnp.float32), precision=highest)
    return signal, charge_grad.reshape(CELLS, X).astype(jnp.bfloat16)
```

```python
import functools
import math

import jax
import jax.numpy as jnp
from jax import lax
from jax.experimental import pallas as pl
from jax.experimental.pallas import tpu as pltpu
from jax.sharding import PartitionSpec as P

TPB = 8
HB = 2
CLASSES = 6
LANES = 128
EDGE = 16
GROUP = 8
WINDOW = 64
LEAD = HB * TPB - TPB // 2
VMEM_LIMIT = 48 * 1024 * 1024
BF16 = jnp.bfloat16
F32 = jnp.float32


def params(semantics=None):
    return pltpu.CompilerParams(vmem_limit_bytes=VMEM_LIMIT, dimension_semantics=semantics)


def vmem():
    return pl.BlockSpec(memory_space=pltpu.VMEM)


def smem():
    return pl.BlockSpec(memory_space=pltpu.SMEM)


def cost(flops, moved):
    return pl.CostEstimate(flops=int(flops), bytes_accessed=int(moved), transcendentals=0)


def swap(block, axis, distance):
    count = lax.axis_size(axis)
    return lax.ppermute(block, axis, [(i, i ^ distance) for i in range(count)])


def widths(number):
    spread = TPB * (0.2 + 0.15 * number)
    half = HB * TPB
    total = sum(math.exp(-((j + 0.5) ** 2) / (2.0 * spread * spread)) for j in range(-half, half))
    return 1.0 / (2.0 * spread * spread), 1.0 / total


def shared_lanes(left, right, shift, lane):
    if shift == 0:
        return left
    back = LANES - shift
    return jnp.where(lane < back, pltpu.roll(left, back, 1), pltpu.roll(right, back, 1))


def table_kernel(class_ref, response_ref, table_ref, taps_ref, smeared_ref, *, tiles, blocks, bins):
    planes, wire_taps, length = response_ref.shape
    plane = pl.program_id(0)
    reach = taps_ref.shape[1]
    rows = taps_ref.shape[0] // planes
    first = lax.axis_index("drift") * bins - (WINDOW // 2 - HB)

    @pl.when(plane == 0)
    def _():
        taps_ref[...] = jnp.zeros(taps_ref.shape, F32)
        for p in range(planes):
            taps_ref[p * rows : p * rows + wire_taps, :length] = response_ref[p].astype(F32)
        taps = taps_ref[...].astype(BF16)
        tap = lax.broadcasted_iota(jnp.int32, (reach, reach), 0)
        tick = lax.broadcasted_iota(jnp.int32, (reach, reach), 1)
        step = tick - tap - LEAD
        offset = step.astype(F32) - (TPB - 1) / 2.0
        squared = offset * offset
        inside = jnp.abs(offset) < HB * TPB
        for kind in range(CLASSES + HB):
            keep = inside
            if kind < CLASSES:
                narrow, scale = widths(kind)
            else:
                edge = kind - CLASSES
                narrow, scale = widths(0)
                for number in range(1, CLASSES):
                    chosen = class_ref[edge] == number
                    narrow = jnp.where(chosen, widths(number)[0], narrow)
                    scale = jnp.where(chosen, widths(number)[1], scale)
                keep = inside & (step >= -TPB * edge)
            smear = jnp.where(keep, jnp.exp(-(squared * narrow)) * scale, 0.0)
            high = smear.astype(BF16)
            low = (smear - high.astype(F32)).astype(BF16)
            smeared_ref[kind] = jnp.dot(taps, high, preferred_element_type=F32) + jnp.dot(
                taps, low, preferred_element_type=F32
            )

    lane = lax.broadcasted_iota(jnp.int32, (GROUP, LANES), 1)
    row = lax.broadcasted_iota(jnp.int32, (GROUP, LANES), 0)
    groups = (bins + WINDOW // 2) // GROUP
    last = class_ref.shape[0] - 1
    kinds = []
    for m in range(groups):
        kind = jnp.zeros((GROUP, LANES), jnp.int32)
        for i in range(GROUP):
            x = first + m * GROUP + i
            number = class_ref[jnp.clip(x, 0, last)]
            number = jnp.where((x >= 0) & (x < HB), CLASSES + x, number)
            kind = jnp.where(row == i, number, kind)
        kinds.append(kind)
    edge_group = (WINDOW // 2 - HB) // GROUP
    starts = [LEAD_SHIFT + odd * (LANES // 2) + TPB * row for odd in range(2)]
    after = [lane >= start for start in starts]
    zero = jnp.zeros((GROUP, LANES), F32)
    empty = jnp.zeros((2 * GROUP, LANES), BF16)

    def body(a, _):
        line = plane * rows + a
        levels = []
        for kind in range(CLASSES + HB):
            values = smeared_ref[kind, pl.ds(line, 1), :]
            levels.append(
                [
                    jnp.broadcast_to(values[:, part * LANES : (part + 1) * LANES], (GROUP, LANES))
                    for part in range(2)
                ]
            )
        pieces = {}
        for m in range(groups):
            odd = m % 2
            parts = []
            for part in range(2):
                picked = levels[0][part]
                for kind in range(1, CLASSES + (HB if m == edge_group else 0)):
                    picked = jnp.where(kinds[m] == kind, levels[kind][part], picked)
                parts.append(
                    pltpu.roll(
                        picked, LEAD_SHIFT + odd * (LANES // 2), 1, stride=TPB, stride_axis=0
                    )
                )
            pieces[m] = (
                jnp.where(after[odd], parts[0], zero),
                jnp.where(after[odd], parts[1], parts[0]),
                jnp.where(after[odd], zero, parts[1]),
            )
        for block in range(blocks):
            for quarter in range(WINDOW // (2 * GROUP)):
                m = 2 * (tiles * block + quarter)
                at = pl.ds(pl.multiple_of(a * WINDOW + quarter * 2 * GROUP, 2 * GROUP), 2 * GROUP)
                for tile in range(tiles):
                    third = tile - quarter + 2
                    if 0 <= third <= 2 and m + 1 < groups:
                        value = jnp.concatenate(
                            [pieces[m][third], pieces[m + 1][third]], axis=0
                        ).astype(BF16)
                    else:
                        value = empty
                    table_ref[0, block, at, tile * LANES : (tile + 1) * LANES] = value
        return 0

    lax.fori_loop(0, wire_taps, body, 0)
    spare = table_ref.shape[2] - wire_taps * WINDOW
    for block in range(blocks):
        table_ref[0, block, wire_taps * WINDOW :, :] = jnp.zeros(
            (spare, tiles * LANES), BF16
        )


LEAD_SHIFT = (TPB * HB - LEAD) % LANES


def build_table(diff_class, response, ticks_here, bins):
    planes, wire_taps, length = response.shape
    tiles = math.gcd(ticks_here, 2 * LANES) // LANES
    blocks = ticks_here // (tiles * LANES)
    reach = 2 * LANES
    rows = -(-wire_taps // 8) * 8
    depth = (wire_taps + wire_taps % 2) * WINDOW
    shape = (planes, blocks, depth, tiles * LANES)
    return pl.pallas_call(
        functools.partial(table_kernel, tiles=tiles, blocks=blocks, bins=bins),
        grid=(planes,),
        out_shape=jax.ShapeDtypeStruct(shape, BF16),
        in_specs=[smem(), pl.BlockSpec(response.shape, lambda p: (0, 0, 0))],
        out_specs=pl.BlockSpec((1,) + shape[1:], lambda p: (p, 0, 0, 0)),
        scratch_shapes=[
            pltpu.VMEM((planes * rows, reach), F32),
            pltpu.VMEM((CLASSES + HB, planes * rows, reach), F32),
        ],
        compiler_params=params(("arbitrary",)),
        cost_estimate=cost(4e9, 2 * math.prod(shape)),
        name="table",
    )(diff_class, response)


def back_kernel(table_ref, own_ref, low_ref, high_ref, out_ref, cot_ref, wide_ref, sum_ref, *, wire_taps):
    blocks, span = table_ref.shape[1], table_ref.shape[3]
    wires = own_ref.shape[1]
    half = (wire_taps - 1) // 2
    cot_ref[:EDGE] = low_ref[0]
    cot_ref[EDGE : EDGE + wires] = own_ref[0]
    cot_ref[EDGE + wires :] = high_ref[0]
    sum_ref[...] = jnp.zeros(sum_ref.shape, F32)
    depth = wire_taps * WINDOW
    extent = cot_ref.shape[0]
    lane = lax.broadcasted_iota(jnp.int32, (WINDOW, LANES), 1)
    step = span * 16 // LANES
    for block in range(blocks):
        wide_ref[:, :extent] = lax.dot_general(
            table_ref[0, block, :depth],
            cot_ref[:, block * span : (block + 1) * span],
            (((1,), (1,)), ((), ())),
            preferred_element_type=F32,
        )
        total = sum_ref[block * step : block * step + WINDOW]
        for a in range(wire_taps):
            part = wide_ref[a * WINDOW : (a + 1) * WINDOW, :]
            total += shared_lanes(
                part[:, :LANES], part[:, LANES:], EDGE + half - a, lane
            )
        sum_ref[block * step : block * step + WINDOW] = total
    out_ref[0] = sum_ref[: out_ref.shape[1], :wires].astype(BF16)


def backward(table, cotangent, low, high, wire_taps, bins):
    planes, blocks, depth, span = table.shape
    _, wires, ticks = cotangent.shape
    extent = wires + 2 * EDGE
    window = bins + WINDOW // 2
    sums = (blocks - 1) * (span * 16 // LANES) + WINDOW
    edge = pl.BlockSpec((1, EDGE, ticks), lambda p: (p, 0, 0))
    return pl.pallas_call(
        functools.partial(back_kernel, wire_taps=wire_taps),
        grid=(planes,),
        out_shape=jax.ShapeDtypeStruct((planes, window, wires), BF16),
        in_specs=[
            pl.BlockSpec((1, blocks, depth, span), lambda p: (p, 0, 0, 0)),
            pl.BlockSpec((1, wires, ticks), lambda p: (p, 0, 0)),
            edge,
            edge,
        ],
        out_specs=pl.BlockSpec((1, window, wires), lambda p: (p, 0, 0)),
        scratch_shapes=[
            pltpu.VMEM((extent, ticks), BF16),
            pltpu.VMEM((wire_taps * WINDOW, 2 * LANES), F32),
            pltpu.VMEM((sums, LANES), F32),
        ],
        compiler_params=params(("arbitrary",)),
        cost_estimate=cost(4e9, 2 * math.prod(table.shape)),
        name="bin_gradients",
    )(table, cotangent, low, high)


def merge_kernel(*refs, bins, lead):
    parts, (cross_ref, local_ref, sum_ref) = refs[:-3], refs[-3:]
    planes, window, wires = parts[0].shape
    total = local_ref.shape[1]
    slab = lax.axis_index("drift")
    sum_ref[...] = jnp.zeros(sum_ref.shape, F32)
    for k, part in enumerate(parts):
        at = pl.ds(pl.multiple_of((slab ^ k) * bins, 8), window)
        for p in range(planes):
            sum_ref[p, at, :wires] += part[p].astype(F32)
    for p in range(planes):
        for tile in range(total // LANES):
            turned = sum_ref[p, lead + tile * LANES : lead + (tile + 1) * LANES, :].T
            here = slice(tile * LANES, (tile + 1) * LANES)
            if p < planes - 1:
                cross_ref[p, :, here] = turned[:wires].astype(BF16)
            else:
                local_ref[:, here] = turned[:wires].astype(BF16)


def merge(parts, bins, total):
    planes, window, wires = parts[0].shape
    lead = WINDOW // 2 - HB
    return pl.pallas_call(
        functools.partial(merge_kernel, bins=bins, lead=lead),
        out_shape=(
            jax.ShapeDtypeStruct((planes - 1, wires, total), BF16),
            jax.ShapeDtypeStruct((wires, total), BF16),
        ),
        in_specs=[vmem()] * len(parts),
        out_specs=(vmem(), vmem()),
        scratch_shapes=[pltpu.VMEM((planes, total + WINDOW // 2, LANES), F32)],
        compiler_params=params(),
        cost_estimate=cost(1e8, 4 * planes * wires * total),
        name="merge_bins",
    )(*parts)


def charge_kernel(block_ref, count_ref, cross_ref, local_ref, share_ref, out_ref, chosen_ref):
    cells, planes, entries, wire_block, width = share_ref.shape
    per_owner = cross_ref.shape[2] // wire_block
    owners = cross_ref.shape[0]
    z = lax.axis_index("gz")
    empty = jnp.zeros((wire_block, out_ref.shape[1]), BF16)
    for b in range(cells):
        for p in range(planes):
            for k in range(entries):
                name = block_ref[b, p, k]
                if p < planes - 1:
                    name = jnp.clip(name, 0, owners * per_owner - 1)
                    owner = name // per_owner
                    start = pl.multiple_of((name - owner * per_owner) * wire_block, wire_block)
                    rows = cross_ref[owner, p, pl.ds(start, wire_block), :]
                else:
                    name = jnp.clip(name - z * per_owner, 0, per_owner - 1)
                    start = pl.multiple_of(name * wire_block, wire_block)
                    rows = local_ref[pl.ds(start, wire_block), :]
                at = ((b * planes + p) * entries + k) * wire_block
                chosen_ref[at : at + wire_block] = jnp.where(k < count_ref[b, p], rows, empty)
    depth = planes * entries * wire_block
    for b in range(cells):
        out_ref[b * width : (b + 1) * width] = lax.dot_general(
            share_ref[b].reshape(depth, width),
            chosen_ref[b * depth : (b + 1) * depth],
            (((0,), (0,)), ((), ())),
            preferred_element_type=F32,
        ).astype(BF16)


def charge_gradient(ovl_block, ovl_count, cross, local, intersection):
    cells, planes, entries, wire_block, width = intersection.shape
    total = local.shape[1]
    return pl.pallas_call(
        charge_kernel,
        out_shape=jax.ShapeDtypeStruct((cells * width, total), BF16),
        in_specs=[smem(), smem(), vmem(), vmem(), vmem()],
        out_specs=vmem(),
        scratch_shapes=[pltpu.VMEM((cells * planes * entries * wire_block, total), BF16)],
        compiler_params=params(),
        cost_estimate=cost(1e8, 2 * math.prod(cross.shape)),
        name="charge_gradient",
    )(ovl_block, ovl_count, cross, local, intersection)


def pieces_kernel(block_ref, count_ref, charge_ref, share_ref, keep_ref, give_ref, local_ref, cross_ref):
    cells, planes, entries, wire_block, width = share_ref.shape
    wires, total = local_ref.shape
    per_owner = wires // wire_block
    owners = 2 * keep_ref.shape[0]
    z = lax.axis_index("gz")
    cross_ref[...] = jnp.zeros(cross_ref.shape, F32)
    local_ref[...] = jnp.zeros(local_ref.shape, F32)
    depth = planes * entries * wire_block
    for b in range(cells):
        pieces = (
            jnp.dot(
                share_ref[b].reshape(depth, width),
                charge_ref[b * width : (b + 1) * width],
                preferred_element_type=F32,
            )
            .astype(BF16)
            .astype(F32)
        )
        for p in range(planes):
            for k in range(entries):
                at = (p * entries + k) * wire_block
                piece = pieces[at : at + wire_block]
                piece = jnp.where(k < count_ref[b, p], piece, jnp.zeros_like(piece))
                name = block_ref[b, p, k]
                if p < planes - 1:
                    name = jnp.clip(name, 0, owners * per_owner - 1)
                    start = pl.multiple_of(EDGE + name * wire_block, EDGE)
                    cross_ref[p, pl.ds(start, wire_block)] += piece
                else:
                    name = jnp.clip(name - z * per_owner, 0, per_owner - 1)
                    start = pl.multiple_of(name * wire_block, wire_block)
                    local_ref[pl.ds(start, wire_block)] += piece
    extent = wires + 2 * EDGE
    edge = (planes - 1) * extent
    none = jnp.zeros((EDGE, total), F32)
    for k in range(owners):
        to = z ^ k
        out = (give_ref if k % 2 else keep_ref).at[k // 2]
        for p in range(planes - 1):
            rows = cross_ref[p, pl.ds(pl.multiple_of(to * wires, EDGE), extent)]
            out[p * extent : (p + 1) * extent] = rows.astype(BF16)
        below = jnp.where(to == z + 1, local_ref[wires - EDGE :], none)
        above = jnp.where(to == z - 1, local_ref[:EDGE], none)
        out[edge : edge + EDGE] = below.astype(BF16)
        out[edge + EDGE : edge + 2 * EDGE] = above.astype(BF16)


def cut_pieces(ovl_block, ovl_count, charge, intersection, wires, owners):
    cells, planes, entries, wire_block, width = intersection.shape
    total = charge.shape[1]
    rows = (planes - 1) * (wires + 2 * EDGE) + 2 * EDGE
    cut = jax.ShapeDtypeStruct((owners // 2, rows, total), BF16)
    return pl.pallas_call(
        pieces_kernel,
        out_shape=(cut, cut, jax.ShapeDtypeStruct((wires, total), F32)),
        in_specs=[smem(), smem(), vmem(), vmem()],
        out_specs=(vmem(), vmem(), vmem()),
        scratch_shapes=[pltpu.VMEM((planes - 1, owners * wires + 2 * EDGE, total), F32)],
        compiler_params=params(),
        cost_estimate=cost(1e8, 4 * owners * rows * total),
        name="pieces",
    )(ovl_block, ovl_count, charge, intersection)


def slabs_kernel(*refs, bins, lead, slabs):
    count = len(refs) - slabs - 1
    parts, local_ref = refs[: count - 1], refs[count - 1]
    outs, cut_ref = refs[count:-1], refs[-1]
    wires, total = local_ref.shape
    extent = wires + 2 * EDGE
    summed = parts[0][...].astype(F32)
    for part in parts[1:]:
        summed += part[...].astype(F32)
    summed = summed.reshape(summed.shape[-2:])
    edge = summed.shape[0] - 2 * EDGE
    rows = jnp.concatenate(
        [summed[:edge], summed[edge : edge + EDGE], local_ref[...], summed[edge + EDGE :]], axis=0
    )
    none = jnp.zeros((rows.shape[0], LANES), F32)
    lane = lax.broadcasted_iota(jnp.int32, none.shape, 1)
    tiles = [rows[:, t * LANES : (t + 1) * LANES] for t in range(total // LANES)]
    for to in range(slabs):
        at = to * bins - lead
        tile, shift = at // LANES, at % LANES
        pair = [tiles[t] if 0 <= t < len(tiles) else none for t in (tile, tile + 1)]
        cut_ref[to] = shared_lanes(pair[0], pair[1], shift, lane).astype(BF16)
    slab = lax.axis_index("drift")
    for k, out in enumerate(outs):
        out[...] = cut_ref[slab ^ k]


def cut_slabs(keep, received, others, local, bins, slabs):
    wires, total = local.shape
    rows = keep.shape[1] + wires
    lead = WINDOW // 2 - HB
    block = pl.BlockSpec((1,) + keep.shape[1:], lambda i: (0, 0, 0))
    cut = jax.ShapeDtypeStruct((rows, LANES), BF16)
    return pl.pallas_call(
        functools.partial(slabs_kernel, bins=bins, lead=lead, slabs=slabs),
        grid=(1,),
        out_shape=(cut,) * slabs,
        in_specs=[block, block]
        + [pl.BlockSpec(other.shape, lambda i: (0, 0)) for other in others]
        + [pl.BlockSpec(local.shape, lambda i: (0, 0))],
        out_specs=(pl.BlockSpec(cut.shape, lambda i: (0, 0)),) * slabs,
        scratch_shapes=[pltpu.VMEM((slabs, rows, LANES), BF16)],
        compiler_params=params(("arbitrary",)),
        cost_estimate=cost(1e8, 4 * rows * total),
        name="slab_currents",
    )(keep, received, *others, local)


def signal_kernel(*refs, wire_taps):
    parts, (table_ref, out_ref, even_ref, odd_ref, lines_ref) = refs[:-5], refs[-5:]
    blocks, span = table_ref.shape[1], table_ref.shape[3]
    wires = out_ref.shape[1]
    half = (wire_taps - 1) // 2
    step = span * 16 // LANES
    currents = parts[0][...].astype(F32)
    for part in parts[1:]:
        currents += part[...].astype(F32)
    lane = lax.broadcasted_iota(jnp.int32, (wires, LANES), 1)
    for block in range(blocks):
        even_ref[...] = pltpu.roll(currents, (-step * block) % LANES, 1)
        odd_ref[...] = pltpu.roll(currents, (WINDOW - step * block) % LANES, 1)
        for pair in range((wire_taps + 1) // 2):
            at = EDGE - half + 2 * pair
            line = jnp.where(
                lane < WINDOW, even_ref[at : at + wires], odd_ref[at + 1 : at + 1 + wires]
            )
            lines_ref[:, pair * LANES : (pair + 1) * LANES] = line.astype(BF16)
        out_ref[0, :, block * span : (block + 1) * span] = jnp.dot(
            lines_ref[...], table_ref[0, block], preferred_element_type=F32
        ).astype(BF16)


def forward(parts, table, wires, wire_taps):
    planes, blocks, depth, span = table.shape
    extent = wires + 2 * EDGE
    part = pl.BlockSpec((extent, LANES), lambda p: (p, 0))
    return pl.pallas_call(
        functools.partial(signal_kernel, wire_taps=wire_taps),
        grid=(planes,),
        out_shape=jax.ShapeDtypeStruct((planes, wires, blocks * span), BF16),
        in_specs=[part] * len(parts)
        + [pl.BlockSpec((1, blocks, depth, span), lambda p: (p, 0, 0, 0))],
        out_specs=pl.BlockSpec((1, wires, blocks * span), lambda p: (p, 0, 0)),
        scratch_shapes=[
            pltpu.VMEM((extent, LANES), F32),
            pltpu.VMEM((extent, LANES), F32),
            pltpu.VMEM((wires, depth), BF16),
        ],
        compiler_params=params(("arbitrary",)),
        cost_estimate=cost(4e9, 2 * math.prod(table.shape)),
        name="signal",
    )(*parts, table)


def local(charge, intersection, ovl_block, ovl_count, diff_class, response, cotangent):
    total = charge.shape[1]
    owners = lax.axis_size("gz")
    slabs = lax.axis_size("drift")
    _, wires, ticks = cotangent.shape
    wire_taps = response.shape[1]
    bins = total // slabs

    up = [(i, i + 1) for i in range(owners - 1)]
    down = [(i + 1, i) for i in range(owners - 1)]
    low = lax.ppermute(cotangent[:, wires - EDGE :], "gz", up)
    high = lax.ppermute(cotangent[:, :EDGE], "gz", down)

    keep, give, local_currents = cut_pieces(
        ovl_block, ovl_count, charge, intersection, wires, owners
    )
    received = swap(give, "gz", 1)

    table = build_table(diff_class, response, ticks, bins)
    partial = backward(table, cotangent, low, high, wire_taps, bins)

    others = []
    if owners > 2:
        sums = (keep[1:].astype(F32) + received[1:].astype(F32)).astype(BF16)
        others = [swap(sums[j - 1], "gz", 2 * j) for j in range(1, owners // 2)]

    spread = [partial] + [swap(partial, "drift", k) for k in range(1, slabs)]
    cross, own = merge(spread, bins, total)
    every = lax.all_gather(cross, "gz", axis=0)
    charge_grad = charge_gradient(ovl_block, ovl_count, every, own, intersection)

    cuts = cut_slabs(keep, received, others, local_currents, bins, slabs)
    windows = [cuts[0]] + [swap(cuts[k], "drift", k) for k in range(1, slabs)]
    signal = forward(windows, table, wires, wire_taps)
    return signal, charge_grad


def solution(mesh):
    return jax.shard_map(
        local,
        mesh=mesh,
        in_specs=(
            P(("apa", "gz", "drift"), None),
            P(("apa", "gz", "drift"), None, None, None, None),
            P(("apa", "gz", "drift"), None, None),
            P(("apa", "gz", "drift"), None),
            P("apa"),
            P(),
            P("apa", "gz", "drift"),
        ),
        out_specs=(P("apa", "gz", "drift"), P(("apa", "gz", "drift"), None)),
        check_vma=False,
    )
```

```python
import functools
import math

import jax
import jax.numpy as jnp
from jax import lax
from jax.experimental import pallas as pl
from jax.experimental.pallas import tpu as pltpu
from jax.sharding import PartitionSpec as P

TPB = 8
HB = 2
CLASSES = 6
LANES = 128
EDGE = 16
GROUP = 8
WINDOW = 64
LEAD = HB * TPB - TPB // 2
VMEM_LIMIT = 24 * 1024 * 1024
WHOLE_VMEM = 61 * 1024 * 1024
BF16 = jnp.bfloat16
F32 = jnp.float32


def params(semantics=None, limit=VMEM_LIMIT):
    return pltpu.CompilerParams(vmem_limit_bytes=limit, dimension_semantics=semantics)


def vmem():
    return pl.BlockSpec(memory_space=pltpu.VMEM)


def smem():
    return pl.BlockSpec(memory_space=pltpu.SMEM)


def anywhere():
    return pl.BlockSpec(memory_space=pl.ANY)


def cost(flops, moved):
    return pl.CostEstimate(flops=int(flops), bytes_accessed=int(moved), transcendentals=0)


def swap(block, axis, distance):
    count = lax.axis_size(axis)
    return lax.ppermute(block, axis, [(i, i ^ distance) for i in range(count)])


def widths(number):
    spread = TPB * (0.2 + 0.15 * number)
    half = HB * TPB
    total = sum(math.exp(-((j + 0.5) ** 2) / (2.0 * spread * spread)) for j in range(-half, half))
    return 1.0 / (2.0 * spread * spread), 1.0 / total


def shared_lanes(left, right, shift, lane):
    if shift == 0:
        return left
    back = LANES - shift
    return jnp.where(lane < back, pltpu.roll(left, back, 1), pltpu.roll(right, back, 1))


def coded(rows, column):
    lane = lax.broadcasted_iota(jnp.int32, rows.shape, 1)
    level = jnp.broadcast_to(rows[:, column : column + 1].astype(BF16).astype(F32), rows.shape)
    return jnp.where(lane == 0, level, rows - level).astype(BF16)


def plain(rows, first):
    rows = rows.astype(F32)
    lane = lax.broadcasted_iota(jnp.int32, rows.shape, 1)
    level = jnp.broadcast_to(rows[:, :1], rows.shape)
    return jnp.where(lane == 0, level if first else jnp.zeros_like(rows), rows + level)


def levels_kernel(class_ref, response_ref, _, level_ref, kind_ref, flat_ref, *, bins):
    planes, wire_taps, length = response_ref.shape
    rows = level_ref.shape[0] // planes
    groups = kind_ref.shape[0]
    row = lax.broadcasted_iota(jnp.int32, (GROUP, LANES), 0)
    first = lax.axis_index("drift") * bins - (WINDOW // 2 - HB)
    last = class_ref.shape[0] - 1
    for m in range(groups):
        kind = jnp.zeros((GROUP, LANES), jnp.int32)
        for i in range(GROUP):
            x = first + m * GROUP + i
            number = class_ref[jnp.clip(x, 0, last)]
            number = jnp.where((x >= 0) & (x < HB), CLASSES + x, number)
            kind = jnp.where(row == i, number, kind)
        kind_ref[m] = kind
    flat_ref[...] = jnp.zeros(flat_ref.shape, F32)
    for p in range(planes):
        flat_ref[p * rows : p * rows + wire_taps, :length] = response_ref[p].astype(F32)
    taps = flat_ref[...].astype(BF16)
    tap = lax.broadcasted_iota(jnp.int32, (LANES, 2 * LANES), 0)
    tick = lax.broadcasted_iota(jnp.int32, (LANES, 2 * LANES), 1)
    step = tick - tap - LEAD
    offset = step.astype(F32) - (TPB - 1) / 2.0
    squared = offset * offset
    inside = jnp.abs(offset) < HB * TPB
    for kind in range(CLASSES + HB):
        keep = inside
        if kind < CLASSES:
            narrow, scale = widths(kind)
        else:
            edge = kind - CLASSES
            narrow, scale = widths(0)
            for number in range(1, CLASSES):
                chosen = class_ref[edge] == number
                narrow = jnp.where(chosen, widths(number)[0], narrow)
                scale = jnp.where(chosen, widths(number)[1], scale)
            keep = inside & (step >= -TPB * edge)
        smear = jnp.where(keep, jnp.exp(-(squared * narrow)) * scale, 0.0)
        high = smear.astype(BF16)
        low = (smear - high.astype(F32)).astype(BF16)
        near = jnp.dot(taps[:, :LANES], high, preferred_element_type=F32) + jnp.dot(
            taps[:, :LANES], low, preferred_element_type=F32
        )
        far = jnp.dot(taps[:, LANES:], high[:, :LANES], preferred_element_type=F32) + jnp.dot(
            taps[:, LANES:], low[:, :LANES], preferred_element_type=F32
        )
        level_ref[:, kind, :LANES] = near[:, :LANES]
        level_ref[:, kind, LANES:] = near[:, LANES:] + far


def smeared_levels(diff_class, response, bins, before):
    planes, wire_taps, _ = response.shape
    rows = -(-wire_taps // 8) * 8
    groups = (bins + WINDOW // 2) // GROUP
    return pl.pallas_call(
        functools.partial(levels_kernel, bins=bins),
        out_shape=(
            jax.ShapeDtypeStruct((planes * rows, CLASSES + HB, 2 * LANES), F32),
            jax.ShapeDtypeStruct((groups, GROUP, LANES), jnp.int32),
        ),
        in_specs=[smem(), vmem(), anywhere()],
        out_specs=(vmem(), vmem()),
        scratch_shapes=[pltpu.VMEM((planes * rows, 2 * LANES), F32)],
        compiler_params=params(),
        cost_estimate=cost(1e8, 1e6),
        name="levels",
    )(diff_class, response, before)


def table_kernel(level_ref, kind_ref, table_ref, sum_ref, *, wire_taps):
    planes, blocks, depth, span = table_ref.shape
    rows = level_ref.shape[0] // planes
    groups = kind_ref.shape[0]
    tiles = span // LANES
    lane = lax.broadcasted_iota(jnp.int32, (GROUP, LANES), 1)
    row = lax.broadcasted_iota(jnp.int32, (GROUP, LANES), 0)
    starts = [LEAD_SHIFT + odd * (LANES // 2) + TPB * row for odd in range(2)]
    after = [lane >= start for start in starts]
    zero = jnp.zeros((GROUP, LANES), F32)
    empty = jnp.zeros((2 * GROUP, LANES), BF16)

    def body(a, plane):
        levels = level_ref[plane * rows + a]
        halves = [levels[:, :LANES], levels[:, LANES:]]
        pieces = []
        for m in range(groups):
            odd = m % 2
            parts = [
                pltpu.roll(
                    jnp.take_along_axis(half, kind_ref[m], axis=0),
                    LEAD_SHIFT + odd * (LANES // 2),
                    1,
                    stride=TPB,
                    stride_axis=0,
                )
                for half in halves
            ]
            pieces.append(
                (
                    jnp.where(after[odd], parts[0], zero),
                    jnp.where(after[odd], parts[1], parts[0]),
                    jnp.where(after[odd], zero, parts[1]),
                )
            )
        for block in range(blocks):
            for tile in range(tiles):
                here = slice(tile * LANES, (tile + 1) * LANES)
                total = zero
                for quarter in range(WINDOW // (2 * GROUP)):
                    m = 2 * (tiles * block + quarter)
                    at = a * WINDOW + quarter * 2 * GROUP
                    at = pl.ds(pl.multiple_of(at, 2 * GROUP), 2 * GROUP)
                    third = tile - quarter + 2
                    value = empty
                    if 0 <= third <= 2 and m + 1 < groups:
                        value = jnp.concatenate(
                            [pieces[m][third], pieces[m + 1][third]], axis=0
                        ).astype(BF16)
                        total = total + pieces[m][third] + pieces[m + 1][third]
                    table_ref[plane, block, at, here] = value
                sum_ref[a, block, :, here] = total
        return plane

    def whole_plane(plane, _):
        lax.fori_loop(0, wire_taps, body, plane, unroll=UNROLL)
        for block in range(blocks):
            total = jnp.sum(sum_ref[:, block], axis=1)
            high = total.astype(BF16).astype(F32)
            spare = jnp.zeros((depth - (WINDOW + 2) * wire_taps, span), F32)
            table_ref[plane, block, wire_taps * WINDOW :, :] = jnp.concatenate(
                [high, total - high, spare], axis=0
            ).astype(BF16)
        return 0

    lax.fori_loop(0, planes, whole_plane, 0)


UNROLL = 7
LEAD_SHIFT = (TPB * HB - LEAD) % LANES


def build_table(levels, kinds, planes, wire_taps, ticks_here):
    tiles = math.gcd(ticks_here, 2 * LANES) // LANES
    blocks = ticks_here // (tiles * LANES)
    shape = (planes, blocks, (wire_taps + 1) * WINDOW, tiles * LANES)
    return pl.pallas_call(
        functools.partial(table_kernel, wire_taps=wire_taps),
        out_shape=jax.ShapeDtypeStruct(shape, BF16),
        in_specs=[vmem(), vmem()],
        out_specs=vmem(),
        scratch_shapes=[pltpu.VMEM((wire_taps, blocks, GROUP, tiles * LANES), F32)],
        compiler_params=params(),
        cost_estimate=cost(4e9, 2 * math.prod(shape)),
        name="table",
    )(levels, kinds)


def back_kernel(table_ref, own_ref, received_ref, next_ref, out_ref, cot_ref, wide_ref, *, wire_taps, rows):
    blocks, span = table_ref.shape[1], table_ref.shape[3]
    _, wires, ticks = own_ref.shape
    total = received_ref.shape[1]
    half = (wire_taps - 1) // 2
    parts = ticks // total
    plane = pl.program_id(0)
    even = lax.rem(lax.axis_index("gz"), 2) == 0
    cot_ref[EDGE : EDGE + wires] = own_ref[0]
    for part in range(parts):
        here = slice(part * total, (part + 1) * total)
        at = rows + (plane * parts + part) * EDGE
        near = received_ref[pl.ds(pl.multiple_of(at, EDGE), EDGE)]
        far = next_ref[0, :, here]
        cot_ref[:EDGE, here] = jnp.where(even, far, near)
        cot_ref[EDGE + wires :, here] = jnp.where(even, near, far)
    lane = lax.broadcasted_iota(jnp.int32, (wires, LANES), 1)
    none = jnp.zeros((wires, LANES), F32)
    step = span * 16 // LANES
    columns = (wire_taps + 1) // 2
    result = none
    for block in range(blocks):
        wide = lax.dot_general(
            cot_ref[:, block * span : (block + 1) * span],
            table_ref[plane, block, : columns * LANES],
            (((1,), (1,)), ((), ())),
            preferred_element_type=F32,
        )
        for column in range(columns):
            wide_ref[column] = wide[:, column * LANES : (column + 1) * LANES]
        left, right = none, none
        for column in range(columns):
            at = EDGE + half - 2 * column
            left += wide_ref[column, at : at + wires]
            if 2 * column + 1 < wire_taps:
                right += wide_ref[column, at - 1 : at - 1 + wires]
        both = jnp.where(lane < WINDOW, left + pltpu.roll(right, WINDOW, 1), none)
        result += pltpu.roll(both, block * step, 1) if block else both
    out_ref[0] = result.astype(BF16)


def backward(table, cotangent, received, beyond, wire_taps, rows):
    planes, blocks, depth, span = table.shape
    _, wires, ticks = cotangent.shape
    extent = wires + 2 * EDGE
    columns = (wire_taps + 1) // 2
    return pl.pallas_call(
        functools.partial(back_kernel, wire_taps=wire_taps, rows=rows),
        grid=(planes,),
        out_shape=jax.ShapeDtypeStruct((planes, wires, LANES), BF16),
        in_specs=[
            vmem(),
            pl.BlockSpec((1, wires, ticks), lambda p: (p, 0, 0)),
            vmem(),
            pl.BlockSpec((1, EDGE, ticks), lambda p: (p, 0, 0)),
        ],
        out_specs=pl.BlockSpec((1, wires, LANES), lambda p: (p, 0, 0)),
        scratch_shapes=[
            pltpu.VMEM((extent, ticks), BF16),
            pltpu.VMEM((columns, extent, LANES), F32),
        ],
        compiler_params=params(("arbitrary",)),
        cost_estimate=cost(4e9, 2 * math.prod(table.shape)),
        name="bin_gradients",
    )(table, cotangent, received, beyond)


def merge_kernel(*refs, bins, lead):
    parts, (cross_ref, local_ref, slab_ref) = refs[:-4], refs[-3:]
    planes, wires, _ = parts[0].shape
    total = local_ref.shape[1]
    slab = lax.axis_index("drift")
    for k, part in enumerate(parts):
        slab_ref[slab ^ k] = part[...]
    lane = lax.broadcasted_iota(jnp.int32, (wires, LANES), 1)
    none = jnp.zeros((wires, LANES), F32)
    for p in range(planes):
        tiles = [none] * (total // LANES)
        for source in range(len(parts)):
            values = slab_ref[source, p].astype(F32)
            tile, shift = (source * bins - lead) // LANES, (source * bins - lead) % LANES
            if shift:
                values = pltpu.roll(values, shift, 1)
            for t, inside in ((tile, lane >= shift), (tile + 1, lane < shift)):
                if 0 <= t < len(tiles):
                    tiles[t] += jnp.where(inside, values, none)
        for t, values in enumerate(tiles):
            here = slice(t * LANES, (t + 1) * LANES)
            if p < planes - 1:
                cross_ref[p, :, here] = values.astype(BF16)
            else:
                local_ref[:, here] = values.astype(BF16)


def merge(parts, bins, total, before):
    planes, wires, _ = parts[0].shape
    return pl.pallas_call(
        functools.partial(merge_kernel, bins=bins, lead=WINDOW // 2 - HB),
        out_shape=(
            jax.ShapeDtypeStruct((planes - 1, wires, total), BF16),
            jax.ShapeDtypeStruct((wires, total), BF16),
        ),
        in_specs=[vmem()] * len(parts) + [anywhere()],
        out_specs=(vmem(), vmem()),
        scratch_shapes=[pltpu.VMEM((len(parts), planes, wires, LANES), BF16)],
        compiler_params=params(),
        cost_estimate=cost(1e8, 4 * planes * wires * total),
        name="merge_bins",
    )(*parts, before)


def charge_kernel(block_ref, count_ref, *refs):
    sources, (local_ref, share_ref, out_ref, all_ref, chosen_ref) = refs[:-5], refs[-5:]
    _, planes, entries, wire_block, width = share_ref.shape
    owners, _, wires, total = all_ref.shape
    per_owner = wires // wire_block
    z = lax.axis_index("gz")
    b = pl.program_id(0)

    @pl.when(b == 0)
    def _():
        if len(sources) == 1:
            all_ref[...] = sources[0][...]
        else:
            for k, source in enumerate(sources):
                all_ref[z ^ k] = source[...]

    empty = jnp.zeros((wire_block, total), BF16)
    for p in range(planes):
        for k in range(entries):
            name = block_ref[p, k, b]
            if p < planes - 1:
                name = jnp.clip(name, 0, owners * per_owner - 1)
                owner = name // per_owner
                start = pl.multiple_of((name - owner * per_owner) * wire_block, wire_block)
                rows = all_ref[owner, p, pl.ds(start, wire_block), :]
            else:
                name = jnp.clip(name - z * per_owner, 0, per_owner - 1)
                start = pl.multiple_of(name * wire_block, wire_block)
                rows = local_ref[pl.ds(start, wire_block), :]
            at = (p * entries + k) * wire_block
            chosen_ref[at : at + wire_block] = jnp.where(k < count_ref[b, p], rows, empty)
    out_ref[...] = lax.dot_general(
        share_ref[0].reshape(planes * entries * wire_block, width),
        chosen_ref[...],
        (((0,), (0,)), ((), ())),
        preferred_element_type=F32,
    ).astype(BF16)


def charge_gradient(ovl_block, ovl_count, sources, local, intersection, owners):
    cells, planes, entries, wire_block, width = intersection.shape
    wires, total = local.shape
    shape = (owners, planes - 1, wires, total)
    return pl.pallas_call(
        charge_kernel,
        grid=(cells,),
        out_shape=jax.ShapeDtypeStruct((cells * width, total), BF16),
        in_specs=[smem(), smem()]
        + [vmem()] * (len(sources) + 1)
        + [pl.BlockSpec((1, planes, entries, wire_block, width), lambda b: (b, 0, 0, 0, 0))],
        out_specs=pl.BlockSpec((width, total), lambda b: (b, 0)),
        scratch_shapes=[
            pltpu.VMEM(shape, BF16),
            pltpu.VMEM((planes * entries * wire_block, total), BF16),
        ],
        compiler_params=params(("arbitrary",)),
        cost_estimate=cost(1e8, 2 * math.prod(shape)),
        name="charge_gradient",
    )(jnp.transpose(ovl_block, (1, 2, 0)), ovl_count, *sources, local, intersection)


def pieces_kernel(
    block_hbm, count_hbm, charge_hbm, share_hbm, cot_hbm, keep_ref, give_ref, local_ref, next_ref,
    block_ref, count_ref, charge_ref, share_ref, edge_ref, cross_ref, sems,
):
    cells, planes, entries, wire_block, width = share_ref.shape
    wires, total = local_ref.shape
    ticks = edge_ref.shape[2]
    per_owner = wires // wire_block
    halves = keep_ref.shape[0]
    owners = 2 * halves
    z = lax.axis_index("gz")
    even = lax.rem(z, 2) == 0
    upper = pl.ds(pl.multiple_of(jnp.where(even, wires - EDGE, 0), EDGE), EDGE)
    lower = pl.ds(pl.multiple_of(jnp.where(even, 0, wires - EDGE), EDGE), EDGE)
    loads = [
        pltpu.make_async_copy(source, target, sems.at[i])
        for i, (source, target) in enumerate(
            (
                (block_hbm, block_ref),
                (count_hbm, count_ref),
                (charge_hbm, charge_ref),
                (share_hbm, share_ref),
                (cot_hbm.at[:, upper], edge_ref),
                (cot_hbm.at[:, lower], next_ref),
            )
        )
    ]
    for load in loads:
        load.start()
    cross_ref[...] = jnp.zeros(cross_ref.shape, F32)
    local_ref[...] = jnp.zeros(local_ref.shape, F32)
    for load in loads:
        load.wait()
    for b in range(cells):
        pieces = (
            jnp.dot(
                share_ref[b].reshape(planes * entries * wire_block, width),
                charge_ref[b * width : (b + 1) * width],
                preferred_element_type=F32,
            )
            .astype(BF16)
            .astype(F32)
        )
        for p in range(planes):
            for k in range(entries):
                at = (p * entries + k) * wire_block
                piece = pieces[at : at + wire_block]
                piece = jnp.where(k < count_ref[b, p], piece, jnp.zeros_like(piece))
                name = block_ref[p, k, b]
                if p < planes - 1:
                    name = jnp.clip(name, 0, owners * per_owner - 1)
                    start = pl.multiple_of(EDGE + name * wire_block, EDGE)
                    cross_ref[p, pl.ds(start, wire_block)] += piece
                else:
                    name = jnp.clip(name - z * per_owner, 0, per_owner - 1)
                    start = pl.multiple_of(name * wire_block, wire_block)
                    local_ref[pl.ds(start, wire_block)] += piece
    extent = wires + 2 * EDGE
    cut = keep_ref.shape[1]
    none = jnp.zeros((EDGE, total), F32)
    for k in range(owners):
        to = z ^ k
        blocks = [
            cross_ref[p, pl.ds(pl.multiple_of(to * wires, EDGE), extent)] for p in range(planes - 1)
        ]
        blocks.append(jnp.where(to == z + 1, local_ref[wires - EDGE :], none))
        blocks.append(jnp.where(to == z - 1, local_ref[:EDGE], none))
        at = 0
        for rows in blocks:
            here = slice(at, at + rows.shape[0])
            at += rows.shape[0]
            if k % 2:
                give_ref[k // 2 * cut + here.start : k // 2 * cut + here.stop] = coded(rows, 0)
            else:
                keep_ref[k // 2, here] = rows
    at = halves * cut
    for p in range(planes):
        for part in range(ticks // total):
            give_ref[at : at + EDGE] = edge_ref[p, :, part * total : (part + 1) * total]
            at += EDGE


def cut_pieces(ovl_block, ovl_count, charge, intersection, cotangent, owners):
    cells, planes, entries, wire_block, width = intersection.shape
    total = charge.shape[1]
    _, wires, ticks = cotangent.shape
    rows = (planes - 1) * (wires + 2 * EDGE) + 2 * EDGE
    cut = (owners // 2, rows, total)
    edges = planes * EDGE * ticks // total
    hbm = pl.BlockSpec(memory_space=pltpu.HBM)
    blocks = jnp.transpose(ovl_block, (1, 2, 0))
    return pl.pallas_call(
        pieces_kernel,
        out_shape=(
            jax.ShapeDtypeStruct(cut, F32),
            jax.ShapeDtypeStruct((owners // 2 * rows + edges, total), BF16),
            jax.ShapeDtypeStruct((wires, total), F32),
            jax.ShapeDtypeStruct((planes, EDGE, ticks), BF16),
        ),
        in_specs=[hbm] * 5,
        out_specs=(vmem(), vmem(), vmem(), vmem()),
        scratch_shapes=[
            pltpu.SMEM(blocks.shape, jnp.int32),
            pltpu.SMEM(ovl_count.shape, jnp.int32),
            pltpu.VMEM(charge.shape, BF16),
            pltpu.VMEM(intersection.shape, BF16),
            pltpu.VMEM((planes, EDGE, ticks), BF16),
            pltpu.VMEM((planes - 1, owners * wires + 2 * EDGE, total), F32),
            pltpu.SemaphoreType.DMA((6,)),
        ],
        compiler_params=params(limit=WHOLE_VMEM),
        cost_estimate=cost(1e8, 4 * owners * rows * total),
        name="pieces",
    )(blocks, ovl_count, charge, intersection, cotangent)


def relay_kernel(keep_ref, received_ref, *outs):
    rows = keep_ref.shape[1]
    for j, out in enumerate(outs, 1):
        summed = keep_ref[j] + plain(received_ref[j * rows : (j + 1) * rows], True)
        out[...] = coded(summed, 0)


def relay(keep, received):
    halves, rows, total = keep.shape
    return pl.pallas_call(
        relay_kernel,
        out_shape=(jax.ShapeDtypeStruct((rows, total), BF16),) * (halves - 1),
        in_specs=[vmem(), vmem()],
        out_specs=(vmem(),) * (halves - 1),
        compiler_params=params(),
        cost_estimate=cost(1e7, 6 * halves * rows * total),
        name="relay",
    )(keep, received)


def slabs_kernel(*refs, bins, lead, slabs):
    count = len(refs) - slabs - 1
    keep_ref, received_ref, others, local_ref = refs[0], refs[1], refs[2 : count - 2], refs[count - 2]
    outs, cut_ref = refs[count:-1], refs[-1]
    total = local_ref.shape[1]
    cut = keep_ref.shape[1]
    summed = keep_ref[0] + plain(received_ref[:cut], True)
    for other in others:
        summed += plain(other[...], True)
    edge = cut - 2 * EDGE
    rows = jnp.concatenate(
        [summed[:edge], summed[edge : edge + EDGE], local_ref[...], summed[edge + EDGE :]], axis=0
    )
    none = jnp.zeros((rows.shape[0], LANES), F32)
    lane = lax.broadcasted_iota(jnp.int32, none.shape, 1)
    level = jnp.broadcast_to(rows[:, :1].astype(BF16).astype(F32), none.shape)
    tiles = [rows[:, t * LANES : (t + 1) * LANES] - level for t in range(total // LANES)]
    for to in range(slabs):
        at = to * bins - lead
        tile, shift = at // LANES, at % LANES
        pair = [tiles[t] if 0 <= t < len(tiles) else -level for t in (tile, tile + 1)]
        value = shared_lanes(pair[0], pair[1], shift, lane)
        cut_ref[to] = jnp.where(lane == 0, level, value).astype(BF16)
    slab = lax.axis_index("drift")
    for k, out in enumerate(outs):
        out[...] = cut_ref[slab ^ k]


def cut_slabs(keep, received, others, local, bins, slabs, before):
    wires, total = local.shape
    rows = keep.shape[1] + wires
    cut = jax.ShapeDtypeStruct((rows, LANES), BF16)
    first = pl.BlockSpec((1,) + keep.shape[1:], lambda i: (0, 0, 0))
    return pl.pallas_call(
        functools.partial(slabs_kernel, bins=bins, lead=WINDOW // 2 - HB, slabs=slabs),
        grid=(1,),
        out_shape=(cut,) * slabs,
        in_specs=[first] + [vmem()] * (2 + len(others)) + [anywhere()],
        out_specs=(vmem(),) * slabs,
        scratch_shapes=[pltpu.VMEM((slabs, rows, LANES), BF16)],
        compiler_params=params(("arbitrary",)),
        cost_estimate=cost(1e8, 4 * rows * total),
        name="slab_currents",
    )(keep, received, *others, local, before)


def signal_kernel(*refs, wire_taps):
    parts, (table_ref, out_ref, even_ref, odd_ref, level_ref, lines_ref) = refs[:-6], refs[-6:]
    blocks, span = table_ref.shape[1], table_ref.shape[3]
    wires = out_ref.shape[1]
    half = (wire_taps - 1) // 2
    step = span * 16 // LANES
    currents = plain(parts[0][...], False)
    for part in parts[1:]:
        currents += plain(part[...], False)
    middle = WINDOW // 2
    level = currents[:, middle : middle + 1].astype(BF16).astype(F32)
    level = jnp.broadcast_to(level, currents.shape)
    level_ref[...] = level
    currents = currents - level
    lane = lax.broadcasted_iota(jnp.int32, (wires, LANES), 1)
    levels = jnp.zeros((wires, LANES), F32)
    for a in range(wire_taps):
        at = EDGE - half + a
        here = (lane == WINDOW + a) | (lane == WINDOW + wire_taps + a)
        levels = jnp.where(here, level_ref[at : at + wires], levels)
    for block in range(blocks):
        even_ref[...] = pltpu.roll(currents, (-step * block) % LANES, 1)
        odd_ref[...] = pltpu.roll(currents, (WINDOW - step * block) % LANES, 1)
        for pair in range((wire_taps + 1) // 2):
            at = EDGE - half + 2 * pair
            right = levels
            if 2 * pair + 1 < wire_taps:
                right = odd_ref[at + 1 : at + 1 + wires]
            line = jnp.where(lane < WINDOW, even_ref[at : at + wires], right)
            lines_ref[:, pair * LANES : (pair + 1) * LANES] = line.astype(BF16)
        out_ref[0, :, block * span : (block + 1) * span] = jnp.dot(
            lines_ref[...], table_ref[pl.program_id(0), block], preferred_element_type=F32
        ).astype(BF16)


def forward(parts, table, wires, wire_taps):
    planes, blocks, depth, span = table.shape
    extent = wires + 2 * EDGE
    part = pl.BlockSpec((extent, LANES), lambda p: (p, 0))
    return pl.pallas_call(
        functools.partial(signal_kernel, wire_taps=wire_taps),
        grid=(planes,),
        out_shape=jax.ShapeDtypeStruct((planes, wires, blocks * span), BF16),
        in_specs=[part] * len(parts)
        + [vmem()],
        out_specs=pl.BlockSpec((1, wires, blocks * span), lambda p: (p, 0, 0)),
        scratch_shapes=[
            pltpu.VMEM((extent, LANES), F32),
            pltpu.VMEM((extent, LANES), F32),
            pltpu.VMEM((extent, LANES), F32),
            pltpu.VMEM((wires, depth), BF16),
        ],
        compiler_params=params(("arbitrary",)),
        cost_estimate=cost(4e9, 2 * math.prod(table.shape)),
        name="signal",
    )(*parts, table)


def local(charge, intersection, ovl_block, ovl_count, diff_class, response, cotangent):
    total = charge.shape[1]
    owners = lax.axis_size("gz")
    slabs = lax.axis_size("drift")
    planes, wires, ticks = cotangent.shape
    wire_taps = response.shape[1]
    bins = total // slabs

    keep, give, local_currents, edges = cut_pieces(
        ovl_block, ovl_count, charge, intersection, cotangent, owners
    )
    received = swap(give, "gz", 1)
    pairs = [(i, i + 1) for i in range(1, owners - 1, 2)]
    beyond = lax.ppermute(edges, "gz", pairs + [(j, i) for i, j in pairs])
    sums = relay(keep, received) if owners > 2 else ()
    others = [swap(block, "gz", 2 * j) for j, block in enumerate(sums, 1)]

    levels, kinds = smeared_levels(diff_class, response, bins, sums[0] if sums else received)
    table = build_table(levels, kinds, planes, wire_taps, ticks)
    rows = keep.shape[0] * keep.shape[1]
    partial = backward(table, cotangent, received, beyond, wire_taps, rows)
    spread = [partial] + [swap(partial, "drift", k) for k in range(1, slabs)]

    cuts = cut_slabs(keep, received, others, local_currents, bins, slabs, partial)
    windows = [cuts[0]] + [swap(cuts[k], "drift", k) for k in range(1, slabs)]
    signal = forward(windows, table, wires, wire_taps)

    cross, own = merge(spread, bins, total, cuts[0])
    if owners == 4:
        across = swap(cross, "gz", 2)
        sources = [cross, swap(cross, "gz", 1), across, swap(across, "gz", 1)]
    else:
        sources = [lax.all_gather(cross, "gz", axis=0)]
    charge_grad = charge_gradient(ovl_block, ovl_count, sources, own, intersection, owners)
    return signal, charge_grad


def solution(mesh):
    return jax.shard_map(
        local,
        mesh=mesh,
        in_specs=(
            P(("apa", "gz", "drift"), None),
            P(("apa", "gz", "drift"), None, None, None, None),
            P(("apa", "gz", "drift"), None, None),
            P(("apa", "gz", "drift"), None),
            P("apa"),
            P(),
            P("apa", "gz", "drift"),
        ),
        out_specs=(P("apa", "gz", "drift"), P(("apa", "gz", "drift"), None)),
        check_vma=False,
    )
```

```python
import functools
import math

import jax
import jax.numpy as jnp
from jax import lax
from jax.experimental import pallas as pl
from jax.experimental.pallas import tpu as pltpu
from jax.sharding import PartitionSpec as P

TPB = 8
HB = 2
CLASSES = 6
LANES = 128
EDGE = 16
GROUP = 8
WINDOW = 64
LEAD = HB * TPB - TPB // 2
VMEM_LIMIT = 24 * 1024 * 1024
WHOLE_VMEM = 61 * 1024 * 1024
BF16 = jnp.bfloat16
F32 = jnp.float32


def params(semantics=None, limit=VMEM_LIMIT):
    return pltpu.CompilerParams(vmem_limit_bytes=limit, dimension_semantics=semantics)


def vmem():
    return pl.BlockSpec(memory_space=pltpu.VMEM)


def smem():
    return pl.BlockSpec(memory_space=pltpu.SMEM)


def anywhere():
    return pl.BlockSpec(memory_space=pl.ANY)


def cost(flops, moved):
    return pl.CostEstimate(flops=int(flops), bytes_accessed=int(moved), transcendentals=0)


def swap(block, axis, distance):
    count = lax.axis_size(axis)
    return lax.ppermute(block, axis, [(i, i ^ distance) for i in range(count)])


def widths(number):
    spread = TPB * (0.2 + 0.15 * number)
    half = HB * TPB
    total = sum(math.exp(-((j + 0.5) ** 2) / (2.0 * spread * spread)) for j in range(-half, half))
    return 1.0 / (2.0 * spread * spread), 1.0 / total


def shared_lanes(left, right, shift, lane):
    if shift == 0:
        return left
    back = LANES - shift
    return jnp.where(lane < back, pltpu.roll(left, back, 1), pltpu.roll(right, back, 1))


def coded(rows, column):
    lane = lax.broadcasted_iota(jnp.int32, rows.shape, 1)
    level = jnp.broadcast_to(rows[:, column : column + 1].astype(BF16).astype(F32), rows.shape)
    return jnp.where(lane == 0, level, rows - level).astype(BF16)


def plain(rows, first):
    rows = rows.astype(F32)
    lane = lax.broadcasted_iota(jnp.int32, rows.shape, 1)
    level = jnp.broadcast_to(rows[:, :1], rows.shape)
    return jnp.where(lane == 0, level if first else jnp.zeros_like(rows), rows + level)


def levels_kernel(class_ref, response_ref, _, level_ref, kind_ref, flat_ref, *, bins, slabs):
    planes, wire_taps, length = response_ref.shape
    rows = level_ref.shape[0] // planes
    groups = kind_ref.shape[0]
    slab = lax.axis_index("drift")
    lane = lax.broadcasted_iota(jnp.int32, (GROUP, LANES), 1)
    classes = jnp.broadcast_to(class_ref[...].astype(F32), (GROUP, class_ref.shape[1]))
    tiles = [classes[:, t : t + LANES] for t in range(0, class_ref.shape[1], LANES)]
    none = jnp.zeros((GROUP, LANES), F32)
    numbers = none
    for source in range(slabs):
        at = source * bins - (WINDOW // 2 - HB)
        tile, shift = at // LANES, at % LANES
        pair = [tiles[t] if 0 <= t < len(tiles) else none for t in (tile, tile + 1)]
        numbers = jnp.where(slab == source, shared_lanes(pair[0], pair[1], shift, lane), numbers)
    x = slab * bins - (WINDOW // 2 - HB) + lane
    numbers = jnp.where((x >= 0) & (x < HB), (CLASSES + x).astype(F32), numbers)
    column = jnp.broadcast_to(numbers[:1], (LANES, LANES)).T.astype(jnp.int32)
    for m in range(groups):
        kind_ref[m] = column[m * GROUP : (m + 1) * GROUP]
    flat_ref[...] = jnp.zeros(flat_ref.shape, F32)
    for p in range(planes):
        flat_ref[p * rows : p * rows + wire_taps, :length] = response_ref[p].astype(F32)
    taps = flat_ref[...].astype(BF16)
    tap = lax.broadcasted_iota(jnp.int32, (LANES, 2 * LANES), 0)
    tick = lax.broadcasted_iota(jnp.int32, (LANES, 2 * LANES), 1)
    step = tick - tap - LEAD
    offset = step.astype(F32) - (TPB - 1) / 2.0
    squared = offset * offset
    inside = jnp.abs(offset) < HB * TPB
    for kind in range(CLASSES + HB):
        keep = inside
        if kind < CLASSES:
            narrow, scale = widths(kind)
        else:
            edge = kind - CLASSES
            narrow, scale = widths(0)
            for number in range(1, CLASSES):
                chosen = classes[:1, edge : edge + 1] == number
                narrow = jnp.where(chosen, widths(number)[0], narrow)
                scale = jnp.where(chosen, widths(number)[1], scale)
            keep = inside & (step >= -TPB * edge)
        smear = jnp.where(keep, jnp.exp(-(squared * narrow)) * scale, 0.0)
        high = smear.astype(BF16)
        low = (smear - high.astype(F32)).astype(BF16)
        near = jnp.dot(taps[:, :LANES], high, preferred_element_type=F32) + jnp.dot(
            taps[:, :LANES], low, preferred_element_type=F32
        )
        far = jnp.dot(taps[:, LANES:], high[:, :LANES], preferred_element_type=F32) + jnp.dot(
            taps[:, LANES:], low[:, :LANES], preferred_element_type=F32
        )
        level_ref[:, kind, :LANES] = near[:, :LANES]
        level_ref[:, kind, LANES:] = near[:, LANES:] + far


def smeared_levels(diff_class, response, bins, slabs, before):
    planes, wire_taps, _ = response.shape
    rows = -(-wire_taps // 8) * 8
    groups = (bins + WINDOW // 2) // GROUP
    return pl.pallas_call(
        functools.partial(levels_kernel, bins=bins, slabs=slabs),
        out_shape=(
            jax.ShapeDtypeStruct((planes * rows, CLASSES + HB, 2 * LANES), F32),
            jax.ShapeDtypeStruct((groups, GROUP, LANES), jnp.int32),
        ),
        in_specs=[vmem(), vmem(), anywhere()],
        out_specs=(vmem(), vmem()),
        scratch_shapes=[pltpu.VMEM((planes * rows, 2 * LANES), F32)],
        compiler_params=params(),
        cost_estimate=cost(1e8, 1e6),
        name="levels",
    )(diff_class[None], response, before)


def table_kernel(level_ref, kind_ref, table_ref, sum_ref, *, wire_taps):
    planes, blocks, depth, span = table_ref.shape
    rows = level_ref.shape[0] // planes
    groups = kind_ref.shape[0]
    tiles = span // LANES
    lane = lax.broadcasted_iota(jnp.int32, (GROUP, LANES), 1)
    row = lax.broadcasted_iota(jnp.int32, (GROUP, LANES), 0)
    starts = [LEAD_SHIFT + odd * (LANES // 2) + TPB * row for odd in range(2)]
    after = [lane >= start for start in starts]
    zero = jnp.zeros((GROUP, LANES), F32)
    empty = jnp.zeros((2 * GROUP, LANES), BF16)

    def body(a, plane):
        levels = level_ref[plane * rows + a]
        halves = [levels[:, :LANES], levels[:, LANES:]]
        pieces = []
        for m in range(groups):
            odd = m % 2
            parts = [
                pltpu.roll(
                    jnp.take_along_axis(half, kind_ref[m], axis=0),
                    LEAD_SHIFT + odd * (LANES // 2),
                    1,
                    stride=TPB,
                    stride_axis=0,
                )
                for half in halves
            ]
            pieces.append(
                (
                    jnp.where(after[odd], parts[0], zero),
                    jnp.where(after[odd], parts[1], parts[0]),
                    jnp.where(after[odd], zero, parts[1]),
                )
            )
        for block in range(blocks):
            for tile in range(tiles):
                here = slice(tile * LANES, (tile + 1) * LANES)
                total = zero
                for quarter in range(WINDOW // (2 * GROUP)):
                    m = 2 * (tiles * block + quarter)
                    at = a * WINDOW + quarter * 2 * GROUP
                    at = pl.ds(pl.multiple_of(at, 2 * GROUP), 2 * GROUP)
                    third = tile - quarter + 2
                    value = empty
                    if 0 <= third <= 2 and m + 1 < groups:
                        value = jnp.concatenate(
                            [pieces[m][third], pieces[m + 1][third]], axis=0
                        ).astype(BF16)
                        total = total + pieces[m][third] + pieces[m + 1][third]
                    table_ref[plane, block, at, here] = value
                sum_ref[a, block, :, here] = total
        return plane

    def whole_plane(plane, _):
        lax.fori_loop(0, wire_taps, body, plane, unroll=UNROLL)
        for block in range(blocks):
            total = jnp.sum(sum_ref[:, block], axis=1)
            high = total.astype(BF16).astype(F32)
            spare = jnp.zeros((depth - (WINDOW + 2) * wire_taps, span), F32)
            table_ref[plane, block, wire_taps * WINDOW :, :] = jnp.concatenate(
                [high, total - high, spare], axis=0
            ).astype(BF16)
        return 0

    lax.fori_loop(0, planes, whole_plane, 0)


UNROLL = 7
LEAD_SHIFT = (TPB * HB - LEAD) % LANES


def build_table(levels, kinds, planes, wire_taps, ticks_here):
    tiles = math.gcd(ticks_here, 2 * LANES) // LANES
    blocks = ticks_here // (tiles * LANES)
    shape = (planes, blocks, (wire_taps + 1) * WINDOW, tiles * LANES)
    return pl.pallas_call(
        functools.partial(table_kernel, wire_taps=wire_taps),
        out_shape=jax.ShapeDtypeStruct(shape, BF16),
        in_specs=[vmem(), vmem()],
        out_specs=vmem(),
        scratch_shapes=[pltpu.VMEM((wire_taps, blocks, GROUP, tiles * LANES), F32)],
        compiler_params=params(),
        cost_estimate=cost(4e9, 2 * math.prod(shape)),
        name="table",
    )(levels, kinds)


def back_kernel(table_ref, own_ref, received_ref, *refs, wire_taps):
    others, (out_ref, cot_ref, wide_ref) = refs[:-3], refs[-3:]
    blocks, span = table_ref.shape[1], table_ref.shape[3]
    planes = table_ref.shape[0]
    _, wires, ticks = own_ref.shape
    total = received_ref.shape[1]
    half = (wire_taps - 1) // 2
    parts = ticks // total
    side = planes * parts * EDGE
    lows = received_ref.shape[0] - 2 * side
    plane = pl.program_id(0)
    even = lax.rem(lax.axis_index("gz"), 2) == 0
    cot_ref[EDGE : EDGE + wires] = own_ref[0]
    for part in range(parts):
        here = slice(part * total, (part + 1) * total)
        at = (plane * parts + part) * EDGE
        low = received_ref[pl.ds(pl.multiple_of(lows + at, EDGE), EDGE)]
        high = received_ref[pl.ds(pl.multiple_of(lows + side + at, EDGE), EDGE)]
        near = jnp.where(even, low, high)
        far = jnp.zeros((EDGE, total), BF16)
        for other in others:
            far += other[pl.ds(pl.multiple_of(at, EDGE), EDGE)]
        cot_ref[:EDGE, here] = jnp.where(even, far, near)
        cot_ref[EDGE + wires :, here] = jnp.where(even, near, far)
    lane = lax.broadcasted_iota(jnp.int32, (wires, LANES), 1)
    none = jnp.zeros((wires, LANES), F32)
    step = span * 16 // LANES
    columns = (wire_taps + 1) // 2
    result = none
    for block in range(blocks):
        wide = lax.dot_general(
            cot_ref[:, block * span : (block + 1) * span],
            table_ref[plane, block, : columns * LANES],
            (((1,), (1,)), ((), ())),
            preferred_element_type=F32,
        )
        for column in range(columns):
            wide_ref[column] = wide[:, column * LANES : (column + 1) * LANES]
        left, right = none, none
        for column in range(columns):
            at = EDGE + half - 2 * column
            left += wide_ref[column, at : at + wires]
            if 2 * column + 1 < wire_taps:
                right += wide_ref[column, at - 1 : at - 1 + wires]
        both = jnp.where(lane < WINDOW, left + pltpu.roll(right, WINDOW, 1), none)
        result += pltpu.roll(both, block * step, 1) if block else both
    out_ref[0] = result.astype(BF16)


def backward(table, cotangent, received, others, wire_taps):
    planes, blocks, depth, span = table.shape
    _, wires, ticks = cotangent.shape
    extent = wires + 2 * EDGE
    columns = (wire_taps + 1) // 2
    return pl.pallas_call(
        functools.partial(back_kernel, wire_taps=wire_taps),
        grid=(planes,),
        out_shape=jax.ShapeDtypeStruct((planes, wires, LANES), BF16),
        in_specs=[
            vmem(),
            pl.BlockSpec((1, wires, ticks), lambda p: (p, 0, 0)),
        ]
        + [vmem()] * (1 + len(others)),
        out_specs=pl.BlockSpec((1, wires, LANES), lambda p: (p, 0, 0)),
        scratch_shapes=[
            pltpu.VMEM((extent, ticks), BF16),
            pltpu.VMEM((columns, extent, LANES), F32),
        ],
        compiler_params=params(("arbitrary",)),
        cost_estimate=cost(4e9, 2 * math.prod(table.shape)),
        name="bin_gradients",
    )(table, cotangent, received, *others)


def merge_kernel(*refs, bins, lead):
    parts, (cross_ref, local_ref, slab_ref) = refs[:-4], refs[-3:]
    planes, wires, _ = parts[0].shape
    total = local_ref.shape[1]
    slab = lax.axis_index("drift")
    for k, part in enumerate(parts):
        slab_ref[slab ^ k] = part[...]
    lane = lax.broadcasted_iota(jnp.int32, (wires, LANES), 1)
    none = jnp.zeros((wires, LANES), F32)
    for p in range(planes):
        tiles = [none] * (total // LANES)
        for source in range(len(parts)):
            values = slab_ref[source, p].astype(F32)
            tile, shift = (source * bins - lead) // LANES, (source * bins - lead) % LANES
            if shift:
                values = pltpu.roll(values, shift, 1)
            for t, inside in ((tile, lane >= shift), (tile + 1, lane < shift)):
                if 0 <= t < len(tiles):
                    tiles[t] += jnp.where(inside, values, none)
        for t, values in enumerate(tiles):
            here = slice(t * LANES, (t + 1) * LANES)
            if p < planes - 1:
                cross_ref[p, :, here] = values.astype(BF16)
            else:
                local_ref[:, here] = values.astype(BF16)


def merge(parts, bins, total, before):
    planes, wires, _ = parts[0].shape
    return pl.pallas_call(
        functools.partial(merge_kernel, bins=bins, lead=WINDOW // 2 - HB),
        out_shape=(
            jax.ShapeDtypeStruct((planes - 1, wires, total), BF16),
            jax.ShapeDtypeStruct((wires, total), BF16),
        ),
        in_specs=[vmem()] * len(parts) + [anywhere()],
        out_specs=(vmem(), vmem()),
        scratch_shapes=[pltpu.VMEM((len(parts), planes, wires, LANES), BF16)],
        compiler_params=params(),
        cost_estimate=cost(1e8, 4 * planes * wires * total),
        name="merge_bins",
    )(*parts, before)


def charge_kernel(block_ref, count_ref, *refs):
    sources, (local_ref, share_ref, _, out_hbm) = refs[:-8], refs[-8:-4]
    all_ref, chosen_ref, out_ref, sems = refs[-4:]
    cells, planes, entries, wire_block, width = share_ref.shape
    owners, _, wires, total = all_ref.shape
    per_owner = wires // wire_block
    z = lax.axis_index("gz")
    if len(sources) == 1:
        all_ref[...] = sources[0][...]
    else:
        for k, source in enumerate(sources):
            all_ref[z ^ k] = source[...]
    empty = jnp.zeros((wire_block, total), BF16)
    stores = []
    for b in range(cells):
        for p in range(planes):
            for k in range(entries):
                name = block_ref[p, k, b]
                if p < planes - 1:
                    name = jnp.clip(name, 0, owners * per_owner - 1)
                    owner = name // per_owner
                    start = pl.multiple_of((name - owner * per_owner) * wire_block, wire_block)
                    rows = all_ref[owner, p, pl.ds(start, wire_block), :]
                else:
                    name = jnp.clip(name - z * per_owner, 0, per_owner - 1)
                    start = pl.multiple_of(name * wire_block, wire_block)
                    rows = local_ref[pl.ds(start, wire_block), :]
                at = (p * entries + k) * wire_block
                chosen_ref[b, at : at + wire_block] = jnp.where(k < count_ref[b, p], rows, empty)
        here = slice(b * width, (b + 1) * width)
        out_ref[here] = lax.dot_general(
            share_ref[b].reshape(planes * entries * wire_block, width),
            chosen_ref[b],
            (((0,), (0,)), ((), ())),
            preferred_element_type=F32,
        ).astype(BF16)
        store = pltpu.make_async_copy(out_ref.at[here], out_hbm.at[here], sems.at[b])
        store.start()
        stores.append(store)
    for store in stores:
        store.wait()


def charge_gradient(ovl_block, ovl_count, sources, local, intersection, owners, before):
    cells, planes, entries, wire_block, width = intersection.shape
    wires, total = local.shape
    shape = (owners, planes - 1, wires, total)
    return pl.pallas_call(
        charge_kernel,
        out_shape=jax.ShapeDtypeStruct((cells * width, total), BF16),
        in_specs=[smem(), smem()] + [vmem()] * (len(sources) + 3),
        out_specs=anywhere(),
        scratch_shapes=[
            pltpu.VMEM(shape, BF16),
            pltpu.VMEM((cells, planes * entries * wire_block, total), BF16),
            pltpu.VMEM((cells * width, total), BF16),
            pltpu.SemaphoreType.DMA((cells,)),
        ],
        compiler_params=params(),
        cost_estimate=cost(1e8, 2 * math.prod(shape)),
        name="charge_gradient",
    )(jnp.transpose(ovl_block, (1, 2, 0)), ovl_count, *sources, local, intersection, before)


def pieces_kernel(
    block_hbm, count_hbm, charge_hbm, share_hbm, cot_hbm, own_ref, keep_ref, give_ref, local_ref,
    block_ref, count_ref, charge_ref, share_ref, edge_ref, cross_ref, sems,
):
    cells, planes, entries, wire_block, width = share_ref.shape
    wires, total = local_ref.shape
    ticks = edge_ref.shape[3]
    per_owner = wires // wire_block
    cut = own_ref.shape[0]
    halves = 1 + keep_ref.shape[0]
    owners = 2 * halves
    z = lax.axis_index("gz")
    loads = [
        pltpu.make_async_copy(source, target, sems.at[i])
        for i, (source, target) in enumerate(
            (
                (block_hbm, block_ref),
                (count_hbm, count_ref),
                (charge_hbm, charge_ref),
                (share_hbm, share_ref),
                (cot_hbm.at[:, :EDGE], edge_ref.at[0]),
                (cot_hbm.at[:, wires - EDGE :], edge_ref.at[1]),
            )
        )
    ]
    for load in loads:
        load.start()
    cross_ref[...] = jnp.zeros(cross_ref.shape, F32)
    local_ref[...] = jnp.zeros(local_ref.shape, F32)
    for load in loads:
        load.wait()
    for b in range(cells):
        pieces = (
            jnp.dot(
                share_ref[b].reshape(planes * entries * wire_block, width),
                charge_ref[b * width : (b + 1) * width],
                preferred_element_type=F32,
            )
            .astype(BF16)
            .astype(F32)
        )
        for p in range(planes):
            for k in range(entries):
                at = (p * entries + k) * wire_block
                piece = pieces[at : at + wire_block]
                piece = jnp.where(k < count_ref[b, p], piece, jnp.zeros_like(piece))
                name = block_ref[p, k, b]
                if p < planes - 1:
                    name = jnp.clip(name, 0, owners * per_owner - 1)
                    start = pl.multiple_of(EDGE + name * wire_block, EDGE)
                    cross_ref[p, pl.ds(start, wire_block)] += piece
                else:
                    name = jnp.clip(name - z * per_owner, 0, per_owner - 1)
                    start = pl.multiple_of(name * wire_block, wire_block)
                    local_ref[pl.ds(start, wire_block)] += piece
    extent = wires + 2 * EDGE
    none = jnp.zeros((EDGE, total), F32)
    for k in range(owners):
        to = z ^ k
        blocks = [
            cross_ref[p, pl.ds(pl.multiple_of(to * wires, EDGE), extent)] for p in range(planes - 1)
        ]
        blocks.append(jnp.where(to == z + 1, local_ref[wires - EDGE :], none))
        blocks.append(jnp.where(to == z - 1, local_ref[:EDGE], none))
        at = 0
        for rows in blocks:
            here = slice(at, at + rows.shape[0])
            at += rows.shape[0]
            if k % 2:
                give_ref[k // 2 * cut + here.start : k // 2 * cut + here.stop] = coded(rows, 0)
            elif k:
                keep_ref[k // 2 - 1, here] = coded(rows, 0)
            else:
                own_ref[here] = rows
    at = halves * cut
    for side in range(2):
        for p in range(planes):
            for part in range(ticks // total):
                give_ref[at : at + EDGE] = edge_ref[side, p, :, part * total : (part + 1) * total]
                at += EDGE


def cut_pieces(ovl_block, ovl_count, charge, intersection, cotangent, owners):
    cells, planes, entries, wire_block, width = intersection.shape
    total = charge.shape[1]
    _, wires, ticks = cotangent.shape
    rows = (planes - 1) * (wires + 2 * EDGE) + 2 * EDGE
    edges = 2 * planes * EDGE * ticks // total
    hbm = pl.BlockSpec(memory_space=pltpu.HBM)
    blocks = jnp.transpose(ovl_block, (1, 2, 0))
    return pl.pallas_call(
        pieces_kernel,
        out_shape=(
            jax.ShapeDtypeStruct((rows, total), F32),
            jax.ShapeDtypeStruct((owners // 2 - 1, rows, total), BF16),
            jax.ShapeDtypeStruct((owners // 2 * rows + edges, total), BF16),
            jax.ShapeDtypeStruct((wires, total), F32),
        ),
        in_specs=[hbm] * 5,
        out_specs=(vmem(), vmem(), vmem(), vmem()),
        scratch_shapes=[
            pltpu.SMEM(blocks.shape, jnp.int32),
            pltpu.SMEM(ovl_count.shape, jnp.int32),
            pltpu.VMEM(charge.shape, BF16),
            pltpu.VMEM(intersection.shape, BF16),
            pltpu.VMEM((2, planes, EDGE, ticks), BF16),
            pltpu.VMEM((planes - 1, owners * wires + 2 * EDGE, total), F32),
            pltpu.SemaphoreType.DMA((6,)),
        ],
        compiler_params=params(limit=WHOLE_VMEM),
        cost_estimate=cost(1e8, 4 * owners * rows * total),
        name="pieces",
    )(blocks, ovl_count, charge, intersection, cotangent)


def relay_kernel(keep_ref, received_ref, *outs):
    others, rows, _ = keep_ref.shape
    edges = (received_ref.shape[0] - (others + 1) * rows) // 2
    z = lax.axis_index("gz")
    even = lax.rem(z, 2) == 0
    low = received_ref[(others + 1) * rows : (others + 1) * rows + edges]
    high = received_ref[(others + 1) * rows + edges :]
    for j in range(others):
        to = z ^ (2 * (j + 1))
        summed = plain(keep_ref[j], True)
        summed += plain(received_ref[(j + 1) * rows : (j + 2) * rows], True)
        outs[j][...] = coded(summed, 0)
        upward, downward = even & (to == z + 2), jnp.logical_not(even) & (to == z - 2)
        outs[others + j][...] = jnp.where(
            upward, high, jnp.where(downward, low, jnp.zeros_like(low))
        )


def relay(keep, received):
    others, rows, total = keep.shape
    edges = (received.shape[0] - (others + 1) * rows) // 2
    outs = pl.pallas_call(
        relay_kernel,
        out_shape=(jax.ShapeDtypeStruct((rows, total), BF16),) * others
        + (jax.ShapeDtypeStruct((edges, total), BF16),) * others,
        in_specs=[vmem(), vmem()],
        out_specs=(vmem(),) * (2 * others),
        compiler_params=params(),
        cost_estimate=cost(1e7, 6 * others * rows * total),
        name="relay",
    )(keep, received)
    return outs[:others], outs[others:]


def slabs_kernel(*refs, bins, lead, slabs):
    count = len(refs) - slabs.bit_length() - 1
    keep_ref, received_ref, others, local_ref = refs[0], refs[1], refs[2 : count - 2], refs[count - 2]
    outs, cut_ref = refs[count:-1], refs[-1]
    total = local_ref.shape[1]
    cut = keep_ref.shape[0]
    summed = keep_ref[...] + plain(received_ref[:cut], True)
    for other in others:
        summed += plain(other[...], True)
    edge = cut - 2 * EDGE
    rows = jnp.concatenate(
        [summed[:edge], summed[edge : edge + EDGE], local_ref[...], summed[edge + EDGE :]], axis=0
    )
    none = jnp.zeros((rows.shape[0], LANES), F32)
    lane = lax.broadcasted_iota(jnp.int32, none.shape, 1)
    level = jnp.broadcast_to(rows[:, :1].astype(BF16).astype(F32), none.shape)
    tiles = [rows[:, t * LANES : (t + 1) * LANES] - level for t in range(total // LANES)]
    for to in range(slabs):
        at = to * bins - lead
        tile, shift = at // LANES, at % LANES
        pair = [tiles[t] if 0 <= t < len(tiles) else -level for t in (tile, tile + 1)]
        value = shared_lanes(pair[0], pair[1], shift, lane)
        cut_ref[to] = jnp.where(lane == 0, level, value).astype(BF16)
    slab = lax.axis_index("drift")
    outs[0][...] = cut_ref[slab]
    size = rows.shape[0]
    for s, out in enumerate(outs[1:]):
        for i in range(slabs >> (s + 1)):
            out[i * size : (i + 1) * size] = cut_ref[slab ^ ((2 * i + 1) << s)]


def cut_slabs(keep, received, others, local, bins, slabs, before):
    wires, total = local.shape
    rows = keep.shape[0] + wires
    steps = slabs.bit_length() - 1
    counts = [1] + [slabs >> (s + 1) for s in range(steps)]
    return pl.pallas_call(
        functools.partial(slabs_kernel, bins=bins, lead=WINDOW // 2 - HB, slabs=slabs),
        out_shape=tuple(jax.ShapeDtypeStruct((n * rows, LANES), BF16) for n in counts),
        in_specs=[vmem()] * (3 + len(others)) + [anywhere()],
        out_specs=(vmem(),) * len(counts),
        scratch_shapes=[pltpu.VMEM((slabs, rows, LANES), BF16)],
        compiler_params=params(),
        cost_estimate=cost(1e8, 4 * rows * total),
        name="slab_currents",
    )(keep, received, *others, local, before)


def pass_kernel(*refs, step, size):
    own_ref, arrived, out_ref = refs[0], refs[1:-1], refs[-1]
    for i in range(own_ref.shape[0] // size):
        here = slice(i * size, (i + 1) * size)
        total = plain(own_ref[here], False)
        for r, other in enumerate(arrived):
            at = ((2 * i + 1) << step) >> (r + 1)
            total += plain(other[at * size : (at + 1) * size], False)
        out_ref[here] = coded(total, WINDOW // 2)


def pass_on(own, arrived, step, size):
    return pl.pallas_call(
        functools.partial(pass_kernel, step=step, size=size),
        out_shape=jax.ShapeDtypeStruct(own.shape, BF16),
        in_specs=[vmem()] * (1 + len(arrived)),
        out_specs=vmem(),
        compiler_params=params(),
        cost_estimate=cost(1e6, 4 * math.prod(own.shape)),
        name="pass_on",
    )(own, *arrived)


def signal_kernel(*refs, wire_taps):
    parts, (table_ref, out_ref, token_ref, even_ref, odd_ref, level_ref, lines_ref) = refs[:-7], refs[-7:]
    token_ref[...] = jnp.zeros(token_ref.shape, F32)
    blocks, span = table_ref.shape[1], table_ref.shape[3]
    wires = out_ref.shape[1]
    half = (wire_taps - 1) // 2
    step = span * 16 // LANES
    currents = plain(parts[0][...], False)
    for part in parts[1:]:
        currents += plain(part[...], False)
    middle = WINDOW // 2
    level = currents[:, middle : middle + 1].astype(BF16).astype(F32)
    level = jnp.broadcast_to(level, currents.shape)
    level_ref[...] = level
    currents = currents - level
    lane = lax.broadcasted_iota(jnp.int32, (wires, LANES), 1)
    levels = jnp.zeros((wires, LANES), F32)
    for a in range(wire_taps):
        at = EDGE - half + a
        here = (lane == WINDOW + a) | (lane == WINDOW + wire_taps + a)
        levels = jnp.where(here, level_ref[at : at + wires], levels)
    for block in range(blocks):
        even_ref[...] = pltpu.roll(currents, (-step * block) % LANES, 1)
        odd_ref[...] = pltpu.roll(currents, (WINDOW - step * block) % LANES, 1)
        for pair in range((wire_taps + 1) // 2):
            at = EDGE - half + 2 * pair
            right = levels
            if 2 * pair + 1 < wire_taps:
                right = odd_ref[at + 1 : at + 1 + wires]
            line = jnp.where(lane < WINDOW, even_ref[at : at + wires], right)
            lines_ref[:, pair * LANES : (pair + 1) * LANES] = line.astype(BF16)
        out_ref[0, :, block * span : (block + 1) * span] = jnp.dot(
            lines_ref[...], table_ref[pl.program_id(0), block], preferred_element_type=F32
        ).astype(BF16)


def forward(parts, table, wires, wire_taps):
    planes, blocks, depth, span = table.shape
    extent = wires + 2 * EDGE
    part = pl.BlockSpec((extent, LANES), lambda p: (p, 0))
    return pl.pallas_call(
        functools.partial(signal_kernel, wire_taps=wire_taps),
        grid=(planes,),
        out_shape=(
            jax.ShapeDtypeStruct((planes, wires, blocks * span), BF16),
            jax.ShapeDtypeStruct((8, LANES), F32),
        ),
        in_specs=[part] * len(parts) + [vmem()],
        out_specs=(
            pl.BlockSpec((1, wires, blocks * span), lambda p: (p, 0, 0)),
            pl.BlockSpec((8, LANES), lambda p: (0, 0)),
        ),
        scratch_shapes=[
            pltpu.VMEM((extent, LANES), F32),
            pltpu.VMEM((extent, LANES), F32),
            pltpu.VMEM((extent, LANES), F32),
            pltpu.VMEM((wires, depth), BF16),
        ],
        compiler_params=params(("arbitrary",)),
        cost_estimate=cost(4e9, 2 * math.prod(table.shape)),
        name="signal",
    )(*parts, table)


def local(charge, intersection, ovl_block, ovl_count, diff_class, response, cotangent):
    total = charge.shape[1]
    owners = lax.axis_size("gz")
    slabs = lax.axis_size("drift")
    planes, wires, ticks = cotangent.shape
    wire_taps = response.shape[1]
    bins = total // slabs

    currents, keep, give, local_currents = cut_pieces(
        ovl_block, ovl_count, charge, intersection, cotangent, owners
    )
    received = swap(give, "gz", 1)
    sums, edges = relay(keep, received) if owners > 2 else ((), ())
    beyond = [swap(block, "gz", 2 * j) for j, block in enumerate(edges, 1)]
    others = [swap(block, "gz", 2 * j) for j, block in enumerate(sums, 1)]

    before = sums[0] if sums else received
    levels, kinds = smeared_levels(diff_class, response, bins, slabs, before)
    table = build_table(levels, kinds, planes, wire_taps, ticks)
    partial = backward(table, cotangent, received, beyond, wire_taps)
    spread = [partial] + [swap(partial, "drift", k) for k in range(1, slabs)]

    cuts = cut_slabs(currents, received, others, local_currents, bins, slabs, partial)
    windows, ready = [cuts[0]], cuts[0]
    for step, block in enumerate(cuts[1:]):
        if step:
            block = ready = pass_on(block, windows[1:], step, cuts[0].shape[0])
        windows.append(swap(block, "drift", 1 << step))

    cross, own = merge(spread, bins, total, ready)
    if owners == 4:
        across = swap(cross, "gz", 2)
        sources = [cross, swap(cross, "gz", 1), across, swap(across, "gz", 1)]
    else:
        sources = [lax.all_gather(cross, "gz", axis=0)]
    signal, done = forward(windows, table, wires, wire_taps)
    charge_grad = charge_gradient(
        ovl_block, ovl_count, sources, own, intersection, owners, done
    )
    return signal, charge_grad


def solution(mesh):
    return jax.shard_map(
        local,
        mesh=mesh,
        in_specs=(
            P(("apa", "gz", "drift"), None),
            P(("apa", "gz", "drift"), None, None, None, None),
            P(("apa", "gz", "drift"), None, None),
            P(("apa", "gz", "drift"), None),
            P("apa"),
            P(),
            P("apa", "gz", "drift"),
        ),
        out_specs=(P("apa", "gz", "drift"), P(("apa", "gz", "drift"), None)),
        check_vma=False,
    )
```

```python
import functools
import math

import jax
import jax.numpy as jnp
from jax import lax
from jax.experimental import pallas as pl
from jax.experimental.pallas import tpu as pltpu
from jax.sharding import PartitionSpec as P

TPB = 8
HB = 2
CLASSES = 6
LANES = 128
EDGE = 16
GROUP = 8
WINDOW = 64
LEAD = HB * TPB - TPB // 2
VMEM_LIMIT = 24 * 1024 * 1024
WHOLE_VMEM = 61 * 1024 * 1024
BF16 = jnp.bfloat16
F32 = jnp.float32


def params(semantics=None, limit=VMEM_LIMIT):
    return pltpu.CompilerParams(vmem_limit_bytes=limit, dimension_semantics=semantics)


def vmem():
    return pl.BlockSpec(memory_space=pltpu.VMEM)


def smem():
    return pl.BlockSpec(memory_space=pltpu.SMEM)


def anywhere():
    return pl.BlockSpec(memory_space=pl.ANY)


def cost(flops, moved):
    return pl.CostEstimate(flops=int(flops), bytes_accessed=int(moved), transcendentals=0)


def swap(block, axis, distance):
    count = lax.axis_size(axis)
    return lax.ppermute(block, axis, [(i, i ^ distance) for i in range(count)])


def widths(number):
    spread = TPB * (0.2 + 0.15 * number)
    half = HB * TPB
    total = sum(math.exp(-((j + 0.5) ** 2) / (2.0 * spread * spread)) for j in range(-half, half))
    return 1.0 / (2.0 * spread * spread), 1.0 / total


def shared_lanes(left, right, shift, lane):
    if shift == 0:
        return left
    back = LANES - shift
    return jnp.where(lane < back, pltpu.roll(left, back, 1), pltpu.roll(right, back, 1))


def coded(rows, column):
    lane = lax.broadcasted_iota(jnp.int32, rows.shape, 1)
    level = jnp.broadcast_to(rows[:, column : column + 1].astype(BF16).astype(F32), rows.shape)
    return jnp.where(lane == 0, level, rows - level).astype(BF16)


def plain(rows, first):
    rows = rows.astype(F32)
    lane = lax.broadcasted_iota(jnp.int32, rows.shape, 1)
    level = jnp.broadcast_to(rows[:, :1], rows.shape)
    return jnp.where(lane == 0, level if first else jnp.zeros_like(rows), rows + level)


def levels_kernel(packed_ref, _, level_ref, kind_ref, *, bins, slabs, total):
    rows = level_ref.shape[0]
    groups = kind_ref.shape[0]
    slab = lax.axis_index("drift")
    lane = lax.broadcasted_iota(jnp.int32, (GROUP, LANES), 1)
    packed = packed_ref[rows:].astype(F32)
    tiles = []
    for t in range(total // LANES):
        at = slice(t % 2 * LANES, (t % 2 + 1) * LANES)
        tiles.append(jnp.broadcast_to(packed[t // 2 : t // 2 + 1, at], (GROUP, LANES)))
    classes = tiles[0]
    none = jnp.zeros((GROUP, LANES), F32)
    numbers = none
    for source in range(slabs):
        at = source * bins - (WINDOW // 2 - HB)
        tile, shift = at // LANES, at % LANES
        pair = [tiles[t] if 0 <= t < len(tiles) else none for t in (tile, tile + 1)]
        numbers = jnp.where(slab == source, shared_lanes(pair[0], pair[1], shift, lane), numbers)
    x = slab * bins - (WINDOW // 2 - HB) + lane
    numbers = jnp.where((x >= 0) & (x < HB), (CLASSES + x).astype(F32), numbers)
    column = jnp.broadcast_to(numbers[:1], (LANES, LANES)).T.astype(jnp.int32)
    for m in range(groups):
        kind_ref[m] = column[m * GROUP : (m + 1) * GROUP]
    taps = packed_ref[:rows]
    tap = lax.broadcasted_iota(jnp.int32, (LANES, 2 * LANES), 0)
    tick = lax.broadcasted_iota(jnp.int32, (LANES, 2 * LANES), 1)
    step = tick - tap - LEAD
    offset = step.astype(F32) - (TPB - 1) / 2.0
    squared = offset * offset
    inside = jnp.abs(offset) < HB * TPB
    for kind in range(CLASSES + HB):
        keep = inside
        if kind < CLASSES:
            narrow, scale = widths(kind)
        else:
            edge = kind - CLASSES
            narrow, scale = widths(0)
            for number in range(1, CLASSES):
                chosen = classes[:1, edge : edge + 1] == number
                narrow = jnp.where(chosen, widths(number)[0], narrow)
                scale = jnp.where(chosen, widths(number)[1], scale)
            keep = inside & (step >= -TPB * edge)
        smear = jnp.where(keep, jnp.exp(-(squared * narrow)) * scale, 0.0)
        high = smear.astype(BF16)
        low = (smear - high.astype(F32)).astype(BF16)
        near = jnp.dot(taps[:, :LANES], high, preferred_element_type=F32) + jnp.dot(
            taps[:, :LANES], low, preferred_element_type=F32
        )
        far = jnp.dot(taps[:, LANES:], high[:, :LANES], preferred_element_type=F32) + jnp.dot(
            taps[:, LANES:], low[:, :LANES], preferred_element_type=F32
        )
        level_ref[:, kind, :LANES] = near[:, :LANES]
        level_ref[:, kind, LANES:] = near[:, LANES:] + far


def packed_inputs(diff_class, response):
    planes, wire_taps, length = response.shape
    reach = 2 * LANES
    rows = -(-wire_taps // 8) * 8
    taps = jnp.pad(response, ((0, 0), (0, rows - wire_taps), (0, reach - length)))
    classes = jnp.pad(diff_class.astype(BF16), (0, 8 * reach - diff_class.shape[0]))
    return jnp.concatenate([taps.reshape(planes * rows, reach), classes.reshape(8, reach)], axis=0)


def smeared_levels(packed, bins, slabs, total, before):
    rows = packed.shape[0] - 8
    groups = (bins + WINDOW // 2) // GROUP
    return pl.pallas_call(
        functools.partial(levels_kernel, bins=bins, slabs=slabs, total=total),
        out_shape=(
            jax.ShapeDtypeStruct((rows, CLASSES + HB, 2 * LANES), F32),
            jax.ShapeDtypeStruct((groups, GROUP, LANES), jnp.int32),
        ),
        in_specs=[vmem(), anywhere()],
        out_specs=(vmem(), vmem()),
        compiler_params=params(),
        cost_estimate=cost(1e8, 1e6),
        name="levels",
    )(packed, before)


def table_kernel(level_ref, kind_ref, table_ref, sum_ref, *, wire_taps):
    planes, blocks, depth, span = table_ref.shape
    rows = level_ref.shape[0] // planes
    groups = kind_ref.shape[0]
    tiles = span // LANES
    lane = lax.broadcasted_iota(jnp.int32, (GROUP, LANES), 1)
    row = lax.broadcasted_iota(jnp.int32, (GROUP, LANES), 0)
    starts = [LEAD_SHIFT + odd * (LANES // 2) + TPB * row for odd in range(2)]
    after = [lane >= start for start in starts]
    zero = jnp.zeros((GROUP, LANES), F32)
    empty = jnp.zeros((2 * GROUP, LANES), BF16)

    def body(a, plane):
        levels = level_ref[plane * rows + a]
        halves = [levels[:, :LANES], levels[:, LANES:]]
        pieces = []
        for m in range(groups):
            odd = m % 2
            parts = [
                pltpu.roll(
                    jnp.take_along_axis(half, kind_ref[m], axis=0),
                    LEAD_SHIFT + odd * (LANES // 2),
                    1,
                    stride=TPB,
                    stride_axis=0,
                )
                for half in halves
            ]
            pieces.append(
                (
                    jnp.where(after[odd], parts[0], zero),
                    jnp.where(after[odd], parts[1], parts[0]),
                    jnp.where(after[odd], zero, parts[1]),
                )
            )
        for block in range(blocks):
            for tile in range(tiles):
                here = slice(tile * LANES, (tile + 1) * LANES)
                total = zero
                for quarter in range(WINDOW // (2 * GROUP)):
                    m = 2 * (tiles * block + quarter)
                    at = a * WINDOW + quarter * 2 * GROUP
                    at = pl.ds(pl.multiple_of(at, 2 * GROUP), 2 * GROUP)
                    third = tile - quarter + 2
                    value = empty
                    if 0 <= third <= 2 and m + 1 < groups:
                        value = jnp.concatenate(
                            [pieces[m][third], pieces[m + 1][third]], axis=0
                        ).astype(BF16)
                        total = total + pieces[m][third] + pieces[m + 1][third]
                    table_ref[plane, block, at, here] = value
                sum_ref[a, block, :, here] = total
        return plane

    def whole_plane(plane, _):
        lax.fori_loop(0, wire_taps, body, plane, unroll=UNROLL)
        for block in range(blocks):
            total = jnp.sum(sum_ref[:, block], axis=1)
            high = total.astype(BF16).astype(F32)
            spare = jnp.zeros((depth - (WINDOW + 2) * wire_taps, span), F32)
            table_ref[plane, block, wire_taps * WINDOW :, :] = jnp.concatenate(
                [high, total - high, spare], axis=0
            ).astype(BF16)
        return 0

    lax.fori_loop(0, planes, whole_plane, 0)


UNROLL = 7
LEAD_SHIFT = (TPB * HB - LEAD) % LANES


def build_table(levels, kinds, planes, wire_taps, ticks_here):
    tiles = math.gcd(ticks_here, 2 * LANES) // LANES
    blocks = ticks_here // (tiles * LANES)
    shape = (planes, blocks, (wire_taps + 1) * WINDOW, tiles * LANES)
    return pl.pallas_call(
        functools.partial(table_kernel, wire_taps=wire_taps),
        out_shape=jax.ShapeDtypeStruct(shape, BF16),
        in_specs=[vmem(), vmem()],
        out_specs=vmem(),
        scratch_shapes=[pltpu.VMEM((wire_taps, blocks, GROUP, tiles * LANES), F32)],
        compiler_params=params(),
        cost_estimate=cost(4e9, 2 * math.prod(shape)),
        name="table",
    )(levels, kinds)


def back_kernel(table_ref, own_ref, received_ref, *refs, wire_taps):
    others, (out_ref, cot_ref, wide_ref) = refs[:-3], refs[-3:]
    planes, blocks, _, span = table_ref.shape
    _, wires, ticks = own_ref.shape
    total = received_ref.shape[1]
    half = (wire_taps - 1) // 2
    parts = ticks // total
    size = packed_rows(planes, half)
    side = parts * size
    lows = received_ref.shape[0] - 2 * side
    even = lax.rem(lax.axis_index("gz"), 2) == 0
    lane = lax.broadcasted_iota(jnp.int32, (wires, LANES), 1)
    none = jnp.zeros((wires, LANES), F32)
    gap = jnp.zeros((EDGE - half, total), F32)
    step = span * 16 // LANES
    columns = (wire_taps + 1) // 2
    edges = []
    for part in range(parts):
        low = received_ref[lows + part * size : lows + (part + 1) * size].astype(F32)
        high = received_ref[lows + side + part * size : lows + side + (part + 1) * size].astype(F32)
        near = jnp.where(even, low, high)
        far = jnp.zeros((size, total), F32)
        for other in others:
            far += other[part * size : (part + 1) * size].astype(F32)
        edges.append((jnp.where(even, far, near), jnp.where(even, near, far)))
    for plane in range(planes):
        cot_ref[plane, EDGE : EDGE + wires] = own_ref[plane]
        for part in range(parts):
            here = slice(part * total, (part + 1) * total)
            before, after = [edge[plane * half : (plane + 1) * half] for edge in edges[part]]
            cot_ref[plane, :EDGE, here] = jnp.concatenate([gap, before], axis=0).astype(BF16)
            cot_ref[plane, EDGE + wires :, here] = jnp.concatenate([after, gap], axis=0).astype(BF16)
        result = none
        for block in range(blocks):
            i = (plane * blocks + block) % wide_ref.shape[0]
            wide = lax.dot_general(
                cot_ref[plane, :, block * span : (block + 1) * span],
                table_ref[plane, block, : columns * LANES],
                (((1,), (1,)), ((), ())),
                preferred_element_type=F32,
            )
            for column in range(columns):
                wide_ref[i, column] = wide[:, column * LANES : (column + 1) * LANES]
            left, right = none, none
            for column in range(columns):
                at = EDGE + half - 2 * column
                left += wide_ref[i, column, at : at + wires]
                if 2 * column + 1 < wire_taps:
                    right += wide_ref[i, column, at - 1 : at - 1 + wires]
            both = jnp.where(lane < WINDOW, left + pltpu.roll(right, WINDOW, 1), none)
            result += pltpu.roll(both, block * step, 1) if block else both
        out_ref[plane] = result.astype(BF16)


def backward(table, cotangent, received, others, wire_taps):
    planes, _, _, _ = table.shape
    _, wires, ticks = cotangent.shape
    extent = wires + 2 * EDGE
    columns = (wire_taps + 1) // 2
    return pl.pallas_call(
        functools.partial(back_kernel, wire_taps=wire_taps),
        out_shape=jax.ShapeDtypeStruct((planes, wires, LANES), BF16),
        in_specs=[vmem()] * (3 + len(others)),
        out_specs=vmem(),
        scratch_shapes=[
            pltpu.VMEM((planes, extent, ticks), BF16),
            pltpu.VMEM((2, columns, extent, LANES), F32),
        ],
        compiler_params=params(),
        cost_estimate=cost(4e9, 2 * math.prod(table.shape)),
        name="bin_gradients",
    )(table, cotangent, received, *others)


def merge_kernel(*refs, bins, lead):
    parts, (cross_ref, local_ref, slab_ref) = refs[:-4], refs[-3:]
    planes, wires, _ = parts[0].shape
    total = local_ref.shape[1]
    slab = lax.axis_index("drift")
    for k, part in enumerate(parts):
        slab_ref[slab ^ k] = part[...]
    lane = lax.broadcasted_iota(jnp.int32, (wires, LANES), 1)
    none = jnp.zeros((wires, LANES), F32)
    for p in range(planes):
        tiles = [none] * (total // LANES)
        for source in range(len(parts)):
            values = slab_ref[source, p].astype(F32)
            tile, shift = (source * bins - lead) // LANES, (source * bins - lead) % LANES
            if shift:
                values = pltpu.roll(values, shift, 1)
            for t, inside in ((tile, lane >= shift), (tile + 1, lane < shift)):
                if 0 <= t < len(tiles):
                    tiles[t] += jnp.where(inside, values, none)
        for t, values in enumerate(tiles):
            here = slice(t * LANES, (t + 1) * LANES)
            if p < planes - 1:
                cross_ref[p, :, here] = values.astype(BF16)
            else:
                local_ref[:, here] = values.astype(BF16)


def merge(parts, bins, total, before):
    planes, wires, _ = parts[0].shape
    return pl.pallas_call(
        functools.partial(merge_kernel, bins=bins, lead=WINDOW // 2 - HB),
        out_shape=(
            jax.ShapeDtypeStruct((planes - 1, wires, total), BF16),
            jax.ShapeDtypeStruct((wires, total), BF16),
        ),
        in_specs=[vmem()] * len(parts) + [anywhere()],
        out_specs=(vmem(), vmem()),
        scratch_shapes=[pltpu.VMEM((len(parts), planes, wires, LANES), BF16)],
        compiler_params=params(),
        cost_estimate=cost(1e8, 4 * planes * wires * total),
        name="merge_bins",
    )(*parts, before)


def charge_kernel(block_ref, count_ref, *refs):
    sources, (local_ref, share_ref, _, out_hbm) = refs[:-8], refs[-8:-4]
    all_ref, chosen_ref, out_ref, sems = refs[-4:]
    cells, planes, entries, wire_block, width = share_ref.shape
    owners, _, wires, total = all_ref.shape
    per_owner = wires // wire_block
    z = lax.axis_index("gz")
    if len(sources) == 1:
        all_ref[...] = sources[0][...]
    else:
        for k, source in enumerate(sources):
            all_ref[z ^ k] = source[...]
    empty = jnp.zeros((wire_block, total), BF16)
    stores = []
    for b in range(cells):
        for p in range(planes):
            for k in range(entries):
                name = block_ref[p, k, b]
                if p < planes - 1:
                    name = jnp.clip(name, 0, owners * per_owner - 1)
                    owner = name // per_owner
                    start = pl.multiple_of((name - owner * per_owner) * wire_block, wire_block)
                    rows = all_ref[owner, p, pl.ds(start, wire_block), :]
                else:
                    name = jnp.clip(name - z * per_owner, 0, per_owner - 1)
                    start = pl.multiple_of(name * wire_block, wire_block)
                    rows = local_ref[pl.ds(start, wire_block), :]
                at = (p * entries + k) * wire_block
                chosen_ref[b, at : at + wire_block] = jnp.where(k < count_ref[b, p], rows, empty)
        here = slice(b * width, (b + 1) * width)
        out_ref[here] = lax.dot_general(
            share_ref[b].reshape(planes * entries * wire_block, width),
            chosen_ref[b],
            (((0,), (0,)), ((), ())),
            preferred_element_type=F32,
        ).astype(BF16)
        store = pltpu.make_async_copy(out_ref.at[here], out_hbm.at[here], sems.at[b])
        store.start()
        stores.append(store)
    for store in stores:
        store.wait()


def charge_gradient(ovl_block, ovl_count, sources, local, intersection, owners, before):
    cells, planes, entries, wire_block, width = intersection.shape
    wires, total = local.shape
    shape = (owners, planes - 1, wires, total)
    return pl.pallas_call(
        charge_kernel,
        out_shape=jax.ShapeDtypeStruct((cells * width, total), BF16),
        in_specs=[smem(), smem()] + [vmem()] * (len(sources) + 3),
        out_specs=anywhere(),
        scratch_shapes=[
            pltpu.VMEM(shape, BF16),
            pltpu.VMEM((cells, planes * entries * wire_block, total), BF16),
            pltpu.VMEM((cells * width, total), BF16),
            pltpu.SemaphoreType.DMA((cells,)),
        ],
        compiler_params=params(),
        cost_estimate=cost(1e8, 2 * math.prod(shape)),
        name="charge_gradient",
    )(jnp.transpose(ovl_block, (1, 2, 0)), ovl_count, *sources, local, intersection, before)


def pieces_kernel(
    block_hbm, count_hbm, charge_hbm, share_hbm, cot_hbm, own_hbm, keep_hbm, give_hbm, local_hbm,
    block_ref, count_ref, charge_ref, share_ref, edge_ref, cross_ref, own_ref, keep_ref, give_ref, local_ref,
    sems, out_sems, *, half,
):
    cells, planes, entries, wire_block, width = share_ref.shape
    wires, total = local_ref.shape
    ticks = edge_ref.shape[3]
    per_owner = wires // wire_block
    cut = own_ref.shape[0]
    halves = 1 + keep_ref.shape[0]
    owners = 2 * halves
    z = lax.axis_index("gz")
    loads = [
        pltpu.make_async_copy(source, target, sems.at[i])
        for i, (source, target) in enumerate(
            (
                (block_hbm, block_ref),
                (count_hbm, count_ref),
                (charge_hbm, charge_ref),
                (share_hbm, share_ref),
                (cot_hbm.at[:, :EDGE], edge_ref.at[0]),
                (cot_hbm.at[:, wires - EDGE :], edge_ref.at[1]),
            )
        )
    ]
    for load in loads:
        load.start()
    cross_ref[...] = jnp.zeros(cross_ref.shape, F32)
    local_ref[...] = jnp.zeros(local_ref.shape, F32)
    for load in loads:
        load.wait()
    for b in range(cells):
        pieces = (
            jnp.dot(
                share_ref[b].reshape(planes * entries * wire_block, width),
                charge_ref[b * width : (b + 1) * width],
                preferred_element_type=F32,
            )
            .astype(BF16)
            .astype(F32)
        )
        for p in range(planes):
            for k in range(entries):
                at = (p * entries + k) * wire_block
                piece = pieces[at : at + wire_block]
                piece = jnp.where(k < count_ref[b, p], piece, jnp.zeros_like(piece))
                name = block_ref[p, k, b]
                if p < planes - 1:
                    name = jnp.clip(name, 0, owners * per_owner - 1)
                    start = pl.multiple_of(EDGE + name * wire_block, EDGE)
                    cross_ref[p, pl.ds(start, wire_block)] += piece
                else:
                    name = jnp.clip(name - z * per_owner, 0, per_owner - 1)
                    start = pl.multiple_of(name * wire_block, wire_block)
                    local_ref[pl.ds(start, wire_block)] += piece
    at = halves * cut
    gap = jnp.zeros((packed_rows(planes, half) - planes * half, ticks), F32)
    for side, first in ((0, 0), (1, EDGE - half)):
        rows = [edge_ref[side, p].astype(F32)[first : first + half] for p in range(planes)]
        rows = jnp.concatenate(rows + [gap], axis=0).astype(BF16)
        for part in range(ticks // total):
            give_ref[at : at + rows.shape[0]] = rows[:, part * total : (part + 1) * total]
            at += rows.shape[0]
    extent = wires + 2 * EDGE
    none = jnp.zeros((EDGE, total), F32)
    stores = [
        pltpu.make_async_copy(source, target, out_sems.at[i])
        for i, (source, target) in enumerate(
            (
                (give_ref, give_hbm),
                (keep_ref, keep_hbm),
                (own_ref, own_hbm),
                (local_ref, local_hbm),
            )
        )
    ]
    stores[3].start()
    for k in [*range(1, owners, 2), *range(2, owners, 2), 0]:
        to = z ^ k
        blocks = [
            cross_ref[p, pl.ds(pl.multiple_of(to * wires, EDGE), extent)] for p in range(planes - 1)
        ]
        blocks.append(jnp.where(to == z + 1, local_ref[wires - EDGE :], none))
        blocks.append(jnp.where(to == z - 1, local_ref[:EDGE], none))
        at = 0
        for rows in blocks:
            here = slice(at, at + rows.shape[0])
            at += rows.shape[0]
            if k % 2:
                give_ref[k // 2 * cut + here.start : k // 2 * cut + here.stop] = coded(rows, 0)
            elif k:
                keep_ref[k // 2 - 1, here] = coded(rows, 0)
            else:
                own_ref[here] = rows
        if k == owners - 1:
            stores[0].start()
        if k == owners - 2 and k:
            stores[1].start()
    if owners == 2:
        stores[1].start()
    stores[2].start()
    for store in stores:
        store.wait()


def packed_rows(planes, half):
    return -(-planes * half // 16) * 16


def cut_pieces(ovl_block, ovl_count, charge, intersection, cotangent, owners, half):
    cells, planes, entries, wire_block, width = intersection.shape
    total = charge.shape[1]
    _, wires, ticks = cotangent.shape
    rows = (planes - 1) * (wires + 2 * EDGE) + 2 * EDGE
    edges = 2 * packed_rows(planes, half) * ticks // total
    hbm = pl.BlockSpec(memory_space=pltpu.HBM)
    blocks = jnp.transpose(ovl_block, (1, 2, 0))
    outs = (
        jax.ShapeDtypeStruct((rows, total), F32),
        jax.ShapeDtypeStruct((owners // 2 - 1, rows, total), BF16),
        jax.ShapeDtypeStruct((owners // 2 * rows + edges, total), BF16),
        jax.ShapeDtypeStruct((wires, total), F32),
    )
    return pl.pallas_call(
        functools.partial(pieces_kernel, half=half),
        out_shape=outs,
        in_specs=[hbm] * 5,
        out_specs=(hbm,) * 4,
        scratch_shapes=[
            pltpu.SMEM(blocks.shape, jnp.int32),
            pltpu.SMEM(ovl_count.shape, jnp.int32),
            pltpu.VMEM(charge.shape, BF16),
            pltpu.VMEM(intersection.shape, BF16),
            pltpu.VMEM((2, planes, EDGE, ticks), BF16),
            pltpu.VMEM((planes - 1, owners * wires + 2 * EDGE, total), F32),
            *[pltpu.VMEM(out.shape, out.dtype) for out in outs],
            pltpu.SemaphoreType.DMA((6,)),
            pltpu.SemaphoreType.DMA((4,)),
        ],
        compiler_params=params(limit=WHOLE_VMEM),
        cost_estimate=cost(1e8, 4 * owners * rows * total),
        name="pieces",
    )(blocks, ovl_count, charge, intersection, cotangent)


def relay_kernel(keep_ref, received_ref, *outs):
    others, rows, _ = keep_ref.shape
    edges = (received_ref.shape[0] - (others + 1) * rows) // 2
    z = lax.axis_index("gz")
    even = lax.rem(z, 2) == 0
    low = received_ref[(others + 1) * rows : (others + 1) * rows + edges]
    high = received_ref[(others + 1) * rows + edges :]
    for j in range(others):
        to = z ^ (2 * (j + 1))
        summed = plain(keep_ref[j], True)
        summed += plain(received_ref[(j + 1) * rows : (j + 2) * rows], True)
        outs[j][...] = coded(summed, 0)
        upward, downward = even & (to == z + 2), jnp.logical_not(even) & (to == z - 2)
        outs[others + j][...] = jnp.where(
            upward, high, jnp.where(downward, low, jnp.zeros_like(low))
        )


def relay(keep, received):
    others, rows, total = keep.shape
    edges = (received.shape[0] - (others + 1) * rows) // 2
    outs = pl.pallas_call(
        relay_kernel,
        out_shape=(jax.ShapeDtypeStruct((rows, total), BF16),) * others
        + (jax.ShapeDtypeStruct((edges, total), BF16),) * others,
        in_specs=[vmem(), vmem()],
        out_specs=(vmem(),) * (2 * others),
        compiler_params=params(),
        cost_estimate=cost(1e7, 6 * others * rows * total),
        name="relay",
    )(keep, received)
    return outs[:others], outs[others:]


def slabs_kernel(*refs, bins, lead, slabs):
    count = len(refs) - slabs.bit_length() - 1
    keep_ref, received_ref, others, local_ref = refs[0], refs[1], refs[2 : count - 2], refs[count - 2]
    outs, cut_ref = refs[count:-1], refs[-1]
    total = local_ref.shape[1]
    cut = keep_ref.shape[0]
    summed = keep_ref[...] + plain(received_ref[:cut], True)
    for other in others:
        summed += plain(other[...], True)
    edge = cut - 2 * EDGE
    rows = jnp.concatenate(
        [summed[:edge], summed[edge : edge + EDGE], local_ref[...], summed[edge + EDGE :]], axis=0
    )
    none = jnp.zeros((rows.shape[0], LANES), F32)
    lane = lax.broadcasted_iota(jnp.int32, none.shape, 1)
    level = jnp.broadcast_to(rows[:, :1].astype(BF16).astype(F32), none.shape)
    tiles = [rows[:, t * LANES : (t + 1) * LANES] - level for t in range(total // LANES)]
    for to in range(slabs):
        at = to * bins - lead
        tile, shift = at // LANES, at % LANES
        pair = [tiles[t] if 0 <= t < len(tiles) else -level for t in (tile, tile + 1)]
        value = shared_lanes(pair[0], pair[1], shift, lane)
        cut_ref[to] = jnp.where(lane == 0, level, value).astype(BF16)
    slab = lax.axis_index("drift")
    outs[0][...] = cut_ref[slab]
    size = rows.shape[0]
    for s, out in enumerate(outs[1:]):
        for i in range(slabs >> (s + 1)):
            out[i * size : (i + 1) * size] = cut_ref[slab ^ ((2 * i + 1) << s)]


def cut_slabs(keep, received, others, local, bins, slabs, before):
    wires, total = local.shape
    rows = keep.shape[0] + wires
    steps = slabs.bit_length() - 1
    counts = [1] + [slabs >> (s + 1) for s in range(steps)]
    return pl.pallas_call(
        functools.partial(slabs_kernel, bins=bins, lead=WINDOW // 2 - HB, slabs=slabs),
        out_shape=tuple(jax.ShapeDtypeStruct((n * rows, LANES), BF16) for n in counts),
        in_specs=[vmem()] * (3 + len(others)) + [anywhere()],
        out_specs=(vmem(),) * len(counts),
        scratch_shapes=[pltpu.VMEM((slabs, rows, LANES), BF16)],
        compiler_params=params(),
        cost_estimate=cost(1e8, 4 * rows * total),
        name="slab_currents",
    )(keep, received, *others, local, before)


def pass_kernel(*refs, step, size):
    own_ref, arrived, out_ref = refs[0], refs[1:-1], refs[-1]
    for i in range(own_ref.shape[0] // size):
        here = slice(i * size, (i + 1) * size)
        total = plain(own_ref[here], False)
        for r, other in enumerate(arrived):
            at = ((2 * i + 1) << step) >> (r + 1)
            total += plain(other[at * size : (at + 1) * size], False)
        out_ref[here] = coded(total, WINDOW // 2)


def pass_on(own, arrived, step, size):
    return pl.pallas_call(
        functools.partial(pass_kernel, step=step, size=size),
        out_shape=jax.ShapeDtypeStruct(own.shape, BF16),
        in_specs=[vmem()] * (1 + len(arrived)),
        out_specs=vmem(),
        compiler_params=params(),
        cost_estimate=cost(1e6, 4 * math.prod(own.shape)),
        name="pass_on",
    )(own, *arrived)


def signal_kernel(*refs, wire_taps):
    parts, (table_ref, out_hbm, token_ref) = refs[:-9], refs[-9:-6]
    even_ref, odd_ref, level_ref, lines_ref, out_ref, sems = refs[-6:]
    planes, blocks, _, span = table_ref.shape
    _, wires, _ = out_ref.shape
    extent = wires + 2 * EDGE
    half = (wire_taps - 1) // 2
    step = span * 16 // LANES
    middle = WINDOW // 2
    token_ref[...] = jnp.zeros(token_ref.shape, F32)
    lane = lax.broadcasted_iota(jnp.int32, (wires, LANES), 1)
    stores = []
    for p in range(planes):
        here = slice(p * extent, (p + 1) * extent)
        currents = plain(parts[0][here], False)
        for part in parts[1:]:
            currents += plain(part[here], False)
        level = currents[:, middle : middle + 1].astype(BF16).astype(F32)
        level = jnp.broadcast_to(level, currents.shape)
        level_ref[p] = level
        currents = currents - level
        levels = jnp.zeros((wires, LANES), F32)
        for a in range(wire_taps):
            at = EDGE - half + a
            both = (lane == WINDOW + a) | (lane == WINDOW + wire_taps + a)
            levels = jnp.where(both, level_ref[p, at : at + wires], levels)
        for block in range(blocks):
            i = p * blocks + block
            even_ref[i] = pltpu.roll(currents, (-step * block) % LANES, 1)
            odd_ref[i] = pltpu.roll(currents, (WINDOW - step * block) % LANES, 1)
            for pair in range((wire_taps + 1) // 2):
                at = EDGE - half + 2 * pair
                right = levels
                if 2 * pair + 1 < wire_taps:
                    right = odd_ref[i, at + 1 : at + 1 + wires]
                line = jnp.where(lane < WINDOW, even_ref[i, at : at + wires], right)
                lines_ref[i % 2, :, pair * LANES : (pair + 1) * LANES] = line.astype(BF16)
            out_ref[p, :, block * span : (block + 1) * span] = jnp.dot(
                lines_ref[i % 2], table_ref[p, block], preferred_element_type=F32
            ).astype(BF16)
        store = pltpu.make_async_copy(out_ref.at[p], out_hbm.at[p], sems.at[p])
        store.start()
        stores.append(store)
    for store in stores:
        store.wait()


def forward(parts, table, wires, wire_taps):
    planes, blocks, depth, span = table.shape
    extent = wires + 2 * EDGE
    shape = (planes, wires, blocks * span)
    return pl.pallas_call(
        functools.partial(signal_kernel, wire_taps=wire_taps),
        out_shape=(
            jax.ShapeDtypeStruct(shape, BF16),
            jax.ShapeDtypeStruct((8, LANES), F32),
        ),
        in_specs=[vmem()] * (len(parts) + 1),
        out_specs=(anywhere(), vmem()),
        scratch_shapes=[
            pltpu.VMEM((planes * blocks, extent, LANES), F32),
            pltpu.VMEM((planes * blocks, extent, LANES), F32),
            pltpu.VMEM((planes, extent, LANES), F32),
            pltpu.VMEM((2, wires, depth), BF16),
            pltpu.VMEM(shape, BF16),
            pltpu.SemaphoreType.DMA((planes,)),
        ],
        compiler_params=params(),
        cost_estimate=cost(4e9, 2 * math.prod(table.shape)),
        name="signal",
    )(*parts, table)


def local(charge, intersection, ovl_block, ovl_count, diff_class, response, cotangent):
    total = charge.shape[1]
    owners = lax.axis_size("gz")
    slabs = lax.axis_size("drift")
    planes, wires, ticks = cotangent.shape
    wire_taps = response.shape[1]
    bins = total // slabs

    currents, keep, give, local_currents = cut_pieces(
        ovl_block, ovl_count, charge, intersection, cotangent, owners, (wire_taps - 1) // 2
    )
    received = swap(give, "gz", 1)
    packed = packed_inputs(diff_class, response)
    sums, edges = relay(keep.astype(F32), received) if owners > 2 else ((), ())
    beyond = [swap(block, "gz", 2 * j) for j, block in enumerate(edges, 1)]
    others = [swap(block, "gz", 2 * j) for j, block in enumerate(sums, 1)]

    levels, kinds = smeared_levels(packed, bins, slabs, total, sums[0] if sums else received)
    table = build_table(levels, kinds, planes, wire_taps, ticks)
    partial = backward(table, cotangent, received, beyond, wire_taps)
    spread = [partial] + [swap(partial, "drift", k) for k in range(1, slabs)]

    cuts = cut_slabs(currents, received, others, local_currents, bins, slabs, partial)
    windows, ready = [cuts[0]], cuts[0]
    for step, block in enumerate(cuts[1:]):
        if step:
            block = ready = pass_on(block, windows[1:], step, cuts[0].shape[0])
        windows.append(swap(block, "drift", 1 << step))

    cross, own = merge(spread, bins, total, ready)
    if owners == 4:
        across = swap(cross, "gz", 2)
        sources = [cross, swap(cross, "gz", 1), across, swap(across, "gz", 1)]
    else:
        sources = [lax.all_gather(cross, "gz", axis=0)]
    signal, done = forward(windows, table, wires, wire_taps)
    charge_grad = charge_gradient(
        ovl_block, ovl_count, sources, own, intersection, owners, done
    )
    return signal, charge_grad


def solution(mesh):
    return jax.shard_map(
        local,
        mesh=mesh,
        in_specs=(
            P(("apa", "gz", "drift"), None),
            P(("apa", "gz", "drift"), None, None, None, None),
            P(("apa", "gz", "drift"), None, None),
            P(("apa", "gz", "drift"), None),
            P("apa"),
            P(),
            P("apa", "gz", "drift"),
        ),
        out_specs=(P("apa", "gz", "drift"), P(("apa", "gz", "drift"), None)),
        check_vma=False,
    )
```

```python
import functools
import math

import jax
import jax.numpy as jnp
from jax import lax
from jax.experimental import pallas as pl
from jax.experimental.pallas import tpu as pltpu
from jax.sharding import PartitionSpec as P

TPB = 8
HB = 2
CLASSES = 6
LANES = 128
EDGE = 16
GROUP = 8
WINDOW = 64
LEAD = HB * TPB - TPB // 2
VMEM_LIMIT = 24 * 1024 * 1024
WHOLE_VMEM = 61 * 1024 * 1024
BF16 = jnp.bfloat16
F32 = jnp.float32


def params(semantics=None, limit=VMEM_LIMIT):
    return pltpu.CompilerParams(vmem_limit_bytes=limit, dimension_semantics=semantics)


def vmem():
    return pl.BlockSpec(memory_space=pltpu.VMEM)


def smem():
    return pl.BlockSpec(memory_space=pltpu.SMEM)


def anywhere():
    return pl.BlockSpec(memory_space=pl.ANY)


def cost(flops, moved):
    return pl.CostEstimate(flops=int(flops), bytes_accessed=int(moved), transcendentals=0)


def swap(block, axis, distance):
    count = lax.axis_size(axis)
    return lax.ppermute(block, axis, [(i, i ^ distance) for i in range(count)])


def widths(number):
    spread = TPB * (0.2 + 0.15 * number)
    half = HB * TPB
    total = sum(math.exp(-((j + 0.5) ** 2) / (2.0 * spread * spread)) for j in range(-half, half))
    return 1.0 / (2.0 * spread * spread), 1.0 / total


def shared_lanes(left, right, shift, lane):
    if shift == 0:
        return left
    back = LANES - shift
    return jnp.where(lane < back, pltpu.roll(left, back, 1), pltpu.roll(right, back, 1))


def coded(rows, column):
    lane = lax.broadcasted_iota(jnp.int32, rows.shape, 1)
    level = jnp.broadcast_to(rows[:, column : column + 1].astype(BF16).astype(F32), rows.shape)
    return jnp.where(lane == 0, level, rows - level).astype(BF16)


def plain(rows, first):
    rows = rows.astype(F32)
    lane = lax.broadcasted_iota(jnp.int32, rows.shape, 1)
    level = jnp.broadcast_to(rows[:, :1], rows.shape)
    return jnp.where(lane == 0, level if first else jnp.zeros_like(rows), rows + level)


def levels_kernel(
    class_ref, response_ref, _, level_ref, kind_ref, flat_ref, *, bins, slabs, total
):
    planes, wire_taps, length = response_ref.shape
    rows = level_ref.shape[0] // planes
    groups = kind_ref.shape[0]
    slab = lax.axis_index("drift")
    lane = lax.broadcasted_iota(jnp.int32, (GROUP, LANES), 1)
    packed = class_ref[...].astype(F32)
    tiles = []
    for t in range(total // LANES):
        at = slice(t % 2 * LANES, (t % 2 + 1) * LANES)
        tiles.append(jnp.broadcast_to(packed[t // 2 : t // 2 + 1, at], (GROUP, LANES)))
    classes = tiles[0]
    none = jnp.zeros((GROUP, LANES), F32)
    numbers = none
    for source in range(slabs):
        at = source * bins - (WINDOW // 2 - HB)
        tile, shift = at // LANES, at % LANES
        pair = [tiles[t] if 0 <= t < len(tiles) else none for t in (tile, tile + 1)]
        numbers = jnp.where(slab == source, shared_lanes(pair[0], pair[1], shift, lane), numbers)
    x = slab * bins - (WINDOW // 2 - HB) + lane
    numbers = jnp.where((x >= 0) & (x < HB), (CLASSES + x).astype(F32), numbers)
    column = jnp.broadcast_to(numbers[:1], (LANES, LANES)).T.astype(jnp.int32)
    for m in range(groups):
        kind_ref[m] = column[m * GROUP : (m + 1) * GROUP]
    flat_ref[...] = jnp.zeros(flat_ref.shape, F32)
    for p in range(planes):
        flat_ref[p * rows : p * rows + wire_taps, :length] = response_ref[p].astype(F32)
    taps = flat_ref[...].astype(BF16)
    tap = lax.broadcasted_iota(jnp.int32, (LANES, 2 * LANES), 0)
    tick = lax.broadcasted_iota(jnp.int32, (LANES, 2 * LANES), 1)
    step = tick - tap - LEAD
    offset = step.astype(F32) - (TPB - 1) / 2.0
    squared = offset * offset
    inside = jnp.abs(offset) < HB * TPB
    for kind in range(CLASSES + HB):
        keep = inside
        if kind < CLASSES:
            narrow, scale = widths(kind)
        else:
            edge = kind - CLASSES
            narrow, scale = widths(0)
            for number in range(1, CLASSES):
                chosen = classes[:1, edge : edge + 1] == number
                narrow = jnp.where(chosen, widths(number)[0], narrow)
                scale = jnp.where(chosen, widths(number)[1], scale)
            keep = inside & (step >= -TPB * edge)
        smear = jnp.where(keep, jnp.exp(-(squared * narrow)) * scale, 0.0)
        high = smear.astype(BF16)
        low = (smear - high.astype(F32)).astype(BF16)
        near = jnp.dot(taps[:, :LANES], high, preferred_element_type=F32) + jnp.dot(
            taps[:, :LANES], low, preferred_element_type=F32
        )
        far = jnp.dot(taps[:, LANES:], high[:, :LANES], preferred_element_type=F32) + jnp.dot(
            taps[:, LANES:], low[:, :LANES], preferred_element_type=F32
        )
        level_ref[:, kind, :LANES] = near[:, :LANES]
        level_ref[:, kind, LANES:] = near[:, LANES:] + far


def smeared_levels(diff_class, response, bins, slabs, before):
    planes, wire_taps, _ = response.shape
    total = diff_class.shape[0]
    reach = 2 * LANES
    rows = -(-wire_taps // 8) * 8
    groups = (bins + WINDOW // 2) // GROUP
    classes = jnp.pad(diff_class.astype(BF16), (0, 8 * reach - total)).reshape(8, reach)
    return pl.pallas_call(
        functools.partial(levels_kernel, bins=bins, slabs=slabs, total=total),
        out_shape=(
            jax.ShapeDtypeStruct((planes * rows, CLASSES + HB, reach), F32),
            jax.ShapeDtypeStruct((groups, GROUP, LANES), jnp.int32),
        ),
        in_specs=[vmem(), vmem(), anywhere()],
        out_specs=(vmem(), vmem()),
        scratch_shapes=[pltpu.VMEM((planes * rows, reach), F32)],
        compiler_params=params(),
        cost_estimate=cost(1e8, 1e6),
        name="levels",
    )(classes, response, before)


def table_kernel(level_ref, kind_ref, table_ref, sum_ref, *, wire_taps):
    planes, blocks, depth, span = table_ref.shape
    rows = level_ref.shape[0] // planes
    groups = kind_ref.shape[0]
    tiles = span // LANES
    lane = lax.broadcasted_iota(jnp.int32, (GROUP, LANES), 1)
    row = lax.broadcasted_iota(jnp.int32, (GROUP, LANES), 0)
    starts = [LEAD_SHIFT + odd * (LANES // 2) + TPB * row for odd in range(2)]
    after = [lane >= start for start in starts]
    zero = jnp.zeros((GROUP, LANES), F32)
    empty = jnp.zeros((2 * GROUP, LANES), BF16)

    def body(a, plane):
        levels = level_ref[plane * rows + a]
        halves = [levels[:, :LANES], levels[:, LANES:]]
        pieces = []
        for m in range(groups):
            odd = m % 2
            parts = [
                pltpu.roll(
                    jnp.take_along_axis(half, kind_ref[m], axis=0),
                    LEAD_SHIFT + odd * (LANES // 2),
                    1,
                    stride=TPB,
                    stride_axis=0,
                )
                for half in halves
            ]
            pieces.append(
                (
                    jnp.where(after[odd], parts[0], zero),
                    jnp.where(after[odd], parts[1], parts[0]),
                    jnp.where(after[odd], zero, parts[1]),
                )
            )
        for block in range(blocks):
            for tile in range(tiles):
                here = slice(tile * LANES, (tile + 1) * LANES)
                total = zero
                for quarter in range(WINDOW // (2 * GROUP)):
                    m = 2 * (tiles * block + quarter)
                    at = a * WINDOW + quarter * 2 * GROUP
                    at = pl.ds(pl.multiple_of(at, 2 * GROUP), 2 * GROUP)
                    third = tile - quarter + 2
                    value = empty
                    if 0 <= third <= 2 and m + 1 < groups:
                        value = jnp.concatenate(
                            [pieces[m][third], pieces[m + 1][third]], axis=0
                        ).astype(BF16)
                        total = total + pieces[m][third] + pieces[m + 1][third]
                    table_ref[plane, block, at, here] = value
                sum_ref[a, block, :, here] = total
        return plane

    def whole_plane(plane, _):
        lax.fori_loop(0, wire_taps, body, plane, unroll=UNROLL)
        for block in range(blocks):
            total = jnp.sum(sum_ref[:, block], axis=1)
            high = total.astype(BF16).astype(F32)
            spare = jnp.zeros((depth - (WINDOW + 2) * wire_taps, span), F32)
            table_ref[plane, block, wire_taps * WINDOW :, :] = jnp.concatenate(
                [high, total - high, spare], axis=0
            ).astype(BF16)
        return 0

    lax.fori_loop(0, planes, whole_plane, 0)


UNROLL = 7
LEAD_SHIFT = (TPB * HB - LEAD) % LANES


def build_table(levels, kinds, planes, wire_taps, ticks_here):
    tiles = math.gcd(ticks_here, 2 * LANES) // LANES
    blocks = ticks_here // (tiles * LANES)
    shape = (planes, blocks, (wire_taps + 1) * WINDOW, tiles * LANES)
    return pl.pallas_call(
        functools.partial(table_kernel, wire_taps=wire_taps),
        out_shape=jax.ShapeDtypeStruct(shape, BF16),
        in_specs=[vmem(), vmem()],
        out_specs=vmem(),
        scratch_shapes=[pltpu.VMEM((wire_taps, blocks, GROUP, tiles * LANES), F32)],
        compiler_params=params(),
        cost_estimate=cost(4e9, 2 * math.prod(shape)),
        name="table",
    )(levels, kinds)


def back_kernel(table_ref, own_ref, received_ref, *refs, wire_taps):
    others, (out_ref, cot_ref, wide_ref) = refs[:-3], refs[-3:]
    planes, blocks, _, span = table_ref.shape
    _, wires, ticks = own_ref.shape
    total = received_ref.shape[1]
    half = (wire_taps - 1) // 2
    parts = ticks // total
    size = packed_rows(planes, half)
    side = parts * size
    lows = received_ref.shape[0] - 2 * side
    even = lax.rem(lax.axis_index("gz"), 2) == 0
    lane = lax.broadcasted_iota(jnp.int32, (wires, LANES), 1)
    none = jnp.zeros((wires, LANES), F32)
    gap = jnp.zeros((EDGE - half, total), F32)
    step = span * 16 // LANES
    columns = (wire_taps + 1) // 2
    edges = []
    for part in range(parts):
        low = received_ref[lows + part * size : lows + (part + 1) * size].astype(F32)
        high = received_ref[lows + side + part * size : lows + side + (part + 1) * size].astype(F32)
        near = jnp.where(even, low, high)
        far = jnp.zeros((size, total), F32)
        for other in others:
            far += other[part * size : (part + 1) * size].astype(F32)
        edges.append((jnp.where(even, far, near), jnp.where(even, near, far)))
    for plane in range(planes):
        cot_ref[plane, EDGE : EDGE + wires] = own_ref[plane]
        for part in range(parts):
            here = slice(part * total, (part + 1) * total)
            before, after = [edge[plane * half : (plane + 1) * half] for edge in edges[part]]
            cot_ref[plane, :EDGE, here] = jnp.concatenate([gap, before], axis=0).astype(BF16)
            cot_ref[plane, EDGE + wires :, here] = jnp.concatenate([after, gap], axis=0).astype(BF16)
        result = none
        for block in range(blocks):
            i = (plane * blocks + block) % wide_ref.shape[0]
            wide = lax.dot_general(
                cot_ref[plane, :, block * span : (block + 1) * span],
                table_ref[plane, block, : columns * LANES],
                (((1,), (1,)), ((), ())),
                preferred_element_type=F32,
            )
            for column in range(columns):
                wide_ref[i, column] = wide[:, column * LANES : (column + 1) * LANES]
            left, right = none, none
            for column in range(columns):
                at = EDGE + half - 2 * column
                left += wide_ref[i, column, at : at + wires]
                if 2 * column + 1 < wire_taps:
                    right += wide_ref[i, column, at - 1 : at - 1 + wires]
            both = jnp.where(lane < WINDOW, left + pltpu.roll(right, WINDOW, 1), none)
            result += pltpu.roll(both, block * step, 1) if block else both
        out_ref[plane] = result.astype(BF16)


def backward(table, cotangent, received, others, wire_taps):
    planes, _, _, _ = table.shape
    _, wires, ticks = cotangent.shape
    extent = wires + 2 * EDGE
    columns = (wire_taps + 1) // 2
    return pl.pallas_call(
        functools.partial(back_kernel, wire_taps=wire_taps),
        out_shape=jax.ShapeDtypeStruct((planes, wires, LANES), BF16),
        in_specs=[vmem()] * (3 + len(others)),
        out_specs=vmem(),
        scratch_shapes=[
            pltpu.VMEM((planes, extent, ticks), BF16),
            pltpu.VMEM((2, columns, extent, LANES), F32),
        ],
        compiler_params=params(),
        cost_estimate=cost(4e9, 2 * math.prod(table.shape)),
        name="bin_gradients",
    )(table, cotangent, received, *others)


def merge_kernel(*refs, bins, lead):
    planes, wires, _ = refs[0].shape
    outs, slab_ref = refs[-planes - 1 : -1], refs[-1]
    parts = refs[: -planes - 2]
    total = outs[0].shape[1]
    slab = lax.axis_index("drift")
    for k, part in enumerate(parts):
        slab_ref[slab ^ k] = part[...]
    lane = lax.broadcasted_iota(jnp.int32, (wires, LANES), 1)
    none = jnp.zeros((wires, LANES), F32)
    for p in range(planes):
        tiles = [none] * (total // LANES)
        for source in range(len(parts)):
            values = slab_ref[source, p].astype(F32)
            tile, shift = (source * bins - lead) // LANES, (source * bins - lead) % LANES
            if shift:
                values = pltpu.roll(values, shift, 1)
            for t, inside in ((tile, lane >= shift), (tile + 1, lane < shift)):
                if 0 <= t < len(tiles):
                    tiles[t] += jnp.where(inside, values, none)
        for t, values in enumerate(tiles):
            outs[p][:, t * LANES : (t + 1) * LANES] = values.astype(BF16)


def merge(parts, bins, total, before):
    planes, wires, _ = parts[0].shape
    return pl.pallas_call(
        functools.partial(merge_kernel, bins=bins, lead=WINDOW // 2 - HB),
        out_shape=(jax.ShapeDtypeStruct((wires, total), BF16),) * planes,
        in_specs=[vmem()] * len(parts) + [anywhere()],
        out_specs=(vmem(),) * planes,
        scratch_shapes=[pltpu.VMEM((len(parts), planes, wires, LANES), BF16)],
        compiler_params=params(),
        cost_estimate=cost(1e8, 4 * planes * wires * total),
        name="merge_bins",
    )(*parts, before)


def charge_kernel(block_ref, count_ref, *refs):
    sources, (local_ref, share_ref, _, out_hbm) = refs[:-8], refs[-8:-4]
    all_ref, chosen_ref, out_ref, sems = refs[-4:]
    cells, planes, entries, wire_block, width = share_ref.shape
    owners, _, wires, total = all_ref.shape
    per_owner = wires // wire_block
    z = lax.axis_index("gz")
    for i, source in enumerate(sources):
        if len(sources) == planes - 1:
            all_ref[:, i] = source[...]
        else:
            all_ref[z ^ (i // (planes - 1)), i % (planes - 1)] = source[...]
    empty = jnp.zeros((wire_block, total), BF16)
    stores = []
    for b in range(cells):
        for p in range(planes):
            for k in range(entries):
                name = block_ref[p, k, b]
                if p < planes - 1:
                    name = jnp.clip(name, 0, owners * per_owner - 1)
                    owner = name // per_owner
                    start = pl.multiple_of((name - owner * per_owner) * wire_block, wire_block)
                    rows = all_ref[owner, p, pl.ds(start, wire_block), :]
                else:
                    name = jnp.clip(name - z * per_owner, 0, per_owner - 1)
                    start = pl.multiple_of(name * wire_block, wire_block)
                    rows = local_ref[pl.ds(start, wire_block), :]
                at = (p * entries + k) * wire_block
                chosen_ref[b, at : at + wire_block] = jnp.where(k < count_ref[b, p], rows, empty)
        here = slice(b * width, (b + 1) * width)
        out_ref[here] = lax.dot_general(
            share_ref[b].reshape(planes * entries * wire_block, width),
            chosen_ref[b],
            (((0,), (0,)), ((), ())),
            preferred_element_type=F32,
        ).astype(BF16)
        store = pltpu.make_async_copy(out_ref.at[here], out_hbm.at[here], sems.at[b])
        store.start()
        stores.append(store)
    for store in stores:
        store.wait()


def charge_gradient(ovl_block, ovl_count, sources, local, intersection, owners, before):
    cells, planes, entries, wire_block, width = intersection.shape
    wires, total = local.shape
    shape = (owners, planes - 1, wires, total)
    return pl.pallas_call(
        charge_kernel,
        out_shape=jax.ShapeDtypeStruct((cells * width, total), BF16),
        in_specs=[smem(), smem()] + [vmem()] * (len(sources) + 3),
        out_specs=anywhere(),
        scratch_shapes=[
            pltpu.VMEM(shape, BF16),
            pltpu.VMEM((cells, planes * entries * wire_block, total), BF16),
            pltpu.VMEM((cells * width, total), BF16),
            pltpu.SemaphoreType.DMA((cells,)),
        ],
        compiler_params=params(),
        cost_estimate=cost(1e8, 2 * math.prod(shape)),
        name="charge_gradient",
    )(jnp.transpose(ovl_block, (1, 2, 0)), ovl_count, *sources, local, intersection, before)


def pieces_kernel(
    block_hbm, count_hbm, charge_hbm, share_hbm, cot_hbm, own_hbm, keep_hbm, give_hbm, local_hbm,
    block_ref, count_ref, charge_ref, share_ref, edge_ref, cross_ref, own_ref, keep_ref, give_ref, local_ref,
    sems, out_sems, *, half,
):
    cells, planes, entries, wire_block, width = share_ref.shape
    wires, total = local_ref.shape
    ticks = edge_ref.shape[3]
    per_owner = wires // wire_block
    cut = own_ref.shape[0]
    halves = 1 + keep_ref.shape[0]
    owners = 2 * halves
    z = lax.axis_index("gz")
    loads = [
        pltpu.make_async_copy(source, target, sems.at[i])
        for i, (source, target) in enumerate(
            (
                (block_hbm, block_ref),
                (count_hbm, count_ref),
                (charge_hbm, charge_ref),
                (share_hbm, share_ref),
                (cot_hbm.at[:, :EDGE], edge_ref.at[0]),
                (cot_hbm.at[:, wires - EDGE :], edge_ref.at[1]),
            )
        )
    ]
    for load in loads:
        load.start()
    cross_ref[...] = jnp.zeros(cross_ref.shape, F32)
    local_ref[...] = jnp.zeros(local_ref.shape, F32)
    for load in loads[:4]:
        load.wait()
    for b in range(cells):
        pieces = (
            jnp.dot(
                share_ref[b].reshape(planes * entries * wire_block, width),
                charge_ref[b * width : (b + 1) * width],
                preferred_element_type=F32,
            )
            .astype(BF16)
            .astype(F32)
        )
        for p in range(planes):
            for k in range(entries):
                at = (p * entries + k) * wire_block
                piece = pieces[at : at + wire_block]
                piece = jnp.where(k < count_ref[b, p], piece, jnp.zeros_like(piece))
                name = block_ref[p, k, b]
                if p < planes - 1:
                    name = jnp.clip(name, 0, owners * per_owner - 1)
                    start = pl.multiple_of(EDGE + name * wire_block, EDGE)
                    cross_ref[p, pl.ds(start, wire_block)] += piece
                else:
                    name = jnp.clip(name - z * per_owner, 0, per_owner - 1)
                    start = pl.multiple_of(name * wire_block, wire_block)
                    local_ref[pl.ds(start, wire_block)] += piece
    for load in loads[4:]:
        load.wait()
    at = halves * cut
    gap = jnp.zeros((packed_rows(planes, half) - planes * half, ticks), F32)
    for side, first in ((0, 0), (1, EDGE - half)):
        rows = [edge_ref[side, p].astype(F32)[first : first + half] for p in range(planes)]
        rows = jnp.concatenate(rows + [gap], axis=0).astype(BF16)
        for part in range(ticks // total):
            give_ref[at : at + rows.shape[0]] = rows[:, part * total : (part + 1) * total]
            at += rows.shape[0]
    extent = wires + 2 * EDGE
    none = jnp.zeros((EDGE, total), F32)
    stores = [
        pltpu.make_async_copy(source, target, out_sems.at[i])
        for i, (source, target) in enumerate(
            (
                (give_ref, give_hbm),
                (keep_ref, keep_hbm),
                (own_ref, own_hbm),
                (local_ref, local_hbm),
            )
        )
    ]
    stores[3].start()
    for k in [*range(1, owners, 2), *range(2, owners, 2), 0]:
        to = z ^ k
        blocks = [
            cross_ref[p, pl.ds(pl.multiple_of(to * wires, EDGE), extent)] for p in range(planes - 1)
        ]
        blocks.append(jnp.where(to == z + 1, local_ref[wires - EDGE :], none))
        blocks.append(jnp.where(to == z - 1, local_ref[:EDGE], none))
        at = 0
        for rows in blocks:
            here = slice(at, at + rows.shape[0])
            at += rows.shape[0]
            if k % 2:
                give_ref[k // 2 * cut + here.start : k // 2 * cut + here.stop] = coded(rows, 0)
            elif k:
                keep_ref[k // 2 - 1, here] = coded(rows, 0)
            else:
                own_ref[here] = rows
        if k == owners - 1:
            stores[0].start()
        if k == owners - 2 and k:
            stores[1].start()
    if owners == 2:
        stores[1].start()
    stores[2].start()
    for store in stores:
        store.wait()


def packed_rows(planes, half):
    return -(-planes * half // 16) * 16


def cut_pieces(ovl_block, ovl_count, charge, intersection, cotangent, owners, half):
    cells, planes, entries, wire_block, width = intersection.shape
    total = charge.shape[1]
    _, wires, ticks = cotangent.shape
    rows = (planes - 1) * (wires + 2 * EDGE) + 2 * EDGE
    edges = 2 * packed_rows(planes, half) * ticks // total
    hbm = pl.BlockSpec(memory_space=pltpu.HBM)
    blocks = jnp.transpose(ovl_block, (1, 2, 0))
    outs = (
        jax.ShapeDtypeStruct((rows, total), F32),
        jax.ShapeDtypeStruct((owners // 2 - 1, rows, total), BF16),
        jax.ShapeDtypeStruct((owners // 2 * rows + edges, total), BF16),
        jax.ShapeDtypeStruct((wires, total), F32),
    )
    return pl.pallas_call(
        functools.partial(pieces_kernel, half=half),
        out_shape=outs,
        in_specs=[hbm] * 5,
        out_specs=(hbm,) * 4,
        scratch_shapes=[
            pltpu.SMEM(blocks.shape, jnp.int32),
            pltpu.SMEM(ovl_count.shape, jnp.int32),
            pltpu.VMEM(charge.shape, BF16),
            pltpu.VMEM(intersection.shape, BF16),
            pltpu.VMEM((2, planes, EDGE, ticks), BF16),
            pltpu.VMEM((planes - 1, owners * wires + 2 * EDGE, total), F32),
            *[pltpu.VMEM(out.shape, out.dtype) for out in outs],
            pltpu.SemaphoreType.DMA((6,)),
            pltpu.SemaphoreType.DMA((4,)),
        ],
        compiler_params=params(limit=WHOLE_VMEM),
        cost_estimate=cost(1e8, 4 * owners * rows * total),
        name="pieces",
    )(blocks, ovl_count, charge, intersection, cotangent)


def relay_kernel(keep_ref, received_ref, *outs):
    others, rows, _ = keep_ref.shape
    edges = (received_ref.shape[0] - (others + 1) * rows) // 2
    z = lax.axis_index("gz")
    even = lax.rem(z, 2) == 0
    low = received_ref[(others + 1) * rows : (others + 1) * rows + edges]
    high = received_ref[(others + 1) * rows + edges :]
    for j in range(others):
        to = z ^ (2 * (j + 1))
        summed = plain(keep_ref[j], True)
        summed += plain(received_ref[(j + 1) * rows : (j + 2) * rows], True)
        outs[j][...] = coded(summed, 0)
        upward, downward = even & (to == z + 2), jnp.logical_not(even) & (to == z - 2)
        outs[others + j][...] = jnp.where(
            upward, high, jnp.where(downward, low, jnp.zeros_like(low))
        )


def relay(keep, received):
    others, rows, total = keep.shape
    edges = (received.shape[0] - (others + 1) * rows) // 2
    outs = pl.pallas_call(
        relay_kernel,
        out_shape=(jax.ShapeDtypeStruct((rows, total), BF16),) * others
        + (jax.ShapeDtypeStruct((edges, total), BF16),) * others,
        in_specs=[vmem(), vmem()],
        out_specs=(vmem(),) * (2 * others),
        compiler_params=params(),
        cost_estimate=cost(1e7, 6 * others * rows * total),
        name="relay",
    )(keep, received)
    return outs[:others], outs[others:]


def slabs_kernel(*refs, bins, lead, slabs):
    count = len(refs) - slabs.bit_length() - 1
    keep_ref, received_ref, others, local_ref = refs[0], refs[1], refs[2 : count - 2], refs[count - 2]
    outs, cut_ref = refs[count:-1], refs[-1]
    total = local_ref.shape[1]
    cut = keep_ref.shape[0]
    summed = keep_ref[...] + plain(received_ref[:cut], True)
    for other in others:
        summed += plain(other[...], True)
    edge = cut - 2 * EDGE
    rows = jnp.concatenate(
        [summed[:edge], summed[edge : edge + EDGE], local_ref[...], summed[edge + EDGE :]], axis=0
    )
    none = jnp.zeros((rows.shape[0], LANES), F32)
    lane = lax.broadcasted_iota(jnp.int32, none.shape, 1)
    level = jnp.broadcast_to(rows[:, :1].astype(BF16).astype(F32), none.shape)
    tiles = [rows[:, t * LANES : (t + 1) * LANES] - level for t in range(total // LANES)]
    for to in range(slabs):
        at = to * bins - lead
        tile, shift = at // LANES, at % LANES
        pair = [tiles[t] if 0 <= t < len(tiles) else -level for t in (tile, tile + 1)]
        value = shared_lanes(pair[0], pair[1], shift, lane)
        cut_ref[to] = jnp.where(lane == 0, level, value).astype(BF16)
    slab = lax.axis_index("drift")
    outs[0][...] = cut_ref[slab]
    size = rows.shape[0]
    for s, out in enumerate(outs[1:]):
        for i in range(slabs >> (s + 1)):
            out[i * size : (i + 1) * size] = cut_ref[slab ^ ((2 * i + 1) << s)]


def cut_slabs(keep, received, others, local, bins, slabs, before):
    wires, total = local.shape
    rows = keep.shape[0] + wires
    steps = slabs.bit_length() - 1
    counts = [1] + [slabs >> (s + 1) for s in range(steps)]
    return pl.pallas_call(
        functools.partial(slabs_kernel, bins=bins, lead=WINDOW // 2 - HB, slabs=slabs),
        out_shape=tuple(jax.ShapeDtypeStruct((n * rows, LANES), BF16) for n in counts),
        in_specs=[vmem()] * (3 + len(others)) + [anywhere()],
        out_specs=(vmem(),) * len(counts),
        scratch_shapes=[pltpu.VMEM((slabs, rows, LANES), BF16)],
        compiler_params=params(),
        cost_estimate=cost(1e8, 4 * rows * total),
        name="slab_currents",
    )(keep, received, *others, local, before)


def pass_kernel(*refs, step, size):
    own_ref, arrived, out_ref = refs[0], refs[1:-1], refs[-1]
    for i in range(own_ref.shape[0] // size):
        here = slice(i * size, (i + 1) * size)
        total = plain(own_ref[here], False)
        for r, other in enumerate(arrived):
            at = ((2 * i + 1) << step) >> (r + 1)
            total += plain(other[at * size : (at + 1) * size], False)
        out_ref[here] = coded(total, WINDOW // 2)


def pass_on(own, arrived, step, size):
    return pl.pallas_call(
        functools.partial(pass_kernel, step=step, size=size),
        out_shape=jax.ShapeDtypeStruct(own.shape, BF16),
        in_specs=[vmem()] * (1 + len(arrived)),
        out_specs=vmem(),
        compiler_params=params(),
        cost_estimate=cost(1e6, 4 * math.prod(own.shape)),
        name="pass_on",
    )(own, *arrived)


def signal_kernel(*refs, wire_taps):
    parts, (table_ref, out_hbm, token_ref) = refs[:-9], refs[-9:-6]
    even_ref, odd_ref, level_ref, lines_ref, out_ref, sems = refs[-6:]
    planes, blocks, _, span = table_ref.shape
    _, wires, _ = out_ref.shape
    extent = wires + 2 * EDGE
    half = (wire_taps - 1) // 2
    step = span * 16 // LANES
    middle = WINDOW // 2
    token_ref[...] = jnp.zeros(token_ref.shape, F32)
    lane = lax.broadcasted_iota(jnp.int32, (wires, LANES), 1)
    stores = []
    for p in range(planes):
        here = slice(p * extent, (p + 1) * extent)
        currents = plain(parts[0][here], False)
        for part in parts[1:]:
            currents += plain(part[here], False)
        level = currents[:, middle : middle + 1].astype(BF16).astype(F32)
        level = jnp.broadcast_to(level, currents.shape)
        level_ref[p] = level
        currents = currents - level
        levels = jnp.zeros((wires, LANES), F32)
        for a in range(wire_taps):
            at = EDGE - half + a
            both = (lane == WINDOW + a) | (lane == WINDOW + wire_taps + a)
            levels = jnp.where(both, level_ref[p, at : at + wires], levels)
        for block in range(blocks):
            i = p * blocks + block
            even_ref[i] = pltpu.roll(currents, (-step * block) % LANES, 1)
            odd_ref[i] = pltpu.roll(currents, (WINDOW - step * block) % LANES, 1)
            for pair in range((wire_taps + 1) // 2):
                at = EDGE - half + 2 * pair
                right = levels
                if 2 * pair + 1 < wire_taps:
                    right = odd_ref[i, at + 1 : at + 1 + wires]
                line = jnp.where(lane < WINDOW, even_ref[i, at : at + wires], right)
                lines_ref[i % 2, :, pair * LANES : (pair + 1) * LANES] = line.astype(BF16)
            out_ref[p, :, block * span : (block + 1) * span] = jnp.dot(
                lines_ref[i % 2], table_ref[p, block], preferred_element_type=F32
            ).astype(BF16)
        store = pltpu.make_async_copy(out_ref.at[p], out_hbm.at[p], sems.at[p])
        store.start()
        stores.append(store)
    for store in stores:
        store.wait()


def forward(parts, table, wires, wire_taps):
    planes, blocks, depth, span = table.shape
    extent = wires + 2 * EDGE
    shape = (planes, wires, blocks * span)
    return pl.pallas_call(
        functools.partial(signal_kernel, wire_taps=wire_taps),
        out_shape=(
            jax.ShapeDtypeStruct(shape, BF16),
            jax.ShapeDtypeStruct((8, LANES), F32),
        ),
        in_specs=[vmem()] * (len(parts) + 1),
        out_specs=(anywhere(), vmem()),
        scratch_shapes=[
            pltpu.VMEM((planes * blocks, extent, LANES), F32),
            pltpu.VMEM((planes * blocks, extent, LANES), F32),
            pltpu.VMEM((planes, extent, LANES), F32),
            pltpu.VMEM((2, wires, depth), BF16),
            pltpu.VMEM(shape, BF16),
            pltpu.SemaphoreType.DMA((planes,)),
        ],
        compiler_params=params(),
        cost_estimate=cost(4e9, 2 * math.prod(table.shape)),
        name="signal",
    )(*parts, table)


def local(charge, intersection, ovl_block, ovl_count, diff_class, response, cotangent):
    total = charge.shape[1]
    owners = lax.axis_size("gz")
    slabs = lax.axis_size("drift")
    planes, wires, ticks = cotangent.shape
    wire_taps = response.shape[1]
    bins = total // slabs

    currents, keep, give, local_currents = cut_pieces(
        ovl_block, ovl_count, charge, intersection, cotangent, owners, (wire_taps - 1) // 2
    )
    received = swap(give, "gz", 1)
    sums, edges = relay(keep.astype(F32), received) if owners > 2 else ((), ())
    beyond = [swap(block, "gz", 2 * j) for j, block in enumerate(edges, 1)]
    others = [swap(block, "gz", 2 * j) for j, block in enumerate(sums, 1)]

    levels, kinds = smeared_levels(
        diff_class, response, bins, slabs, sums[0] if sums else received
    )
    table = build_table(levels, kinds, planes, wire_taps, ticks)
    partial = backward(table, cotangent, received, beyond, wire_taps)
    spread = [partial] + [swap(partial, "drift", k) for k in range(1, slabs)]

    cuts = cut_slabs(currents, received, others, local_currents, bins, slabs, partial)
    windows, ready = [cuts[0]], cuts[0]
    for step, block in enumerate(cuts[1:]):
        if step:
            block = ready = pass_on(block, windows[1:], step, cuts[0].shape[0])
        windows.append(swap(block, "drift", 1 << step))

    *cross, own = merge(spread, bins, total, ready)
    if owners == 4:
        across = [swap(block, "gz", 2) for block in cross]
        sources = [*cross, *(swap(block, "gz", 1) for block in cross)]
        sources += [*across, *(swap(block, "gz", 1) for block in across)]
    else:
        sources = [lax.all_gather(block, "gz", axis=0) for block in cross]
    signal, done = forward(windows, table, wires, wire_taps)
    charge_grad = charge_gradient(
        ovl_block, ovl_count, sources, own, intersection, owners, done
    )
    return signal, charge_grad


def solution(mesh):
    return jax.shard_map(
        local,
        mesh=mesh,
        in_specs=(
            P(("apa", "gz", "drift"), None),
            P(("apa", "gz", "drift"), None, None, None, None),
            P(("apa", "gz", "drift"), None, None),
            P(("apa", "gz", "drift"), None),
            P("apa"),
            P(),
            P("apa", "gz", "drift"),
        ),
        out_specs=(P("apa", "gz", "drift"), P(("apa", "gz", "drift"), None)),
        check_vma=False,
    )
```

```python
import functools
import math

import jax
import jax.numpy as jnp
from jax import lax
from jax.experimental import pallas as pl
from jax.experimental.pallas import tpu as pltpu
from jax.sharding import PartitionSpec as P

TPB = 8
HB = 2
CLASSES = 6
LANES = 128
EDGE = 16
GROUP = 8
WINDOW = 64
LEAD = HB * TPB - TPB // 2
VMEM_LIMIT = 24 * 1024 * 1024
WHOLE_VMEM = 61 * 1024 * 1024
BF16 = jnp.bfloat16
F32 = jnp.float32


def params(semantics=None, limit=VMEM_LIMIT):
    return pltpu.CompilerParams(vmem_limit_bytes=limit, dimension_semantics=semantics)


def vmem():
    return pl.BlockSpec(memory_space=pltpu.VMEM)


def smem():
    return pl.BlockSpec(memory_space=pltpu.SMEM)


def anywhere():
    return pl.BlockSpec(memory_space=pl.ANY)


def cost(flops, moved):
    return pl.CostEstimate(flops=int(flops), bytes_accessed=int(moved), transcendentals=0)


def swap(block, axis, distance):
    count = lax.axis_size(axis)
    return lax.ppermute(block, axis, [(i, i ^ distance) for i in range(count)])


def widths(number):
    spread = TPB * (0.2 + 0.15 * number)
    half = HB * TPB
    total = sum(math.exp(-((j + 0.5) ** 2) / (2.0 * spread * spread)) for j in range(-half, half))
    return 1.0 / (2.0 * spread * spread), 1.0 / total


def shared_lanes(left, right, shift, lane):
    if shift == 0:
        return left
    back = LANES - shift
    return jnp.where(lane < back, pltpu.roll(left, back, 1), pltpu.roll(right, back, 1))


def coded(rows, column):
    lane = lax.broadcasted_iota(jnp.int32, rows.shape, 1)
    level = jnp.broadcast_to(rows[:, column : column + 1].astype(BF16).astype(F32), rows.shape)
    return jnp.where(lane == 0, level, rows - level).astype(BF16)


def plain(rows, first):
    rows = rows.astype(F32)
    lane = lax.broadcasted_iota(jnp.int32, rows.shape, 1)
    level = jnp.broadcast_to(rows[:, :1], rows.shape)
    return jnp.where(lane == 0, level if first else jnp.zeros_like(rows), rows + level)


def levels_kernel(
    class_ref, response_ref, _, level_ref, kind_ref, flat_ref, *, bins, slabs, total
):
    planes, wire_taps, length = response_ref.shape
    rows = level_ref.shape[0] // planes
    groups = kind_ref.shape[0]
    slab = lax.axis_index("drift")
    lane = lax.broadcasted_iota(jnp.int32, (GROUP, LANES), 1)
    packed = class_ref[...].astype(F32)
    tiles = []
    for t in range(total // LANES):
        at = slice(t % 2 * LANES, (t % 2 + 1) * LANES)
        tiles.append(jnp.broadcast_to(packed[t // 2 : t // 2 + 1, at], (GROUP, LANES)))
    classes = tiles[0]
    none = jnp.zeros((GROUP, LANES), F32)
    numbers = none
    for source in range(slabs):
        at = source * bins - (WINDOW // 2 - HB)
        tile, shift = at // LANES, at % LANES
        pair = [tiles[t] if 0 <= t < len(tiles) else none for t in (tile, tile + 1)]
        numbers = jnp.where(slab == source, shared_lanes(pair[0], pair[1], shift, lane), numbers)
    x = slab * bins - (WINDOW // 2 - HB) + lane
    numbers = jnp.where((x >= 0) & (x < HB), (CLASSES + x).astype(F32), numbers)
    column = jnp.broadcast_to(numbers[:1], (LANES, LANES)).T.astype(jnp.int32)
    for m in range(groups):
        kind_ref[m] = column[m * GROUP : (m + 1) * GROUP]
    flat_ref[...] = jnp.zeros(flat_ref.shape, F32)
    for p in range(planes):
        flat_ref[p * rows : p * rows + wire_taps, :length] = response_ref[p].astype(F32)
    taps = flat_ref[...].astype(BF16)
    tap = lax.broadcasted_iota(jnp.int32, (LANES, 2 * LANES), 0)
    tick = lax.broadcasted_iota(jnp.int32, (LANES, 2 * LANES), 1)
    step = tick - tap - LEAD
    offset = step.astype(F32) - (TPB - 1) / 2.0
    squared = offset * offset
    inside = jnp.abs(offset) < HB * TPB
    for kind in range(CLASSES + HB):
        keep = inside
        if kind < CLASSES:
            narrow, scale = widths(kind)
        else:
            edge = kind - CLASSES
            narrow, scale = widths(0)
            for number in range(1, CLASSES):
                chosen = classes[:1, edge : edge + 1] == number
                narrow = jnp.where(chosen, widths(number)[0], narrow)
                scale = jnp.where(chosen, widths(number)[1], scale)
            keep = inside & (step >= -TPB * edge)
        smear = jnp.where(keep, jnp.exp(-(squared * narrow)) * scale, 0.0)
        high = smear.astype(BF16)
        low = (smear - high.astype(F32)).astype(BF16)
        near = jnp.dot(taps[:, :LANES], high, preferred_element_type=F32) + jnp.dot(
            taps[:, :LANES], low, preferred_element_type=F32
        )
        far = jnp.dot(taps[:, LANES:], high[:, :LANES], preferred_element_type=F32) + jnp.dot(
            taps[:, LANES:], low[:, :LANES], preferred_element_type=F32
        )
        level_ref[:, kind, :LANES] = near[:, :LANES]
        level_ref[:, kind, LANES:] = near[:, LANES:] + far


def smeared_levels(diff_class, response, bins, slabs, before):
    planes, wire_taps, _ = response.shape
    total = diff_class.shape[0]
    reach = 2 * LANES
    rows = -(-wire_taps // 8) * 8
    groups = (bins + WINDOW // 2) // GROUP
    classes = jnp.pad(diff_class.astype(BF16), (0, 8 * reach - total)).reshape(8, reach)
    return pl.pallas_call(
        functools.partial(levels_kernel, bins=bins, slabs=slabs, total=total),
        out_shape=(
            jax.ShapeDtypeStruct((planes * rows, CLASSES + HB, reach), F32),
            jax.ShapeDtypeStruct((groups, GROUP, LANES), jnp.int32),
        ),
        in_specs=[vmem(), vmem(), anywhere()],
        out_specs=(vmem(), vmem()),
        scratch_shapes=[pltpu.VMEM((planes * rows, reach), F32)],
        compiler_params=params(),
        cost_estimate=cost(1e8, 1e6),
        name="levels",
    )(classes, response, before)


def table_kernel(level_ref, kind_ref, table_ref, sum_ref, *, wire_taps):
    planes, blocks, depth, span = table_ref.shape
    rows = level_ref.shape[0] // planes
    groups = kind_ref.shape[0]
    tiles = span // LANES
    lane = lax.broadcasted_iota(jnp.int32, (GROUP, LANES), 1)
    row = lax.broadcasted_iota(jnp.int32, (GROUP, LANES), 0)
    starts = [LEAD_SHIFT + odd * (LANES // 2) + TPB * row for odd in range(2)]
    after = [lane >= start for start in starts]
    zero = jnp.zeros((GROUP, LANES), F32)
    empty = jnp.zeros((2 * GROUP, LANES), BF16)

    def body(a, plane):
        levels = level_ref[plane * rows + a]
        halves = [levels[:, :LANES], levels[:, LANES:]]
        pieces = []
        for m in range(groups):
            odd = m % 2
            parts = [
                pltpu.roll(
                    jnp.take_along_axis(half, kind_ref[m], axis=0),
                    LEAD_SHIFT + odd * (LANES // 2),
                    1,
                    stride=TPB,
                    stride_axis=0,
                )
                for half in halves
            ]
            pieces.append(
                (
                    jnp.where(after[odd], parts[0], zero),
                    jnp.where(after[odd], parts[1], parts[0]),
                    jnp.where(after[odd], zero, parts[1]),
                )
            )
        for block in range(blocks):
            for tile in range(tiles):
                here = slice(tile * LANES, (tile + 1) * LANES)
                total = zero
                for quarter in range(WINDOW // (2 * GROUP)):
                    m = 2 * (tiles * block + quarter)
                    at = a * WINDOW + quarter * 2 * GROUP
                    at = pl.ds(pl.multiple_of(at, 2 * GROUP), 2 * GROUP)
                    third = tile - quarter + 2
                    value = empty
                    if 0 <= third <= 2 and m + 1 < groups:
                        value = jnp.concatenate(
                            [pieces[m][third], pieces[m + 1][third]], axis=0
                        ).astype(BF16)
                        total = total + pieces[m][third] + pieces[m + 1][third]
                    table_ref[plane, block, at, here] = value
                sum_ref[a, block, :, here] = total
        return plane

    def whole_plane(plane, _):
        lax.fori_loop(0, wire_taps, body, plane, unroll=UNROLL)
        for block in range(blocks):
            total = jnp.sum(sum_ref[:, block], axis=1)
            high = total.astype(BF16).astype(F32)
            spare = jnp.zeros((depth - (WINDOW + 2) * wire_taps, span), F32)
            table_ref[plane, block, wire_taps * WINDOW :, :] = jnp.concatenate(
                [high, total - high, spare], axis=0
            ).astype(BF16)
        return 0

    lax.fori_loop(0, planes, whole_plane, 0)


UNROLL = 7
LEAD_SHIFT = (TPB * HB - LEAD) % LANES


def build_table(levels, kinds, planes, wire_taps, ticks_here):
    tiles = math.gcd(ticks_here, 2 * LANES) // LANES
    blocks = ticks_here // (tiles * LANES)
    shape = (planes, blocks, (wire_taps + 1) * WINDOW, tiles * LANES)
    return pl.pallas_call(
        functools.partial(table_kernel, wire_taps=wire_taps),
        out_shape=jax.ShapeDtypeStruct(shape, BF16),
        in_specs=[vmem(), vmem()],
        out_specs=vmem(),
        scratch_shapes=[pltpu.VMEM((wire_taps, blocks, GROUP, tiles * LANES), F32)],
        compiler_params=params(),
        cost_estimate=cost(4e9, 2 * math.prod(shape)),
        name="table",
    )(levels, kinds)


def back_kernel(table_ref, own_ref, received_ref, *refs, wire_taps):
    others, (out_ref, cot_ref, wide_ref) = refs[:-3], refs[-3:]
    planes, blocks, _, span = table_ref.shape
    _, wires, ticks = own_ref.shape
    total = received_ref.shape[1]
    half = (wire_taps - 1) // 2
    parts = ticks // total
    size = sixteens(planes * half)
    side = parts * size
    lows = received_ref.shape[0] - 2 * side
    even = lax.rem(lax.axis_index("gz"), 2) == 0
    lane = lax.broadcasted_iota(jnp.int32, (wires, LANES), 1)
    none = jnp.zeros((wires, LANES), F32)
    gap = jnp.zeros((EDGE - half, total), F32)
    step = span * 16 // LANES
    columns = (wire_taps + 1) // 2
    edges = []
    for part in range(parts):
        low = received_ref[lows + part * size : lows + (part + 1) * size].astype(F32)
        high = received_ref[lows + side + part * size : lows + side + (part + 1) * size].astype(F32)
        near = jnp.where(even, low, high)
        far = jnp.zeros((size, total), F32)
        for other in others:
            far += other[part * size : (part + 1) * size].astype(F32)
        edges.append((jnp.where(even, far, near), jnp.where(even, near, far)))
    for plane in range(planes):
        cot_ref[plane, EDGE : EDGE + wires] = own_ref[plane]
        for part in range(parts):
            here = slice(part * total, (part + 1) * total)
            before, after = [edge[plane * half : (plane + 1) * half] for edge in edges[part]]
            cot_ref[plane, :EDGE, here] = jnp.concatenate([gap, before], axis=0).astype(BF16)
            cot_ref[plane, EDGE + wires :, here] = jnp.concatenate([after, gap], axis=0).astype(BF16)
        result = none
        for block in range(blocks):
            i = (plane * blocks + block) % wide_ref.shape[0]
            wide = lax.dot_general(
                cot_ref[plane, :, block * span : (block + 1) * span],
                table_ref[plane, block, : columns * LANES],
                (((1,), (1,)), ((), ())),
                preferred_element_type=F32,
            )
            for column in range(columns):
                wide_ref[i, column] = wide[:, column * LANES : (column + 1) * LANES]
            left, right = none, none
            for column in range(columns):
                at = EDGE + half - 2 * column
                left += wide_ref[i, column, at : at + wires]
                if 2 * column + 1 < wire_taps:
                    right += wide_ref[i, column, at - 1 : at - 1 + wires]
            both = jnp.where(lane < WINDOW, left + pltpu.roll(right, WINDOW, 1), none)
            result += pltpu.roll(both, block * step, 1) if block else both
        out_ref[plane] = result.astype(BF16)


def backward(table, cotangent, received, others, wire_taps):
    planes, _, _, _ = table.shape
    _, wires, ticks = cotangent.shape
    extent = wires + 2 * EDGE
    columns = (wire_taps + 1) // 2
    return pl.pallas_call(
        functools.partial(back_kernel, wire_taps=wire_taps),
        out_shape=jax.ShapeDtypeStruct((planes, wires, LANES), BF16),
        in_specs=[vmem()] * (3 + len(others)),
        out_specs=vmem(),
        scratch_shapes=[
            pltpu.VMEM((planes, extent, ticks), BF16),
            pltpu.VMEM((2, columns, extent, LANES), F32),
        ],
        compiler_params=params(),
        cost_estimate=cost(4e9, 2 * math.prod(table.shape)),
        name="bin_gradients",
    )(table, cotangent, received, *others)


def merge_kernel(*refs, bins, lead):
    planes, wires, _ = refs[0].shape
    outs, slab_ref = refs[-planes - 1 : -1], refs[-1]
    parts = refs[: -planes - 2]
    total = outs[0].shape[1]
    slab = lax.axis_index("drift")
    for k, part in enumerate(parts):
        slab_ref[slab ^ k] = part[...]
    lane = lax.broadcasted_iota(jnp.int32, (wires, LANES), 1)
    none = jnp.zeros((wires, LANES), F32)
    for p in range(planes):
        tiles = [none] * (total // LANES)
        for source in range(len(parts)):
            values = slab_ref[source, p].astype(F32)
            tile, shift = (source * bins - lead) // LANES, (source * bins - lead) % LANES
            if shift:
                values = pltpu.roll(values, shift, 1)
            for t, inside in ((tile, lane >= shift), (tile + 1, lane < shift)):
                if 0 <= t < len(tiles):
                    tiles[t] += jnp.where(inside, values, none)
        for t, values in enumerate(tiles):
            outs[p][:, t * LANES : (t + 1) * LANES] = values.astype(BF16)


def merge(parts, bins, total, before):
    planes, wires, _ = parts[0].shape
    return pl.pallas_call(
        functools.partial(merge_kernel, bins=bins, lead=WINDOW // 2 - HB),
        out_shape=(jax.ShapeDtypeStruct((wires, total), BF16),) * planes,
        in_specs=[vmem()] * len(parts) + [anywhere()],
        out_specs=(vmem(),) * planes,
        scratch_shapes=[pltpu.VMEM((len(parts), planes, wires, LANES), BF16)],
        compiler_params=params(),
        cost_estimate=cost(1e8, 4 * planes * wires * total),
        name="merge_bins",
    )(*parts, before)


def charge_kernel(block_ref, count_ref, *refs):
    sources, (local_ref, share_ref, _, out_hbm) = refs[:-8], refs[-8:-4]
    all_ref, chosen_ref, out_ref, sems = refs[-4:]
    cells, planes, entries, wire_block, width = share_ref.shape
    owners, _, wires, total = all_ref.shape
    per_owner = wires // wire_block
    z = lax.axis_index("gz")
    for i, source in enumerate(sources):
        if len(sources) == planes - 1:
            all_ref[:, i] = source[...]
        else:
            all_ref[z ^ (i // (planes - 1)), i % (planes - 1)] = source[...]
    empty = jnp.zeros((wire_block, total), BF16)
    stores = []
    for b in range(cells):
        for p in range(planes):
            for k in range(entries):
                name = block_ref[p, k, b]
                if p < planes - 1:
                    name = jnp.clip(name, 0, owners * per_owner - 1)
                    owner = name // per_owner
                    start = pl.multiple_of((name - owner * per_owner) * wire_block, wire_block)
                    rows = all_ref[owner, p, pl.ds(start, wire_block), :]
                else:
                    name = jnp.clip(name - z * per_owner, 0, per_owner - 1)
                    start = pl.multiple_of(name * wire_block, wire_block)
                    rows = local_ref[pl.ds(start, wire_block), :]
                at = (p * entries + k) * wire_block
                chosen_ref[b, at : at + wire_block] = jnp.where(k < count_ref[b, p], rows, empty)
        here = slice(b * width, (b + 1) * width)
        out_ref[here] = lax.dot_general(
            share_ref[b].reshape(planes * entries * wire_block, width),
            chosen_ref[b],
            (((0,), (0,)), ((), ())),
            preferred_element_type=F32,
        ).astype(BF16)
        store = pltpu.make_async_copy(out_ref.at[here], out_hbm.at[here], sems.at[b])
        store.start()
        stores.append(store)
    for store in stores:
        store.wait()


def charge_gradient(ovl_block, ovl_count, sources, local, intersection, owners, before):
    cells, planes, entries, wire_block, width = intersection.shape
    wires, total = local.shape
    shape = (owners, planes - 1, wires, total)
    return pl.pallas_call(
        charge_kernel,
        out_shape=jax.ShapeDtypeStruct((cells * width, total), BF16),
        in_specs=[smem(), smem()] + [vmem()] * (len(sources) + 3),
        out_specs=anywhere(),
        scratch_shapes=[
            pltpu.VMEM(shape, BF16),
            pltpu.VMEM((cells, planes * entries * wire_block, total), BF16),
            pltpu.VMEM((cells * width, total), BF16),
            pltpu.SemaphoreType.DMA((cells,)),
        ],
        compiler_params=params(),
        cost_estimate=cost(1e8, 2 * math.prod(shape)),
        name="charge_gradient",
    )(jnp.transpose(ovl_block, (1, 2, 0)), ovl_count, *sources, local, intersection, before)


def pieces_kernel(
    block_hbm, count_hbm, charge_hbm, share_hbm, cot_hbm, own_hbm, keep_hbm, give_hbm, local_hbm,
    block_ref, count_ref, charge_ref, share_ref, edge_ref, cross_ref, own_ref, keep_ref, give_ref, local_ref,
    sems, out_sems, *, half,
):
    cells, planes, entries, wire_block, width = share_ref.shape
    wires, total = local_ref.shape
    ticks = edge_ref.shape[3]
    per_owner = wires // wire_block
    cut = own_ref.shape[0]
    halves = 1 + keep_ref.shape[0]
    owners = 2 * halves
    z = lax.axis_index("gz")
    loads = [
        pltpu.make_async_copy(source, target, sems.at[i])
        for i, (source, target) in enumerate(
            (
                (block_hbm, block_ref),
                (count_hbm, count_ref),
                (charge_hbm, charge_ref),
                (share_hbm, share_ref),
                (cot_hbm.at[:, :EDGE], edge_ref.at[0]),
                (cot_hbm.at[:, wires - EDGE :], edge_ref.at[1]),
            )
        )
    ]
    for load in loads:
        load.start()
    cross_ref[...] = jnp.zeros(cross_ref.shape, F32)
    local_ref[...] = jnp.zeros(local_ref.shape, F32)
    for load in loads[:4]:
        load.wait()
    for b in range(cells):
        pieces = (
            jnp.dot(
                share_ref[b].reshape(planes * entries * wire_block, width),
                charge_ref[b * width : (b + 1) * width],
                preferred_element_type=F32,
            )
            .astype(BF16)
            .astype(F32)
        )
        for p in range(planes):
            for k in range(entries):
                at = (p * entries + k) * wire_block
                piece = pieces[at : at + wire_block]
                piece = jnp.where(k < count_ref[b, p], piece, jnp.zeros_like(piece))
                name = block_ref[p, k, b]
                if p < planes - 1:
                    name = jnp.clip(name, 0, owners * per_owner - 1)
                    start = pl.multiple_of(EDGE + name * wire_block, EDGE)
                    cross_ref[p, pl.ds(start, wire_block)] += piece
                else:
                    name = jnp.clip(name - z * per_owner, 0, per_owner - 1)
                    start = pl.multiple_of(name * wire_block, wire_block)
                    local_ref[pl.ds(start, wire_block)] += piece
    for load in loads[4:]:
        load.wait()
    at = halves * cut
    gap = jnp.zeros((sixteens(planes * half) - planes * half, ticks), F32)
    for side, first in ((0, 0), (1, EDGE - half)):
        rows = [edge_ref[side, p].astype(F32)[first : first + half] for p in range(planes)]
        rows = jnp.concatenate(rows + [gap], axis=0).astype(BF16)
        for part in range(ticks // total):
            give_ref[at : at + rows.shape[0]] = rows[:, part * total : (part + 1) * total]
            at += rows.shape[0]
    extent = wires + 2 * EDGE
    none = jnp.zeros((half, total), F32)
    stores = [
        pltpu.make_async_copy(source, target, out_sems.at[i])
        for i, (source, target) in enumerate(
            (
                (give_ref, give_hbm),
                (keep_ref, keep_hbm),
                (own_ref, own_hbm),
                (local_ref, local_hbm),
            )
        )
    ]
    stores[3].start()
    for k in [*range(1, owners, 2), *range(2, owners, 2), 0]:
        to = z ^ k
        blocks = []
        for p in range(planes - 1):
            rows = cross_ref[p, pl.ds(pl.multiple_of(to * wires, EDGE), extent)]
            blocks.append(rows[EDGE - half : extent - EDGE + half])
        blocks.append(jnp.where(to == z + 1, local_ref[wires - half :], none))
        blocks.append(jnp.where(to == z - 1, local_ref[:half], none))
        rows = padded(blocks)
        if k % 2:
            give_ref[k // 2 * cut : (k // 2 + 1) * cut] = coded(rows, 0)
        elif k:
            keep_ref[k // 2 - 1] = coded(rows, 0)
        else:
            own_ref[...] = rows
        if k == owners - 1:
            stores[0].start()
        if k == owners - 2 and k:
            stores[1].start()
    if owners == 2:
        stores[1].start()
    stores[2].start()
    for store in stores:
        store.wait()


def sixteens(rows):
    return -(-rows // 16) * 16


def padded(blocks):
    count = sum(block.shape[0] for block in blocks)
    if count % 16:
        blocks = blocks + [jnp.zeros((sixteens(count) - count, blocks[0].shape[1]), F32)]
    return jnp.concatenate(blocks, axis=0)


def cut_pieces(ovl_block, ovl_count, charge, intersection, cotangent, owners, half):
    cells, planes, entries, wire_block, width = intersection.shape
    total = charge.shape[1]
    _, wires, ticks = cotangent.shape
    rows = sixteens((planes - 1) * (wires + 2 * half) + 2 * half)
    edges = 2 * sixteens(planes * half) * ticks // total
    hbm = pl.BlockSpec(memory_space=pltpu.HBM)
    blocks = jnp.transpose(ovl_block, (1, 2, 0))
    outs = (
        jax.ShapeDtypeStruct((rows, total), F32),
        jax.ShapeDtypeStruct((owners // 2 - 1, rows, total), BF16),
        jax.ShapeDtypeStruct((owners // 2 * rows + edges, total), BF16),
        jax.ShapeDtypeStruct((wires, total), F32),
    )
    return pl.pallas_call(
        functools.partial(pieces_kernel, half=half),
        out_shape=outs,
        in_specs=[hbm] * 5,
        out_specs=(hbm,) * 4,
        scratch_shapes=[
            pltpu.SMEM(blocks.shape, jnp.int32),
            pltpu.SMEM(ovl_count.shape, jnp.int32),
            pltpu.VMEM(charge.shape, BF16),
            pltpu.VMEM(intersection.shape, BF16),
            pltpu.VMEM((2, planes, EDGE, ticks), BF16),
            pltpu.VMEM((planes - 1, owners * wires + 2 * EDGE, total), F32),
            *[pltpu.VMEM(out.shape, out.dtype) for out in outs],
            pltpu.SemaphoreType.DMA((6,)),
            pltpu.SemaphoreType.DMA((4,)),
        ],
        compiler_params=params(limit=WHOLE_VMEM),
        cost_estimate=cost(1e8, 4 * owners * rows * total),
        name="pieces",
    )(blocks, ovl_count, charge, intersection, cotangent)


def relay_kernel(keep_ref, received_ref, *outs):
    others, rows, _ = keep_ref.shape
    edges = (received_ref.shape[0] - (others + 1) * rows) // 2
    z = lax.axis_index("gz")
    even = lax.rem(z, 2) == 0
    low = received_ref[(others + 1) * rows : (others + 1) * rows + edges]
    high = received_ref[(others + 1) * rows + edges :]
    for j in range(others):
        to = z ^ (2 * (j + 1))
        summed = plain(keep_ref[j], True)
        summed += plain(received_ref[(j + 1) * rows : (j + 2) * rows], True)
        outs[j][...] = coded(summed, 0)
        upward, downward = even & (to == z + 2), jnp.logical_not(even) & (to == z - 2)
        outs[others + j][...] = jnp.where(
            upward, high, jnp.where(downward, low, jnp.zeros_like(low))
        )


def relay(keep, received):
    others, rows, total = keep.shape
    edges = (received.shape[0] - (others + 1) * rows) // 2
    outs = pl.pallas_call(
        relay_kernel,
        out_shape=(jax.ShapeDtypeStruct((rows, total), BF16),) * others
        + (jax.ShapeDtypeStruct((edges, total), BF16),) * others,
        in_specs=[vmem(), vmem()],
        out_specs=(vmem(),) * (2 * others),
        compiler_params=params(),
        cost_estimate=cost(1e7, 6 * others * rows * total),
        name="relay",
    )(keep, received)
    return outs[:others], outs[others:]


def slabs_kernel(*refs, bins, lead, slabs, cross, half):
    count = len(refs) - slabs.bit_length() - 1
    keep_ref, received_ref, others, local_ref = refs[0], refs[1], refs[2 : count - 2], refs[count - 2]
    outs, cut_ref = refs[count:-1], refs[-1]
    total = local_ref.shape[1]
    cut = keep_ref.shape[0]
    summed = keep_ref[...] + plain(received_ref[:cut], True)
    for other in others:
        summed += plain(other[...], True)
    wires = local_ref.shape[0]
    edge = cross * (wires + 2 * half)
    rows = padded([summed[: edge + half], local_ref[...], summed[edge + half : edge + 2 * half]])
    none = jnp.zeros((rows.shape[0], LANES), F32)
    lane = lax.broadcasted_iota(jnp.int32, none.shape, 1)
    level = jnp.broadcast_to(rows[:, :1].astype(BF16).astype(F32), none.shape)
    tiles = [rows[:, t * LANES : (t + 1) * LANES] - level for t in range(total // LANES)]
    for to in range(slabs):
        at = to * bins - lead
        tile, shift = at // LANES, at % LANES
        pair = [tiles[t] if 0 <= t < len(tiles) else -level for t in (tile, tile + 1)]
        value = shared_lanes(pair[0], pair[1], shift, lane)
        cut_ref[to] = jnp.where(lane == 0, level, value).astype(BF16)
    slab = lax.axis_index("drift")
    outs[0][...] = cut_ref[slab]
    size = rows.shape[0]
    for s, out in enumerate(outs[1:]):
        for i in range(slabs >> (s + 1)):
            out[i * size : (i + 1) * size] = cut_ref[slab ^ ((2 * i + 1) << s)]


def cut_slabs(keep, received, others, local, bins, slabs, cross, half, before):
    wires, total = local.shape
    rows = sixteens((cross + 1) * (wires + 2 * half))
    steps = slabs.bit_length() - 1
    counts = [1] + [slabs >> (s + 1) for s in range(steps)]
    return pl.pallas_call(
        functools.partial(
            slabs_kernel, bins=bins, lead=WINDOW // 2 - HB, slabs=slabs, cross=cross, half=half
        ),
        out_shape=tuple(jax.ShapeDtypeStruct((n * rows, LANES), BF16) for n in counts),
        in_specs=[vmem()] * (3 + len(others)) + [anywhere()],
        out_specs=(vmem(),) * len(counts),
        scratch_shapes=[pltpu.VMEM((slabs, rows, LANES), BF16)],
        compiler_params=params(),
        cost_estimate=cost(1e8, 4 * rows * total),
        name="slab_currents",
    )(keep, received, *others, local, before)


def pass_kernel(*refs, step, size):
    own_ref, arrived, out_ref = refs[0], refs[1:-1], refs[-1]
    for i in range(own_ref.shape[0] // size):
        here = slice(i * size, (i + 1) * size)
        total = plain(own_ref[here], False)
        for r, other in enumerate(arrived):
            at = ((2 * i + 1) << step) >> (r + 1)
            total += plain(other[at * size : (at + 1) * size], False)
        out_ref[here] = coded(total, WINDOW // 2)


def pass_on(own, arrived, step, size):
    return pl.pallas_call(
        functools.partial(pass_kernel, step=step, size=size),
        out_shape=jax.ShapeDtypeStruct(own.shape, BF16),
        in_specs=[vmem()] * (1 + len(arrived)),
        out_specs=vmem(),
        compiler_params=params(),
        cost_estimate=cost(1e6, 4 * math.prod(own.shape)),
        name="pass_on",
    )(own, *arrived)


def signal_kernel(*refs, wire_taps):
    parts, (table_ref, out_hbm, token_ref) = refs[:-9], refs[-9:-6]
    even_ref, odd_ref, level_ref, lines_ref, out_ref, sems = refs[-6:]
    planes, blocks, _, span = table_ref.shape
    _, wires, _ = out_ref.shape
    half = (wire_taps - 1) // 2
    extent = wires + 2 * half
    step = span * 16 // LANES
    middle = WINDOW // 2
    token_ref[...] = jnp.zeros(token_ref.shape, F32)
    lane = lax.broadcasted_iota(jnp.int32, (wires, LANES), 1)
    stores = []
    size = parts[0].shape[0]
    summed = plain(parts[0][...], False)
    for part in parts[1:]:
        summed += plain(part[:size], False)
    for p in range(planes):
        currents = summed[p * extent : (p + 1) * extent]
        level = currents[:, middle : middle + 1].astype(BF16).astype(F32)
        level = jnp.broadcast_to(level, currents.shape)
        level_ref[p] = level
        currents = currents - level
        levels = jnp.zeros((wires, LANES), F32)
        for a in range(wire_taps):
            at = a
            both = (lane == WINDOW + a) | (lane == WINDOW + wire_taps + a)
            levels = jnp.where(both, level_ref[p, at : at + wires], levels)
        for block in range(blocks):
            i = p * blocks + block
            even_ref[i] = pltpu.roll(currents, (-step * block) % LANES, 1)
            odd_ref[i] = pltpu.roll(currents, (WINDOW - step * block) % LANES, 1)
            for pair in range((wire_taps + 1) // 2):
                at = 2 * pair
                right = levels
                if 2 * pair + 1 < wire_taps:
                    right = odd_ref[i, at + 1 : at + 1 + wires]
                line = jnp.where(lane < WINDOW, even_ref[i, at : at + wires], right)
                lines_ref[i % 2, :, pair * LANES : (pair + 1) * LANES] = line.astype(BF16)
            out_ref[p, :, block * span : (block + 1) * span] = jnp.dot(
                lines_ref[i % 2], table_ref[p, block], preferred_element_type=F32
            ).astype(BF16)
        store = pltpu.make_async_copy(out_ref.at[p], out_hbm.at[p], sems.at[p])
        store.start()
        stores.append(store)
    for store in stores:
        store.wait()


def forward(parts, table, wires, wire_taps):
    planes, blocks, depth, span = table.shape
    extent = wires + wire_taps - 1
    shape = (planes, wires, blocks * span)
    return pl.pallas_call(
        functools.partial(signal_kernel, wire_taps=wire_taps),
        out_shape=(
            jax.ShapeDtypeStruct(shape, BF16),
            jax.ShapeDtypeStruct((8, LANES), F32),
        ),
        in_specs=[vmem()] * (len(parts) + 1),
        out_specs=(anywhere(), vmem()),
        scratch_shapes=[
            pltpu.VMEM((planes * blocks, extent, LANES), F32),
            pltpu.VMEM((planes * blocks, extent, LANES), F32),
            pltpu.VMEM((planes, extent, LANES), F32),
            pltpu.VMEM((2, wires, depth), BF16),
            pltpu.VMEM(shape, BF16),
            pltpu.SemaphoreType.DMA((planes,)),
        ],
        compiler_params=params(),
        cost_estimate=cost(4e9, 2 * math.prod(table.shape)),
        name="signal",
    )(*parts, table)


def local(charge, intersection, ovl_block, ovl_count, diff_class, response, cotangent):
    total = charge.shape[1]
    owners = lax.axis_size("gz")
    slabs = lax.axis_size("drift")
    planes, wires, ticks = cotangent.shape
    wire_taps = response.shape[1]
    half = (wire_taps - 1) // 2
    bins = total // slabs

    currents, keep, give, local_currents = cut_pieces(
        ovl_block, ovl_count, charge, intersection, cotangent, owners, half
    )
    received = swap(give, "gz", 1)
    sums, edges = relay(keep.astype(F32), received) if owners > 2 else ((), ())
    beyond = [swap(block, "gz", 2 * j) for j, block in enumerate(edges, 1)]
    others = [swap(block, "gz", 2 * j) for j, block in enumerate(sums, 1)]

    levels, kinds = smeared_levels(
        diff_class, response, bins, slabs, sums[0] if sums else received
    )
    table = build_table(levels, kinds, planes, wire_taps, ticks)
    partial = backward(table, cotangent, received, beyond, wire_taps)
    spread = [partial] + [swap(partial, "drift", k) for k in range(1, slabs)]

    cuts = cut_slabs(
        currents, received, others, local_currents, bins, slabs, planes - 1, half, partial
    )
    windows, ready = [cuts[0]], cuts[0]
    for step, block in enumerate(cuts[1:]):
        if step:
            block = ready = pass_on(block, windows[1:], step, cuts[0].shape[0])
        windows.append(swap(block, "drift", 1 << step))

    *cross, own = merge(spread, bins, total, ready)
    if owners == 4:
        across = [swap(block, "gz", 2) for block in cross]
        sources = [*cross, *(swap(block, "gz", 1) for block in cross)]
        sources += [*across, *(swap(block, "gz", 1) for block in across)]
    else:
        sources = [lax.all_gather(block, "gz", axis=0) for block in cross]
    signal, done = forward(windows, table, wires, wire_taps)
    charge_grad = charge_gradient(
        ovl_block, ovl_count, sources, own, intersection, owners, done
    )
    return signal, charge_grad


def solution(mesh):
    return jax.shard_map(
        local,
        mesh=mesh,
        in_specs=(
            P(("apa", "gz", "drift"), None),
            P(("apa", "gz", "drift"), None, None, None, None),
            P(("apa", "gz", "drift"), None, None),
            P(("apa", "gz", "drift"), None),
            P("apa"),
            P(),
            P("apa", "gz", "drift"),
        ),
        out_specs=(P("apa", "gz", "drift"), P(("apa", "gz", "drift"), None)),
        check_vma=False,
    )
```

```python
import functools
import math

import jax
import jax.numpy as jnp
from jax import lax
from jax.experimental import pallas as pl
from jax.experimental.pallas import tpu as pltpu
from jax.sharding import PartitionSpec as P

TPB = 8
HB = 2
CLASSES = 6
LANES = 128
EDGE = 16
GROUP = 8
WINDOW = 64
LEAD = HB * TPB - TPB // 2
VMEM_LIMIT = 24 * 1024 * 1024
WHOLE_VMEM = 61 * 1024 * 1024
BF16 = jnp.bfloat16
F32 = jnp.float32


def params(semantics=None, limit=VMEM_LIMIT):
    return pltpu.CompilerParams(vmem_limit_bytes=limit, dimension_semantics=semantics)


def vmem():
    return pl.BlockSpec(memory_space=pltpu.VMEM)


def smem():
    return pl.BlockSpec(memory_space=pltpu.SMEM)


def anywhere():
    return pl.BlockSpec(memory_space=pl.ANY)


def cost(flops, moved):
    return pl.CostEstimate(flops=int(flops), bytes_accessed=int(moved), transcendentals=0)


def swap(block, axis, distance):
    count = lax.axis_size(axis)
    return lax.ppermute(block, axis, [(i, i ^ distance) for i in range(count)])


def widths(number):
    spread = TPB * (0.2 + 0.15 * number)
    half = HB * TPB
    total = sum(math.exp(-((j + 0.5) ** 2) / (2.0 * spread * spread)) for j in range(-half, half))
    return 1.0 / (2.0 * spread * spread), 1.0 / total


def shared_lanes(left, right, shift, lane):
    if shift == 0:
        return left
    back = LANES - shift
    return jnp.where(lane < back, pltpu.roll(left, back, 1), pltpu.roll(right, back, 1))


def coded(rows, column):
    lane = lax.broadcasted_iota(jnp.int32, rows.shape, 1)
    level = jnp.broadcast_to(rows[:, column : column + 1].astype(BF16).astype(F32), rows.shape)
    return jnp.where(lane == 0, level, rows - level).astype(BF16)


def plain(rows, first):
    rows = rows.astype(F32)
    lane = lax.broadcasted_iota(jnp.int32, rows.shape, 1)
    level = jnp.broadcast_to(rows[:, :1], rows.shape)
    return jnp.where(lane == 0, level if first else jnp.zeros_like(rows), rows + level)


def levels_kernel(
    class_ref, response_ref, _, level_ref, kind_ref, flat_ref, *, bins, slabs, total
):
    planes, wire_taps, length = response_ref.shape
    rows = level_ref.shape[0] // planes
    groups = kind_ref.shape[0]
    slab = lax.axis_index("drift")
    lane = lax.broadcasted_iota(jnp.int32, (GROUP, LANES), 1)
    packed = class_ref[...].astype(F32)
    tiles = []
    for t in range(total // LANES):
        at = slice(t % 2 * LANES, (t % 2 + 1) * LANES)
        tiles.append(jnp.broadcast_to(packed[t // 2 : t // 2 + 1, at], (GROUP, LANES)))
    classes = tiles[0]
    none = jnp.zeros((GROUP, LANES), F32)
    numbers = none
    for source in range(slabs):
        at = source * bins - (WINDOW // 2 - HB)
        tile, shift = at // LANES, at % LANES
        pair = [tiles[t] if 0 <= t < len(tiles) else none for t in (tile, tile + 1)]
        numbers = jnp.where(slab == source, shared_lanes(pair[0], pair[1], shift, lane), numbers)
    x = slab * bins - (WINDOW // 2 - HB) + lane
    numbers = jnp.where((x >= 0) & (x < HB), (CLASSES + x).astype(F32), numbers)
    column = jnp.broadcast_to(numbers[:1], (LANES, LANES)).T.astype(jnp.int32)
    for m in range(groups):
        kind_ref[m] = column[m * GROUP : (m + 1) * GROUP]
    flat_ref[...] = jnp.zeros(flat_ref.shape, F32)
    for p in range(planes):
        flat_ref[p * rows : p * rows + wire_taps, :length] = response_ref[p].astype(F32)
    taps = flat_ref[...].astype(BF16)
    tap = lax.broadcasted_iota(jnp.int32, (LANES, 2 * LANES), 0)
    tick = lax.broadcasted_iota(jnp.int32, (LANES, 2 * LANES), 1)
    step = tick - tap - LEAD
    offset = step.astype(F32) - (TPB - 1) / 2.0
    squared = offset * offset
    inside = jnp.abs(offset) < HB * TPB
    for kind in range(CLASSES + HB):
        keep = inside
        if kind < CLASSES:
            narrow, scale = widths(kind)
        else:
            edge = kind - CLASSES
            narrow, scale = widths(0)
            for number in range(1, CLASSES):
                chosen = classes[:1, edge : edge + 1] == number
                narrow = jnp.where(chosen, widths(number)[0], narrow)
                scale = jnp.where(chosen, widths(number)[1], scale)
            keep = inside & (step >= -TPB * edge)
        smear = jnp.where(keep, jnp.exp(-(squared * narrow)) * scale, 0.0)
        high = smear.astype(BF16)
        low = (smear - high.astype(F32)).astype(BF16)
        near = jnp.dot(taps[:, :LANES], high, preferred_element_type=F32) + jnp.dot(
            taps[:, :LANES], low, preferred_element_type=F32
        )
        far = jnp.dot(taps[:, LANES:], high[:, :LANES], preferred_element_type=F32) + jnp.dot(
            taps[:, LANES:], low[:, :LANES], preferred_element_type=F32
        )
        level_ref[:, kind, :LANES] = near[:, :LANES]
        level_ref[:, kind, LANES:] = near[:, LANES:] + far


def smeared_levels(diff_class, response, bins, slabs, before):
    planes, wire_taps, _ = response.shape
    total = diff_class.shape[0]
    reach = 2 * LANES
    rows = -(-wire_taps // 8) * 8
    groups = (bins + WINDOW // 2) // GROUP
    classes = jnp.pad(diff_class.astype(BF16), (0, 8 * reach - total)).reshape(8, reach)
    return pl.pallas_call(
        functools.partial(levels_kernel, bins=bins, slabs=slabs, total=total),
        out_shape=(
            jax.ShapeDtypeStruct((planes * rows, CLASSES + HB, reach), F32),
            jax.ShapeDtypeStruct((groups, GROUP, LANES), jnp.int32),
        ),
        in_specs=[vmem(), vmem(), anywhere()],
        out_specs=(vmem(), vmem()),
        scratch_shapes=[pltpu.VMEM((planes * rows, reach), F32)],
        compiler_params=params(),
        cost_estimate=cost(1e8, 1e6),
        name="levels",
    )(classes, response, before)


def table_kernel(level_ref, kind_ref, table_ref, sum_ref, *, wire_taps):
    planes, blocks, depth, span = table_ref.shape
    rows = level_ref.shape[0] // planes
    groups = kind_ref.shape[0]
    tiles = span // LANES
    lane = lax.broadcasted_iota(jnp.int32, (GROUP, LANES), 1)
    row = lax.broadcasted_iota(jnp.int32, (GROUP, LANES), 0)
    starts = [LEAD_SHIFT + odd * (LANES // 2) + TPB * row for odd in range(2)]
    after = [lane >= start for start in starts]
    zero = jnp.zeros((GROUP, LANES), F32)
    empty = jnp.zeros((2 * GROUP, LANES), BF16)

    def body(a, plane):
        levels = level_ref[plane * rows + a]
        halves = [levels[:, :LANES], levels[:, LANES:]]
        pieces = []
        for m in range(groups):
            odd = m % 2
            parts = [
                pltpu.roll(
                    jnp.take_along_axis(half, kind_ref[m], axis=0),
                    LEAD_SHIFT + odd * (LANES // 2),
                    1,
                    stride=TPB,
                    stride_axis=0,
                )
                for half in halves
            ]
            pieces.append(
                (
                    jnp.where(after[odd], parts[0], zero),
                    jnp.where(after[odd], parts[1], parts[0]),
                    jnp.where(after[odd], zero, parts[1]),
                )
            )
        for block in range(blocks):
            for tile in range(tiles):
                here = slice(tile * LANES, (tile + 1) * LANES)
                total = zero
                for quarter in range(WINDOW // (2 * GROUP)):
                    m = 2 * (tiles * block + quarter)
                    at = a * WINDOW + quarter * 2 * GROUP
                    at = pl.ds(pl.multiple_of(at, 2 * GROUP), 2 * GROUP)
                    third = tile - quarter + 2
                    value = empty
                    if 0 <= third <= 2 and m + 1 < groups:
                        value = jnp.concatenate(
                            [pieces[m][third], pieces[m + 1][third]], axis=0
                        ).astype(BF16)
                        total = total + pieces[m][third] + pieces[m + 1][third]
                    table_ref[plane, block, at, here] = value
                sum_ref[a, block, :, here] = total
        return plane

    def whole_plane(plane, _):
        lax.fori_loop(0, wire_taps, body, plane, unroll=UNROLL)
        for block in range(blocks):
            total = jnp.sum(sum_ref[:, block], axis=1)
            high = total.astype(BF16).astype(F32)
            spare = jnp.zeros((depth - (WINDOW + 2) * wire_taps, span), F32)
            table_ref[plane, block, wire_taps * WINDOW :, :] = jnp.concatenate(
                [high, total - high, spare], axis=0
            ).astype(BF16)
        return 0

    lax.fori_loop(0, planes, whole_plane, 0)


UNROLL = 7
LEAD_SHIFT = (TPB * HB - LEAD) % LANES


def build_table(levels, kinds, planes, wire_taps, ticks_here):
    tiles = math.gcd(ticks_here, 2 * LANES) // LANES
    blocks = ticks_here // (tiles * LANES)
    shape = (planes, blocks, (wire_taps + 1) * WINDOW, tiles * LANES)
    return pl.pallas_call(
        functools.partial(table_kernel, wire_taps=wire_taps),
        out_shape=jax.ShapeDtypeStruct(shape, BF16),
        in_specs=[vmem(), vmem()],
        out_specs=vmem(),
        scratch_shapes=[pltpu.VMEM((wire_taps, blocks, GROUP, tiles * LANES), F32)],
        compiler_params=params(),
        cost_estimate=cost(4e9, 2 * math.prod(shape)),
        name="table",
    )(levels, kinds)


def back_kernel(table_ref, own_ref, received_ref, *refs, wire_taps):
    others, (out_ref, cot_ref, wide_ref) = refs[:-3], refs[-3:]
    planes, blocks, _, span = table_ref.shape
    _, wires, ticks = own_ref.shape
    total = received_ref.shape[1]
    half = (wire_taps - 1) // 2
    parts = ticks // total
    size = sixteens(planes * half)
    side = parts * size
    lows = received_ref.shape[0] - 2 * side
    even = lax.rem(lax.axis_index("gz"), 2) == 0
    lane = lax.broadcasted_iota(jnp.int32, (wires, LANES), 1)
    none = jnp.zeros((wires, LANES), F32)
    gap = jnp.zeros((EDGE - half, total), F32)
    step = span * 16 // LANES
    columns = (wire_taps + 1) // 2
    edges = []
    for part in range(parts):
        low = received_ref[lows + part * size : lows + (part + 1) * size].astype(F32)
        high = received_ref[lows + side + part * size : lows + side + (part + 1) * size].astype(F32)
        near = jnp.where(even, low, high)
        far = jnp.zeros((size, total), F32)
        for other in others:
            far += other[part * size : (part + 1) * size].astype(F32)
        edges.append((jnp.where(even, far, near), jnp.where(even, near, far)))
    for plane in range(planes):
        cot_ref[plane, EDGE : EDGE + wires] = own_ref[plane]
        for part in range(parts):
            here = slice(part * total, (part + 1) * total)
            before, after = [edge[plane * half : (plane + 1) * half] for edge in edges[part]]
            cot_ref[plane, :EDGE, here] = jnp.concatenate([gap, before], axis=0).astype(BF16)
            cot_ref[plane, EDGE + wires :, here] = jnp.concatenate([after, gap], axis=0).astype(BF16)
        result = none
        for block in range(blocks):
            i = (plane * blocks + block) % wide_ref.shape[0]
            wide = lax.dot_general(
                cot_ref[plane, :, block * span : (block + 1) * span],
                table_ref[plane, block, : columns * LANES],
                (((1,), (1,)), ((), ())),
                preferred_element_type=F32,
            )
            for column in range(columns):
                wide_ref[i, column] = wide[:, column * LANES : (column + 1) * LANES]
            left, right = none, none
            for column in range(columns):
                at = EDGE + half - 2 * column
                left += wide_ref[i, column, at : at + wires]
                if 2 * column + 1 < wire_taps:
                    right += wide_ref[i, column, at - 1 : at - 1 + wires]
            both = jnp.where(lane < WINDOW, left + pltpu.roll(right, WINDOW, 1), none)
            result += pltpu.roll(both, block * step, 1) if block else both
        out_ref[plane] = result.astype(BF16)


def backward(table, cotangent, received, others, wire_taps):
    planes, _, _, _ = table.shape
    _, wires, ticks = cotangent.shape
    extent = wires + 2 * EDGE
    columns = (wire_taps + 1) // 2
    return pl.pallas_call(
        functools.partial(back_kernel, wire_taps=wire_taps),
        out_shape=jax.ShapeDtypeStruct((planes, wires, LANES), BF16),
        in_specs=[vmem()] * (3 + len(others)),
        out_specs=vmem(),
        scratch_shapes=[
            pltpu.VMEM((planes, extent, ticks), BF16),
            pltpu.VMEM((2, columns, extent, LANES), F32),
        ],
        compiler_params=params(),
        cost_estimate=cost(4e9, 2 * math.prod(table.shape)),
        name="bin_gradients",
    )(table, cotangent, received, *others)


def merge_kernel(*refs, bins, lead):
    planes, wires, _ = refs[0].shape
    outs, slab_ref = refs[-planes - 1 : -1], refs[-1]
    parts = refs[: -planes - 2]
    total = outs[0].shape[1]
    slab = lax.axis_index("drift")
    for k, part in enumerate(parts):
        slab_ref[slab ^ k] = part[...]
    lane = lax.broadcasted_iota(jnp.int32, (wires, LANES), 1)
    none = jnp.zeros((wires, LANES), F32)
    for p in range(planes):
        tiles = [none] * (total // LANES)
        for source in range(len(parts)):
            values = slab_ref[source, p].astype(F32)
            tile, shift = (source * bins - lead) // LANES, (source * bins - lead) % LANES
            if shift:
                values = pltpu.roll(values, shift, 1)
            for t, inside in ((tile, lane >= shift), (tile + 1, lane < shift)):
                if 0 <= t < len(tiles):
                    tiles[t] += jnp.where(inside, values, none)
        for t, values in enumerate(tiles):
            outs[p][:, t * LANES : (t + 1) * LANES] = values.astype(BF16)


def merge(parts, bins, total, before):
    planes, wires, _ = parts[0].shape
    return pl.pallas_call(
        functools.partial(merge_kernel, bins=bins, lead=WINDOW // 2 - HB),
        out_shape=(jax.ShapeDtypeStruct((wires, total), BF16),) * planes,
        in_specs=[vmem()] * len(parts) + [anywhere()],
        out_specs=(vmem(),) * planes,
        scratch_shapes=[pltpu.VMEM((len(parts), planes, wires, LANES), BF16)],
        compiler_params=params(),
        cost_estimate=cost(1e8, 4 * planes * wires * total),
        name="merge_bins",
    )(*parts, before)


def charge_kernel(block_ref, count_ref, *refs):
    sources, (local_ref, share_ref, signal_ref, out_hbm, signal_hbm) = refs[:-9], refs[-9:-4]
    all_ref, chosen_ref, out_ref, sems = refs[-4:]
    cells, planes, entries, wire_block, width = share_ref.shape
    owners, _, wires, total = all_ref.shape
    per_owner = wires // wire_block
    z = lax.axis_index("gz")
    for i, source in enumerate(sources):
        if len(sources) == planes - 1:
            all_ref[:, i] = source[...]
        else:
            all_ref[z ^ (i // (planes - 1)), i % (planes - 1)] = source[...]
    empty = jnp.zeros((wire_block, total), BF16)
    stores = [pltpu.make_async_copy(signal_ref, signal_hbm, sems.at[cells])]
    stores[0].start()
    for b in range(cells):
        for p in range(planes):
            for k in range(entries):
                name = block_ref[p, k, b]
                if p < planes - 1:
                    name = jnp.clip(name, 0, owners * per_owner - 1)
                    owner = name // per_owner
                    start = pl.multiple_of((name - owner * per_owner) * wire_block, wire_block)
                    rows = all_ref[owner, p, pl.ds(start, wire_block), :]
                else:
                    name = jnp.clip(name - z * per_owner, 0, per_owner - 1)
                    start = pl.multiple_of(name * wire_block, wire_block)
                    rows = local_ref[pl.ds(start, wire_block), :]
                at = (p * entries + k) * wire_block
                chosen_ref[b, at : at + wire_block] = jnp.where(k < count_ref[b, p], rows, empty)
        here = slice(b * width, (b + 1) * width)
        out_ref[here] = lax.dot_general(
            share_ref[b].reshape(planes * entries * wire_block, width),
            chosen_ref[b],
            (((0,), (0,)), ((), ())),
            preferred_element_type=F32,
        ).astype(BF16)
        store = pltpu.make_async_copy(out_ref.at[here], out_hbm.at[here], sems.at[b])
        store.start()
        stores.append(store)
    for store in stores:
        store.wait()


def charge_gradient(ovl_block, ovl_count, sources, local, intersection, owners, signal):
    cells, planes, entries, wire_block, width = intersection.shape
    wires, total = local.shape
    shape = (owners, planes - 1, wires, total)
    return pl.pallas_call(
        charge_kernel,
        out_shape=(
            jax.ShapeDtypeStruct((cells * width, total), BF16),
            jax.ShapeDtypeStruct(signal.shape, BF16),
        ),
        in_specs=[smem(), smem()] + [vmem()] * (len(sources) + 3),
        out_specs=(anywhere(), anywhere()),
        scratch_shapes=[
            pltpu.VMEM(shape, BF16),
            pltpu.VMEM((cells, planes * entries * wire_block, total), BF16),
            pltpu.VMEM((cells * width, total), BF16),
            pltpu.SemaphoreType.DMA((cells + 1,)),
        ],
        compiler_params=params(),
        cost_estimate=cost(1e8, 2 * math.prod(shape)),
        name="charge_gradient",
    )(jnp.transpose(ovl_block, (1, 2, 0)), ovl_count, *sources, local, intersection, signal)


def pieces_kernel(
    block_hbm, count_hbm, charge_hbm, share_hbm, cot_hbm, own_hbm, keep_hbm, give_hbm, local_hbm,
    block_ref, count_ref, charge_ref, share_ref, edge_ref, cross_ref, own_ref, keep_ref, give_ref, local_ref,
    sems, out_sems, *, half,
):
    cells, planes, entries, wire_block, width = share_ref.shape
    wires, total = local_ref.shape
    ticks = edge_ref.shape[3]
    per_owner = wires // wire_block
    cut = own_ref.shape[0]
    halves = 1 + keep_ref.shape[0]
    owners = 2 * halves
    z = lax.axis_index("gz")
    loads = [
        pltpu.make_async_copy(source, target, sems.at[i])
        for i, (source, target) in enumerate(
            (
                (block_hbm, block_ref),
                (count_hbm, count_ref),
                (charge_hbm, charge_ref),
                (share_hbm, share_ref),
                (cot_hbm.at[:, :EDGE], edge_ref.at[0]),
                (cot_hbm.at[:, wires - EDGE :], edge_ref.at[1]),
            )
        )
    ]
    for load in loads:
        load.start()
    cross_ref[...] = jnp.zeros(cross_ref.shape, F32)
    local_ref[...] = jnp.zeros(local_ref.shape, F32)
    for load in loads[:4]:
        load.wait()
    for b in range(cells):
        pieces = (
            jnp.dot(
                share_ref[b].reshape(planes * entries * wire_block, width),
                charge_ref[b * width : (b + 1) * width],
                preferred_element_type=F32,
            )
            .astype(BF16)
            .astype(F32)
        )
        for p in range(planes):
            for k in range(entries):
                at = (p * entries + k) * wire_block
                piece = pieces[at : at + wire_block]
                piece = jnp.where(k < count_ref[b, p], piece, jnp.zeros_like(piece))
                name = block_ref[p, k, b]
                if p < planes - 1:
                    name = jnp.clip(name, 0, owners * per_owner - 1)
                    start = pl.multiple_of(EDGE + name * wire_block, EDGE)
                    cross_ref[p, pl.ds(start, wire_block)] += piece
                else:
                    name = jnp.clip(name - z * per_owner, 0, per_owner - 1)
                    start = pl.multiple_of(name * wire_block, wire_block)
                    local_ref[pl.ds(start, wire_block)] += piece
    for load in loads[4:]:
        load.wait()
    at = halves * cut
    gap = jnp.zeros((sixteens(planes * half) - planes * half, ticks), F32)
    for side, first in ((0, 0), (1, EDGE - half)):
        rows = [edge_ref[side, p].astype(F32)[first : first + half] for p in range(planes)]
        rows = jnp.concatenate(rows + [gap], axis=0).astype(BF16)
        for part in range(ticks // total):
            give_ref[at : at + rows.shape[0]] = rows[:, part * total : (part + 1) * total]
            at += rows.shape[0]
    extent = wires + 2 * EDGE
    none = jnp.zeros((half, total), F32)
    stores = [
        pltpu.make_async_copy(source, target, out_sems.at[i])
        for i, (source, target) in enumerate(
            (
                (give_ref, give_hbm),
                (keep_ref, keep_hbm),
                (own_ref, own_hbm),
                (local_ref, local_hbm),
            )
        )
    ]
    stores[3].start()
    for k in [*range(1, owners, 2), *range(2, owners, 2), 0]:
        to = z ^ k
        blocks = []
        for p in range(planes - 1):
            rows = cross_ref[p, pl.ds(pl.multiple_of(to * wires, EDGE), extent)]
            blocks.append(rows[EDGE - half : extent - EDGE + half])
        blocks.append(jnp.where(to == z + 1, local_ref[wires - half :], none))
        blocks.append(jnp.where(to == z - 1, local_ref[:half], none))
        rows = padded(blocks)
        if k % 2:
            give_ref[k // 2 * cut : (k // 2 + 1) * cut] = coded(rows, 0)
        elif k:
            keep_ref[k // 2 - 1] = coded(rows, 0)
        else:
            own_ref[...] = rows
        if k == owners - 1:
            stores[0].start()
        if k == owners - 2 and k:
            stores[1].start()
    if owners == 2:
        stores[1].start()
    stores[2].start()
    for store in stores:
        store.wait()


def sixteens(rows):
    return -(-rows // 16) * 16


def padded(blocks):
    count = sum(block.shape[0] for block in blocks)
    if count % 16:
        blocks = blocks + [jnp.zeros((sixteens(count) - count, blocks[0].shape[1]), F32)]
    return jnp.concatenate(blocks, axis=0)


def cut_pieces(ovl_block, ovl_count, charge, intersection, cotangent, owners, half):
    cells, planes, entries, wire_block, width = intersection.shape
    total = charge.shape[1]
    _, wires, ticks = cotangent.shape
    rows = sixteens((planes - 1) * (wires + 2 * half) + 2 * half)
    edges = 2 * sixteens(planes * half) * ticks // total
    hbm = pl.BlockSpec(memory_space=pltpu.HBM)
    blocks = jnp.transpose(ovl_block, (1, 2, 0))
    outs = (
        jax.ShapeDtypeStruct((rows, total), F32),
        jax.ShapeDtypeStruct((owners // 2 - 1, rows, total), BF16),
        jax.ShapeDtypeStruct((owners // 2 * rows + edges, total), BF16),
        jax.ShapeDtypeStruct((wires, total), F32),
    )
    return pl.pallas_call(
        functools.partial(pieces_kernel, half=half),
        out_shape=outs,
        in_specs=[hbm] * 5,
        out_specs=(hbm,) * 4,
        scratch_shapes=[
            pltpu.SMEM(blocks.shape, jnp.int32),
            pltpu.SMEM(ovl_count.shape, jnp.int32),
            pltpu.VMEM(charge.shape, BF16),
            pltpu.VMEM(intersection.shape, BF16),
            pltpu.VMEM((2, planes, EDGE, ticks), BF16),
            pltpu.VMEM((planes - 1, owners * wires + 2 * EDGE, total), F32),
            *[pltpu.VMEM(out.shape, out.dtype) for out in outs],
            pltpu.SemaphoreType.DMA((6,)),
            pltpu.SemaphoreType.DMA((4,)),
        ],
        compiler_params=params(limit=WHOLE_VMEM),
        cost_estimate=cost(1e8, 4 * owners * rows * total),
        name="pieces",
    )(blocks, ovl_count, charge, intersection, cotangent)


def relay_kernel(keep_ref, received_ref, *outs):
    others, rows, _ = keep_ref.shape
    edges = (received_ref.shape[0] - (others + 1) * rows) // 2
    z = lax.axis_index("gz")
    even = lax.rem(z, 2) == 0
    low = received_ref[(others + 1) * rows : (others + 1) * rows + edges]
    high = received_ref[(others + 1) * rows + edges :]
    for j in range(others):
        to = z ^ (2 * (j + 1))
        summed = plain(keep_ref[j], True)
        summed += plain(received_ref[(j + 1) * rows : (j + 2) * rows], True)
        outs[j][...] = coded(summed, 0)
        upward, downward = even & (to == z + 2), jnp.logical_not(even) & (to == z - 2)
        outs[others + j][...] = jnp.where(
            upward, high, jnp.where(downward, low, jnp.zeros_like(low))
        )


def relay(keep, received):
    others, rows, total = keep.shape
    edges = (received.shape[0] - (others + 1) * rows) // 2
    outs = pl.pallas_call(
        relay_kernel,
        out_shape=(jax.ShapeDtypeStruct((rows, total), BF16),) * others
        + (jax.ShapeDtypeStruct((edges, total), BF16),) * others,
        in_specs=[vmem(), vmem()],
        out_specs=(vmem(),) * (2 * others),
        compiler_params=params(),
        cost_estimate=cost(1e7, 6 * others * rows * total),
        name="relay",
    )(keep, received)
    return outs[:others], outs[others:]


def slabs_kernel(*refs, bins, lead, slabs, cross, half):
    count = len(refs) - slabs.bit_length() - 1
    keep_ref, received_ref, others, local_ref = refs[0], refs[1], refs[2 : count - 2], refs[count - 2]
    outs, cut_ref = refs[count:-1], refs[-1]
    total = local_ref.shape[1]
    cut = keep_ref.shape[0]
    summed = keep_ref[...] + plain(received_ref[:cut], True)
    for other in others:
        summed += plain(other[...], True)
    wires = local_ref.shape[0]
    edge = cross * (wires + 2 * half)
    rows = padded([summed[: edge + half], local_ref[...], summed[edge + half : edge + 2 * half]])
    none = jnp.zeros((rows.shape[0], LANES), F32)
    lane = lax.broadcasted_iota(jnp.int32, none.shape, 1)
    level = jnp.broadcast_to(rows[:, :1].astype(BF16).astype(F32), none.shape)
    tiles = [rows[:, t * LANES : (t + 1) * LANES] - level for t in range(total // LANES)]
    for to in range(slabs):
        at = to * bins - lead
        tile, shift = at // LANES, at % LANES
        pair = [tiles[t] if 0 <= t < len(tiles) else -level for t in (tile, tile + 1)]
        value = shared_lanes(pair[0], pair[1], shift, lane)
        cut_ref[to] = jnp.where(lane == 0, level, value).astype(BF16)
    slab = lax.axis_index("drift")
    outs[0][...] = cut_ref[slab]
    size = rows.shape[0]
    for s, out in enumerate(outs[1:]):
        for i in range(slabs >> (s + 1)):
            out[i * size : (i + 1) * size] = cut_ref[slab ^ ((2 * i + 1) << s)]


def cut_slabs(keep, received, others, local, bins, slabs, cross, half, before):
    wires, total = local.shape
    rows = sixteens((cross + 1) * (wires + 2 * half))
    steps = slabs.bit_length() - 1
    counts = [1] + [slabs >> (s + 1) for s in range(steps)]
    return pl.pallas_call(
        functools.partial(
            slabs_kernel, bins=bins, lead=WINDOW // 2 - HB, slabs=slabs, cross=cross, half=half
        ),
        out_shape=tuple(jax.ShapeDtypeStruct((n * rows, LANES), BF16) for n in counts),
        in_specs=[vmem()] * (3 + len(others)) + [anywhere()],
        out_specs=(vmem(),) * len(counts),
        scratch_shapes=[pltpu.VMEM((slabs, rows, LANES), BF16)],
        compiler_params=params(),
        cost_estimate=cost(1e8, 4 * rows * total),
        name="slab_currents",
    )(keep, received, *others, local, before)


def pass_kernel(*refs, step, size):
    own_ref, arrived, out_ref = refs[0], refs[1:-1], refs[-1]
    for i in range(own_ref.shape[0] // size):
        here = slice(i * size, (i + 1) * size)
        total = plain(own_ref[here], False)
        for r, other in enumerate(arrived):
            at = ((2 * i + 1) << step) >> (r + 1)
            total += plain(other[at * size : (at + 1) * size], False)
        out_ref[here] = coded(total, WINDOW // 2)


def pass_on(own, arrived, step, size):
    return pl.pallas_call(
        functools.partial(pass_kernel, step=step, size=size),
        out_shape=jax.ShapeDtypeStruct(own.shape, BF16),
        in_specs=[vmem()] * (1 + len(arrived)),
        out_specs=vmem(),
        compiler_params=params(),
        cost_estimate=cost(1e6, 4 * math.prod(own.shape)),
        name="pass_on",
    )(own, *arrived)


def signal_kernel(*refs, wire_taps):
    parts, (table_ref, out_ref, even_ref, odd_ref, level_ref, lines_ref) = refs[:-6], refs[-6:]
    planes, blocks, _, span = table_ref.shape
    _, wires, _ = out_ref.shape
    half = (wire_taps - 1) // 2
    extent = wires + 2 * half
    step = span * 16 // LANES
    middle = WINDOW // 2
    lane = lax.broadcasted_iota(jnp.int32, (wires, LANES), 1)
    size = parts[0].shape[0]
    summed = plain(parts[0][...], False)
    for part in parts[1:]:
        summed += plain(part[:size], False)
    for p in range(planes):
        currents = summed[p * extent : (p + 1) * extent]
        level = currents[:, middle : middle + 1].astype(BF16).astype(F32)
        level = jnp.broadcast_to(level, currents.shape)
        level_ref[p] = level
        currents = currents - level
        levels = jnp.zeros((wires, LANES), F32)
        for a in range(wire_taps):
            at = a
            both = (lane == WINDOW + a) | (lane == WINDOW + wire_taps + a)
            levels = jnp.where(both, level_ref[p, at : at + wires], levels)
        for block in range(blocks):
            i = p * blocks + block
            even_ref[i] = pltpu.roll(currents, (-step * block) % LANES, 1)
            odd_ref[i] = pltpu.roll(currents, (WINDOW - step * block) % LANES, 1)
            for pair in range((wire_taps + 1) // 2):
                at = 2 * pair
                right = levels
                if 2 * pair + 1 < wire_taps:
                    right = odd_ref[i, at + 1 : at + 1 + wires]
                line = jnp.where(lane < WINDOW, even_ref[i, at : at + wires], right)
                lines_ref[i % 2, :, pair * LANES : (pair + 1) * LANES] = line.astype(BF16)
            out_ref[p, :, block * span : (block + 1) * span] = jnp.dot(
                lines_ref[i % 2], table_ref[p, block], preferred_element_type=F32
            ).astype(BF16)


def forward(parts, table, wires, wire_taps):
    planes, blocks, depth, span = table.shape
    extent = wires + wire_taps - 1
    shape = (planes, wires, blocks * span)
    return pl.pallas_call(
        functools.partial(signal_kernel, wire_taps=wire_taps),
        out_shape=jax.ShapeDtypeStruct(shape, BF16),
        in_specs=[vmem()] * (len(parts) + 1),
        out_specs=vmem(),
        scratch_shapes=[
            pltpu.VMEM((planes * blocks, extent, LANES), F32),
            pltpu.VMEM((planes * blocks, extent, LANES), F32),
            pltpu.VMEM((planes, extent, LANES), F32),
            pltpu.VMEM((2, wires, depth), BF16),
        ],
        compiler_params=params(),
        cost_estimate=cost(4e9, 2 * math.prod(table.shape)),
        name="signal",
    )(*parts, table)


def local(charge, intersection, ovl_block, ovl_count, diff_class, response, cotangent):
    total = charge.shape[1]
    owners = lax.axis_size("gz")
    slabs = lax.axis_size("drift")
    planes, wires, ticks = cotangent.shape
    wire_taps = response.shape[1]
    half = (wire_taps - 1) // 2
    bins = total // slabs

    currents, keep, give, local_currents = cut_pieces(
        ovl_block, ovl_count, charge, intersection, cotangent, owners, half
    )
    received = swap(give, "gz", 1)
    sums, edges = relay(keep.astype(F32), received) if owners > 2 else ((), ())
    beyond = [swap(block, "gz", 2 * j) for j, block in enumerate(edges, 1)]
    others = [swap(block, "gz", 2 * j) for j, block in enumerate(sums, 1)]

    levels, kinds = smeared_levels(
        diff_class, response, bins, slabs, sums[0] if sums else received
    )
    table = build_table(levels, kinds, planes, wire_taps, ticks)
    partial = backward(table, cotangent, received, beyond, wire_taps)
    spread = [partial] + [swap(partial, "drift", k) for k in range(1, slabs)]

    cuts = cut_slabs(
        currents, received, others, local_currents, bins, slabs, planes - 1, half, partial
    )
    windows, ready = [cuts[0]], cuts[0]
    for step, block in enumerate(cuts[1:]):
        if step:
            block = ready = pass_on(block, windows[1:], step, cuts[0].shape[0])
        windows.append(swap(block, "drift", 1 << step))

    *cross, own = merge(spread, bins, total, ready)
    if owners == 4:
        across = [swap(block, "gz", 2) for block in cross]
        sources = [*cross, *(swap(block, "gz", 1) for block in cross)]
        sources += [*across, *(swap(block, "gz", 1) for block in across)]
    else:
        sources = [lax.all_gather(block, "gz", axis=0) for block in cross]
    signal = forward(windows, table, wires, wire_taps)
    charge_grad, signal = charge_gradient(
        ovl_block, ovl_count, sources, own, intersection, owners, signal
    )
    return signal, charge_grad


def solution(mesh):
    return jax.shard_map(
        local,
        mesh=mesh,
        in_specs=(
            P(("apa", "gz", "drift"), None),
            P(("apa", "gz", "drift"), None, None, None, None),
            P(("apa", "gz", "drift"), None, None),
            P(("apa", "gz", "drift"), None),
            P("apa"),
            P(),
            P("apa", "gz", "drift"),
        ),
        out_specs=(P("apa", "gz", "drift"), P(("apa", "gz", "drift"), None)),
        check_vma=False,
    )
```

```python
import functools
import math

import jax
import jax.numpy as jnp
from jax import lax
from jax.experimental import pallas as pl
from jax.experimental.pallas import tpu as pltpu
from jax.sharding import PartitionSpec as P

TPB = 8
HB = 2
CLASSES = 6
LANES = 128
EDGE = 16
GROUP = 8
WINDOW = 64
LEAD = HB * TPB - TPB // 2
VMEM_LIMIT = 24 * 1024 * 1024
WHOLE_VMEM = 61 * 1024 * 1024
BF16 = jnp.bfloat16
F32 = jnp.float32


def params(semantics=None, limit=VMEM_LIMIT):
    return pltpu.CompilerParams(vmem_limit_bytes=limit, dimension_semantics=semantics)


def vmem():
    return pl.BlockSpec(memory_space=pltpu.VMEM)


def smem():
    return pl.BlockSpec(memory_space=pltpu.SMEM)


def anywhere():
    return pl.BlockSpec(memory_space=pl.ANY)


def cost(flops, moved):
    return pl.CostEstimate(flops=int(flops), bytes_accessed=int(moved), transcendentals=0)


def swap(block, axis, distance):
    count = lax.axis_size(axis)
    return lax.ppermute(block, axis, [(i, i ^ distance) for i in range(count)])


def widths(number):
    spread = TPB * (0.2 + 0.15 * number)
    half = HB * TPB
    total = sum(math.exp(-((j + 0.5) ** 2) / (2.0 * spread * spread)) for j in range(-half, half))
    return 1.0 / (2.0 * spread * spread), 1.0 / total


def shared_lanes(left, right, shift, lane):
    if shift == 0:
        return left
    back = LANES - shift
    return jnp.where(lane < back, pltpu.roll(left, back, 1), pltpu.roll(right, back, 1))


def coded(rows, column):
    lane = lax.broadcasted_iota(jnp.int32, rows.shape, 1)
    level = jnp.broadcast_to(rows[:, column : column + 1].astype(BF16).astype(F32), rows.shape)
    return jnp.where(lane == 0, level, rows - level).astype(BF16)


def plain(rows, first):
    rows = rows.astype(F32)
    lane = lax.broadcasted_iota(jnp.int32, rows.shape, 1)
    level = jnp.broadcast_to(rows[:, :1], rows.shape)
    return jnp.where(lane == 0, level if first else jnp.zeros_like(rows), rows + level)


def levels_kernel(
    class_ref, response_ref, _, level_ref, kind_ref, flat_ref, *, bins, slabs, total
):
    planes, wire_taps, length = response_ref.shape
    rows = level_ref.shape[0] // planes
    groups = kind_ref.shape[0]
    slab = lax.axis_index("drift")
    lane = lax.broadcasted_iota(jnp.int32, (GROUP, LANES), 1)
    packed = class_ref[...].astype(F32)
    tiles = []
    for t in range(total // LANES):
        at = slice(t % 2 * LANES, (t % 2 + 1) * LANES)
        tiles.append(jnp.broadcast_to(packed[t // 2 : t // 2 + 1, at], (GROUP, LANES)))
    classes = tiles[0]
    none = jnp.zeros((GROUP, LANES), F32)
    numbers = none
    for source in range(slabs):
        at = source * bins - (WINDOW // 2 - HB)
        tile, shift = at // LANES, at % LANES
        pair = [tiles[t] if 0 <= t < len(tiles) else none for t in (tile, tile + 1)]
        numbers = jnp.where(slab == source, shared_lanes(pair[0], pair[1], shift, lane), numbers)
    x = slab * bins - (WINDOW // 2 - HB) + lane
    numbers = jnp.where((x >= 0) & (x < HB), (CLASSES + x).astype(F32), numbers)
    column = jnp.broadcast_to(numbers[:1], (LANES, LANES)).T.astype(jnp.int32)
    for m in range(groups):
        kind_ref[m] = column[m * GROUP : (m + 1) * GROUP]
    flat_ref[...] = jnp.zeros(flat_ref.shape, F32)
    for p in range(planes):
        flat_ref[p * rows : p * rows + wire_taps, :length] = response_ref[p].astype(F32)
    taps = flat_ref[...].astype(BF16)
    tap = lax.broadcasted_iota(jnp.int32, (LANES, 2 * LANES), 0)
    tick = lax.broadcasted_iota(jnp.int32, (LANES, 2 * LANES), 1)
    step = tick - tap - LEAD
    offset = step.astype(F32) - (TPB - 1) / 2.0
    squared = offset * offset
    inside = jnp.abs(offset) < HB * TPB
    for kind in range(CLASSES + HB):
        keep = inside
        if kind < CLASSES:
            narrow, scale = widths(kind)
        else:
            edge = kind - CLASSES
            narrow, scale = widths(0)
            for number in range(1, CLASSES):
                chosen = classes[:1, edge : edge + 1] == number
                narrow = jnp.where(chosen, widths(number)[0], narrow)
                scale = jnp.where(chosen, widths(number)[1], scale)
            keep = inside & (step >= -TPB * edge)
        smear = jnp.where(keep, jnp.exp(-(squared * narrow)) * scale, 0.0)
        high = smear.astype(BF16)
        low = (smear - high.astype(F32)).astype(BF16)
        near = jnp.dot(taps[:, :LANES], high, preferred_element_type=F32) + jnp.dot(
            taps[:, :LANES], low, preferred_element_type=F32
        )
        far = jnp.dot(taps[:, LANES:], high[:, :LANES], preferred_element_type=F32) + jnp.dot(
            taps[:, LANES:], low[:, :LANES], preferred_element_type=F32
        )
        level_ref[:, kind, :LANES] = near[:, :LANES]
        level_ref[:, kind, LANES:] = near[:, LANES:] + far


def smeared_levels(diff_class, response, bins, slabs, before):
    planes, wire_taps, _ = response.shape
    total = diff_class.shape[0]
    reach = 2 * LANES
    rows = -(-wire_taps // 8) * 8
    groups = (bins + WINDOW // 2) // GROUP
    classes = jnp.pad(diff_class.astype(BF16), (0, 8 * reach - total)).reshape(8, reach)
    return pl.pallas_call(
        functools.partial(levels_kernel, bins=bins, slabs=slabs, total=total),
        out_shape=(
            jax.ShapeDtypeStruct((planes * rows, CLASSES + HB, reach), F32),
            jax.ShapeDtypeStruct((groups, GROUP, LANES), jnp.int32),
        ),
        in_specs=[vmem(), vmem(), anywhere()],
        out_specs=(vmem(), vmem()),
        scratch_shapes=[pltpu.VMEM((planes * rows, reach), F32)],
        compiler_params=params(),
        cost_estimate=cost(1e8, 1e6),
        name="levels",
    )(classes, response, before)


def table_kernel(level_ref, kind_ref, table_ref, sum_ref, *, wire_taps):
    planes, blocks, depth, span = table_ref.shape
    rows = level_ref.shape[0] // planes
    groups = kind_ref.shape[0]
    tiles = span // LANES
    lane = lax.broadcasted_iota(jnp.int32, (GROUP, LANES), 1)
    row = lax.broadcasted_iota(jnp.int32, (GROUP, LANES), 0)
    starts = [LEAD_SHIFT + odd * (LANES // 2) + TPB * row for odd in range(2)]
    after = [lane >= start for start in starts]
    zero = jnp.zeros((GROUP, LANES), F32)
    empty = jnp.zeros((2 * GROUP, LANES), BF16)

    def body(a, plane):
        levels = level_ref[plane * rows + a]
        halves = [levels[:, :LANES], levels[:, LANES:]]
        pieces = []
        for m in range(groups):
            odd = m % 2
            parts = [
                pltpu.roll(
                    jnp.take_along_axis(half, kind_ref[m], axis=0),
                    LEAD_SHIFT + odd * (LANES // 2),
                    1,
                    stride=TPB,
                    stride_axis=0,
                )
                for half in halves
            ]
            pieces.append(
                (
                    jnp.where(after[odd], parts[0], zero),
                    jnp.where(after[odd], parts[1], parts[0]),
                    jnp.where(after[odd], zero, parts[1]),
                )
            )
        for block in range(blocks):
            for tile in range(tiles):
                here = slice(tile * LANES, (tile + 1) * LANES)
                total = zero
                for quarter in range(WINDOW // (2 * GROUP)):
                    m = 2 * (tiles * block + quarter)
                    at = a * WINDOW + quarter * 2 * GROUP
                    at = pl.ds(pl.multiple_of(at, 2 * GROUP), 2 * GROUP)
                    third = tile - quarter + 2
                    value = empty
                    if 0 <= third <= 2 and m + 1 < groups:
                        value = jnp.concatenate(
                            [pieces[m][third], pieces[m + 1][third]], axis=0
                        ).astype(BF16)
                        total = total + pieces[m][third] + pieces[m + 1][third]
                    table_ref[plane, block, at, here] = value
                sum_ref[a, block, :, here] = total
        return plane

    def whole_plane(plane, _):
        lax.fori_loop(0, wire_taps, body, plane, unroll=UNROLL)
        for block in range(blocks):
            total = jnp.sum(sum_ref[:, block], axis=1)
            high = total.astype(BF16).astype(F32)
            spare = jnp.zeros((depth - (WINDOW + 2) * wire_taps, span), F32)
            table_ref[plane, block, wire_taps * WINDOW :, :] = jnp.concatenate(
                [high, total - high, spare], axis=0
            ).astype(BF16)
        return 0

    lax.fori_loop(0, planes, whole_plane, 0)


UNROLL = 7
LEAD_SHIFT = (TPB * HB - LEAD) % LANES


def build_table(levels, kinds, planes, wire_taps, ticks_here):
    tiles = math.gcd(ticks_here, 2 * LANES) // LANES
    blocks = ticks_here // (tiles * LANES)
    shape = (planes, blocks, (wire_taps + 1) * WINDOW, tiles * LANES)
    return pl.pallas_call(
        functools.partial(table_kernel, wire_taps=wire_taps),
        out_shape=jax.ShapeDtypeStruct(shape, BF16),
        in_specs=[vmem(), vmem()],
        out_specs=vmem(),
        scratch_shapes=[pltpu.VMEM((wire_taps, blocks, GROUP, tiles * LANES), F32)],
        compiler_params=params(),
        cost_estimate=cost(4e9, 2 * math.prod(shape)),
        name="table",
    )(levels, kinds)


def back_kernel(table_ref, own_ref, received_ref, *refs, wire_taps):
    others, (out_ref, cross_ref, cot_ref, wide_ref) = refs[:-4], refs[-4:]
    planes, blocks, _, span = table_ref.shape
    _, wires, ticks = own_ref.shape
    total = received_ref.shape[1]
    half = (wire_taps - 1) // 2
    parts = ticks // total
    size = sixteens(planes * half)
    side = parts * size
    lows = received_ref.shape[0] - 2 * side
    even = lax.rem(lax.axis_index("gz"), 2) == 0
    lane = lax.broadcasted_iota(jnp.int32, (wires, LANES), 1)
    none = jnp.zeros((wires, LANES), F32)
    gap = jnp.zeros((EDGE - half, total), F32)
    step = span * 16 // LANES
    columns = (wire_taps + 1) // 2
    edges = []
    for part in range(parts):
        low = received_ref[lows + part * size : lows + (part + 1) * size].astype(F32)
        high = received_ref[lows + side + part * size : lows + side + (part + 1) * size].astype(F32)
        near = jnp.where(even, low, high)
        far = jnp.zeros((size, total), F32)
        for other in others:
            far += other[part * size : (part + 1) * size].astype(F32)
        edges.append((jnp.where(even, far, near), jnp.where(even, near, far)))
    for plane in range(planes):
        cot_ref[plane, EDGE : EDGE + wires] = own_ref[plane]
        for part in range(parts):
            here = slice(part * total, (part + 1) * total)
            before, after = [edge[plane * half : (plane + 1) * half] for edge in edges[part]]
            cot_ref[plane, :EDGE, here] = jnp.concatenate([gap, before], axis=0).astype(BF16)
            cot_ref[plane, EDGE + wires :, here] = jnp.concatenate([after, gap], axis=0).astype(BF16)
        result = none
        for block in range(blocks):
            i = (plane * blocks + block) % wide_ref.shape[0]
            wide = lax.dot_general(
                cot_ref[plane, :, block * span : (block + 1) * span],
                table_ref[plane, block, : columns * LANES],
                (((1,), (1,)), ((), ())),
                preferred_element_type=F32,
            )
            for column in range(columns):
                wide_ref[i, column] = wide[:, column * LANES : (column + 1) * LANES]
            left, right = none, none
            for column in range(columns):
                at = EDGE + half - 2 * column
                left += wide_ref[i, column, at : at + wires]
                if 2 * column + 1 < wire_taps:
                    right += wide_ref[i, column, at - 1 : at - 1 + wires]
            both = jnp.where(lane < WINDOW, left + pltpu.roll(right, WINDOW, 1), none)
            result += pltpu.roll(both, block * step, 1) if block else both
        out_ref[plane] = result.astype(BF16)
        if plane < planes - 1:
            cross_ref[plane] = result.astype(BF16)


def backward(table, cotangent, received, others, wire_taps):
    planes, _, _, _ = table.shape
    _, wires, ticks = cotangent.shape
    extent = wires + 2 * EDGE
    columns = (wire_taps + 1) // 2
    return pl.pallas_call(
        functools.partial(back_kernel, wire_taps=wire_taps),
        out_shape=(
            jax.ShapeDtypeStruct((planes, wires, LANES), BF16),
            jax.ShapeDtypeStruct((planes - 1, wires, LANES), BF16),
        ),
        in_specs=[vmem()] * (3 + len(others)),
        out_specs=(vmem(), vmem()),
        scratch_shapes=[
            pltpu.VMEM((planes, extent, ticks), BF16),
            pltpu.VMEM((2, columns, extent, LANES), F32),
        ],
        compiler_params=params(),
        cost_estimate=cost(4e9, 2 * math.prod(table.shape)),
        name="bin_gradients",
    )(table, cotangent, received, *others)


def join_kernel(first_ref, second_ref, out_ref):
    count = out_ref.shape[0] // 2
    out_ref[:count] = first_ref[first_ref.shape[0] - count :]
    out_ref[count:] = second_ref[second_ref.shape[0] - count :]


def join(first, second, count):
    shape = (2 * count,) + first.shape[1:]
    return pl.pallas_call(
        join_kernel,
        out_shape=jax.ShapeDtypeStruct(shape, BF16),
        in_specs=[vmem()] * 2,
        out_specs=vmem(),
        compiler_params=params(),
        cost_estimate=cost(1e6, 4 * math.prod(shape)),
        name="join",
    )(first, second)


def added(slab_ref, p, bins, lead, total):
    slabs, _, wires, _ = slab_ref.shape
    lane = lax.broadcasted_iota(jnp.int32, (wires, LANES), 1)
    none = jnp.zeros((wires, LANES), F32)
    tiles = [none] * (total // LANES)
    for source in range(slabs):
        values = slab_ref[source, p].astype(F32)
        tile, shift = (source * bins - lead) // LANES, (source * bins - lead) % LANES
        if shift:
            values = pltpu.roll(values, shift, 1)
        for t, inside in ((tile, lane >= shift), (tile + 1, lane < shift)):
            if 0 <= t < len(tiles):
                tiles[t] += jnp.where(inside, values, none)
    return [values.astype(BF16) for values in tiles]


def merge_kernel(*refs, bins, lead, planes):
    outs, slab_ref = refs[-planes - 2 : -1], refs[-1]
    total = outs[0].shape[1]
    slab = lax.axis_index("drift")
    for k in range(slab_ref.shape[0]):
        slab_ref[slab ^ k] = refs[k][:planes]
    for p in range(planes):
        for t, values in enumerate(added(slab_ref, p, bins, lead, total)):
            here = slice(t * LANES, (t + 1) * LANES)
            outs[p][:, here] = values
            outs[planes][p, :, here] = values


def merge(arrays, bins, total, before):
    planes, wires, _ = arrays[0].shape
    return pl.pallas_call(
        functools.partial(merge_kernel, bins=bins, lead=WINDOW // 2 - HB, planes=planes),
        out_shape=(jax.ShapeDtypeStruct((wires, total), BF16),) * planes
        + (jax.ShapeDtypeStruct((planes, wires, total), BF16),),
        in_specs=[vmem()] * len(arrays) + [anywhere()],
        out_specs=(vmem(),) * (planes + 1),
        scratch_shapes=[pltpu.VMEM((len(arrays), planes, wires, LANES), BF16)],
        compiler_params=params(),
        cost_estimate=cost(1e8, 4 * planes * wires * total),
        name="merge_bins",
    )(*arrays, before)


def charge_kernel(block_ref, count_ref, *refs, places, order, bins, lead):
    sources, refs = refs[:-12], refs[-12:]
    held_ref, brought_ref, share_ref, signal_ref, out_hbm, signal_hbm = refs[:6]
    all_ref, chosen_ref, out_ref, slab_ref, local_ref, sems = refs[6:]
    cells, planes, entries, wire_block, width = share_ref.shape
    owners, _, wires, total = all_ref.shape
    per_owner = wires // wire_block
    z = lax.axis_index("gz")
    slab = lax.axis_index("drift")
    for i, k in enumerate(order):
        slab_ref[slab ^ k, 0] = held_ref[i]
        slab_ref[slab ^ k ^ 1, 0] = brought_ref[i]
    for t, values in enumerate(added(slab_ref, 0, bins, lead, total)):
        local_ref[:, t * LANES : (t + 1) * LANES] = values
    for (k, p), source in zip(places, sources, strict=True):
        if k is None:
            all_ref[:, p] = source[...]
        elif p is None:
            all_ref[z ^ k] = source[...]
        else:
            all_ref[z ^ k, p] = source[...]
    empty = jnp.zeros((wire_block, total), BF16)
    stores = [pltpu.make_async_copy(signal_ref, signal_hbm, sems.at[cells])]
    stores[0].start()
    for b in range(cells):
        for p in range(planes):
            for k in range(entries):
                name = block_ref[p, k, b]
                if p < planes - 1:
                    name = jnp.clip(name, 0, owners * per_owner - 1)
                    owner = name // per_owner
                    start = pl.multiple_of((name - owner * per_owner) * wire_block, wire_block)
                    rows = all_ref[owner, p, pl.ds(start, wire_block), :]
                else:
                    name = jnp.clip(name - z * per_owner, 0, per_owner - 1)
                    start = pl.multiple_of(name * wire_block, wire_block)
                    rows = local_ref[pl.ds(start, wire_block), :]
                at = (p * entries + k) * wire_block
                chosen_ref[b, at : at + wire_block] = jnp.where(k < count_ref[b, p], rows, empty)
        here = slice(b * width, (b + 1) * width)
        out_ref[here] = lax.dot_general(
            share_ref[b].reshape(planes * entries * wire_block, width),
            chosen_ref[b],
            (((0,), (0,)), ((), ())),
            preferred_element_type=F32,
        ).astype(BF16)
        store = pltpu.make_async_copy(out_ref.at[here], out_hbm.at[here], sems.at[b])
        store.start()
        stores.append(store)
    for store in stores:
        store.wait()


def charge_gradient(
    ovl_block, ovl_count, sources, places, ends, order, intersection, owners, signal, bins, total
):
    cells, planes, entries, wire_block, width = intersection.shape
    wires = ends[0].shape[1]
    shape = (owners, planes - 1, wires, total)
    return pl.pallas_call(
        functools.partial(
            charge_kernel, places=places, order=order, bins=bins, lead=WINDOW // 2 - HB
        ),
        out_shape=(
            jax.ShapeDtypeStruct((cells * width, total), BF16),
            jax.ShapeDtypeStruct(signal.shape, BF16),
        ),
        in_specs=[smem(), smem()] + [vmem()] * (len(sources) + 4),
        out_specs=(anywhere(), anywhere()),
        scratch_shapes=[
            pltpu.VMEM(shape, BF16),
            pltpu.VMEM((cells, planes * entries * wire_block, total), BF16),
            pltpu.VMEM((cells * width, total), BF16),
            pltpu.VMEM((2 * len(order), 1, wires, LANES), BF16),
            pltpu.VMEM((wires, total), BF16),
            pltpu.SemaphoreType.DMA((cells + 1,)),
        ],
        compiler_params=params(),
        cost_estimate=cost(1e8, 2 * math.prod(shape)),
        name="charge_gradient",
    )(jnp.transpose(ovl_block, (1, 2, 0)), ovl_count, *sources, *ends, intersection, signal)


def pieces_kernel(
    block_hbm, count_hbm, charge_hbm, share_hbm, cot_hbm, own_hbm, keep_hbm, give_hbm, local_hbm,
    block_ref, count_ref, charge_ref, share_ref, edge_ref, cross_ref, own_ref, keep_ref, give_ref, local_ref,
    sems, out_sems, *, half,
):
    cells, planes, entries, wire_block, width = share_ref.shape
    wires, total = local_ref.shape
    ticks = edge_ref.shape[3]
    per_owner = wires // wire_block
    cut = own_ref.shape[0]
    halves = 1 + keep_ref.shape[0]
    owners = 2 * halves
    z = lax.axis_index("gz")
    loads = [
        pltpu.make_async_copy(source, target, sems.at[i])
        for i, (source, target) in enumerate(
            (
                (block_hbm, block_ref),
                (count_hbm, count_ref),
                (charge_hbm, charge_ref),
                (share_hbm, share_ref),
                (cot_hbm.at[:, :EDGE], edge_ref.at[0]),
                (cot_hbm.at[:, wires - EDGE :], edge_ref.at[1]),
            )
        )
    ]
    for load in loads:
        load.start()
    cross_ref[...] = jnp.zeros(cross_ref.shape, F32)
    local_ref[...] = jnp.zeros(local_ref.shape, F32)
    for load in loads[:4]:
        load.wait()
    for b in range(cells):
        pieces = (
            jnp.dot(
                share_ref[b].reshape(planes * entries * wire_block, width),
                charge_ref[b * width : (b + 1) * width],
                preferred_element_type=F32,
            )
            .astype(BF16)
            .astype(F32)
        )
        for p in range(planes):
            for k in range(entries):
                at = (p * entries + k) * wire_block
                piece = pieces[at : at + wire_block]
                piece = jnp.where(k < count_ref[b, p], piece, jnp.zeros_like(piece))
                name = block_ref[p, k, b]
                if p < planes - 1:
                    name = jnp.clip(name, 0, owners * per_owner - 1)
                    start = pl.multiple_of(EDGE + name * wire_block, EDGE)
                    cross_ref[p, pl.ds(start, wire_block)] += piece
                else:
                    name = jnp.clip(name - z * per_owner, 0, per_owner - 1)
                    start = pl.multiple_of(name * wire_block, wire_block)
                    local_ref[pl.ds(start, wire_block)] += piece
    for load in loads[4:]:
        load.wait()
    at = halves * cut
    gap = jnp.zeros((sixteens(planes * half) - planes * half, ticks), F32)
    for side, first in ((0, 0), (1, EDGE - half)):
        rows = [edge_ref[side, p].astype(F32)[first : first + half] for p in range(planes)]
        rows = jnp.concatenate(rows + [gap], axis=0).astype(BF16)
        for part in range(ticks // total):
            give_ref[at : at + rows.shape[0]] = rows[:, part * total : (part + 1) * total]
            at += rows.shape[0]
    extent = wires + 2 * EDGE
    none = jnp.zeros((half, total), F32)
    stores = [
        pltpu.make_async_copy(source, target, out_sems.at[i])
        for i, (source, target) in enumerate(
            (
                (give_ref, give_hbm),
                (keep_ref, keep_hbm),
                (own_ref, own_hbm),
                (local_ref, local_hbm),
            )
        )
    ]
    stores[3].start()
    for k in [*range(1, owners, 2), *range(2, owners, 2), 0]:
        to = z ^ k
        blocks = []
        for p in range(planes - 1):
            rows = cross_ref[p, pl.ds(pl.multiple_of(to * wires, EDGE), extent)]
            blocks.append(rows[EDGE - half : extent - EDGE + half])
        blocks.append(jnp.where(to == z + 1, local_ref[wires - half :], none))
        blocks.append(jnp.where(to == z - 1, local_ref[:half], none))
        rows = padded(blocks)
        if k % 2:
            give_ref[k // 2 * cut : (k // 2 + 1) * cut] = coded(rows, 0)
        elif k:
            keep_ref[k // 2 - 1] = coded(rows, 0)
        else:
            own_ref[...] = rows
        if k == owners - 1:
            stores[0].start()
        if k == owners - 2 and k:
            stores[1].start()
    if owners == 2:
        stores[1].start()
    stores[2].start()
    for store in stores:
        store.wait()


def sixteens(rows):
    return -(-rows // 16) * 16


def padded(blocks):
    count = sum(block.shape[0] for block in blocks)
    if count % 16:
        blocks = blocks + [jnp.zeros((sixteens(count) - count, blocks[0].shape[1]), F32)]
    return jnp.concatenate(blocks, axis=0)


def cut_pieces(ovl_block, ovl_count, charge, intersection, cotangent, owners, half):
    cells, planes, entries, wire_block, width = intersection.shape
    total = charge.shape[1]
    _, wires, ticks = cotangent.shape
    rows = sixteens((planes - 1) * (wires + 2 * half) + 2 * half)
    edges = 2 * sixteens(planes * half) * ticks // total
    hbm = pl.BlockSpec(memory_space=pltpu.HBM)
    blocks = jnp.transpose(ovl_block, (1, 2, 0))
    outs = (
        jax.ShapeDtypeStruct((rows, total), F32),
        jax.ShapeDtypeStruct((owners // 2 - 1, rows, total), BF16),
        jax.ShapeDtypeStruct((owners // 2 * rows + edges, total), BF16),
        jax.ShapeDtypeStruct((wires, total), F32),
    )
    return pl.pallas_call(
        functools.partial(pieces_kernel, half=half),
        out_shape=outs,
        in_specs=[hbm] * 5,
        out_specs=(hbm,) * 4,
        scratch_shapes=[
            pltpu.SMEM(blocks.shape, jnp.int32),
            pltpu.SMEM(ovl_count.shape, jnp.int32),
            pltpu.VMEM(charge.shape, BF16),
            pltpu.VMEM(intersection.shape, BF16),
            pltpu.VMEM((2, planes, EDGE, ticks), BF16),
            pltpu.VMEM((planes - 1, owners * wires + 2 * EDGE, total), F32),
            *[pltpu.VMEM(out.shape, out.dtype) for out in outs],
            pltpu.SemaphoreType.DMA((6,)),
            pltpu.SemaphoreType.DMA((4,)),
        ],
        compiler_params=params(limit=WHOLE_VMEM),
        cost_estimate=cost(1e8, 4 * owners * rows * total),
        name="pieces",
    )(blocks, ovl_count, charge, intersection, cotangent)


def relay_kernel(keep_ref, received_ref, *outs):
    others, rows, _ = keep_ref.shape
    edges = (received_ref.shape[0] - (others + 1) * rows) // 2
    z = lax.axis_index("gz")
    even = lax.rem(z, 2) == 0
    low = received_ref[(others + 1) * rows : (others + 1) * rows + edges]
    high = received_ref[(others + 1) * rows + edges :]
    for j in range(others):
        to = z ^ (2 * (j + 1))
        summed = plain(keep_ref[j], True)
        summed += plain(received_ref[(j + 1) * rows : (j + 2) * rows], True)
        outs[j][...] = coded(summed, 0)
        upward, downward = even & (to == z + 2), jnp.logical_not(even) & (to == z - 2)
        outs[others + j][...] = jnp.where(
            upward, high, jnp.where(downward, low, jnp.zeros_like(low))
        )


def relay(keep, received):
    others, rows, total = keep.shape
    edges = (received.shape[0] - (others + 1) * rows) // 2
    outs = pl.pallas_call(
        relay_kernel,
        out_shape=(jax.ShapeDtypeStruct((rows, total), BF16),) * others
        + (jax.ShapeDtypeStruct((edges, total), BF16),) * others,
        in_specs=[vmem(), vmem()],
        out_specs=(vmem(),) * (2 * others),
        compiler_params=params(),
        cost_estimate=cost(1e7, 6 * others * rows * total),
        name="relay",
    )(keep, received)
    return outs[:others], outs[others:]


def slabs_kernel(*refs, bins, lead, slabs, cross, half):
    count = len(refs) - slabs.bit_length() - 1
    keep_ref, received_ref, others, local_ref = refs[0], refs[1], refs[2 : count - 2], refs[count - 2]
    outs, cut_ref = refs[count:-1], refs[-1]
    total = local_ref.shape[1]
    cut = keep_ref.shape[0]
    summed = keep_ref[...] + plain(received_ref[:cut], True)
    for other in others:
        summed += plain(other[...], True)
    wires = local_ref.shape[0]
    edge = cross * (wires + 2 * half)
    rows = padded([summed[: edge + half], local_ref[...], summed[edge + half : edge + 2 * half]])
    none = jnp.zeros((rows.shape[0], LANES), F32)
    lane = lax.broadcasted_iota(jnp.int32, none.shape, 1)
    level = jnp.broadcast_to(rows[:, :1].astype(BF16).astype(F32), none.shape)
    tiles = [rows[:, t * LANES : (t + 1) * LANES] - level for t in range(total // LANES)]
    for to in range(slabs):
        at = to * bins - lead
        tile, shift = at // LANES, at % LANES
        pair = [tiles[t] if 0 <= t < len(tiles) else -level for t in (tile, tile + 1)]
        value = shared_lanes(pair[0], pair[1], shift, lane)
        cut_ref[to] = jnp.where(lane == 0, level, value).astype(BF16)
    slab = lax.axis_index("drift")
    outs[0][...] = cut_ref[slab]
    size = rows.shape[0]
    for s, out in enumerate(outs[1:]):
        for i in range(slabs >> (s + 1)):
            out[i * size : (i + 1) * size] = cut_ref[slab ^ ((2 * i + 1) << s)]


def cut_slabs(keep, received, others, local, bins, slabs, cross, half, before):
    wires, total = local.shape
    rows = sixteens((cross + 1) * (wires + 2 * half))
    steps = slabs.bit_length() - 1
    counts = [1] + [slabs >> (s + 1) for s in range(steps)]
    return pl.pallas_call(
        functools.partial(
            slabs_kernel, bins=bins, lead=WINDOW // 2 - HB, slabs=slabs, cross=cross, half=half
        ),
        out_shape=tuple(jax.ShapeDtypeStruct((n * rows, LANES), BF16) for n in counts),
        in_specs=[vmem()] * (3 + len(others)) + [anywhere()],
        out_specs=(vmem(),) * len(counts),
        scratch_shapes=[pltpu.VMEM((slabs, rows, LANES), BF16)],
        compiler_params=params(),
        cost_estimate=cost(1e8, 4 * rows * total),
        name="slab_currents",
    )(keep, received, *others, local, before)


def pass_kernel(*refs, step, size):
    own_ref, arrived, out_ref = refs[0], refs[1:-1], refs[-1]
    for i in range(own_ref.shape[0] // size):
        here = slice(i * size, (i + 1) * size)
        total = plain(own_ref[here], False)
        for r, other in enumerate(arrived):
            at = ((2 * i + 1) << step) >> (r + 1)
            total += plain(other[at * size : (at + 1) * size], False)
        out_ref[here] = coded(total, WINDOW // 2)


def pass_on(own, arrived, step, size):
    return pl.pallas_call(
        functools.partial(pass_kernel, step=step, size=size),
        out_shape=jax.ShapeDtypeStruct(own.shape, BF16),
        in_specs=[vmem()] * (1 + len(arrived)),
        out_specs=vmem(),
        compiler_params=params(),
        cost_estimate=cost(1e6, 4 * math.prod(own.shape)),
        name="pass_on",
    )(own, *arrived)


def signal_kernel(*refs, wire_taps):
    parts, (table_ref, out_ref, even_ref, odd_ref, level_ref, lines_ref) = refs[:-6], refs[-6:]
    planes, blocks, _, span = table_ref.shape
    _, wires, _ = out_ref.shape
    half = (wire_taps - 1) // 2
    extent = wires + 2 * half
    step = span * 16 // LANES
    middle = WINDOW // 2
    lane = lax.broadcasted_iota(jnp.int32, (wires, LANES), 1)
    size = parts[0].shape[0]
    summed = plain(parts[0][...], False)
    for part in parts[1:]:
        summed += plain(part[:size], False)
    for p in range(planes):
        currents = summed[p * extent : (p + 1) * extent]
        level = currents[:, middle : middle + 1].astype(BF16).astype(F32)
        level = jnp.broadcast_to(level, currents.shape)
        level_ref[p] = level
        currents = currents - level
        levels = jnp.zeros((wires, LANES), F32)
        for a in range(wire_taps):
            at = a
            both = (lane == WINDOW + a) | (lane == WINDOW + wire_taps + a)
            levels = jnp.where(both, level_ref[p, at : at + wires], levels)
        for block in range(blocks):
            i = p * blocks + block
            even_ref[i] = pltpu.roll(currents, (-step * block) % LANES, 1)
            odd_ref[i] = pltpu.roll(currents, (WINDOW - step * block) % LANES, 1)
            for pair in range((wire_taps + 1) // 2):
                at = 2 * pair
                right = levels
                if 2 * pair + 1 < wire_taps:
                    right = odd_ref[i, at + 1 : at + 1 + wires]
                line = jnp.where(lane < WINDOW, even_ref[i, at : at + wires], right)
                lines_ref[i % 2, :, pair * LANES : (pair + 1) * LANES] = line.astype(BF16)
            out_ref[p, :, block * span : (block + 1) * span] = jnp.dot(
                lines_ref[i % 2], table_ref[p, block], preferred_element_type=F32
            ).astype(BF16)


def forward(parts, table, wires, wire_taps):
    planes, blocks, depth, span = table.shape
    extent = wires + wire_taps - 1
    shape = (planes, wires, blocks * span)
    return pl.pallas_call(
        functools.partial(signal_kernel, wire_taps=wire_taps),
        out_shape=jax.ShapeDtypeStruct(shape, BF16),
        in_specs=[vmem()] * (len(parts) + 1),
        out_specs=vmem(),
        scratch_shapes=[
            pltpu.VMEM((planes * blocks, extent, LANES), F32),
            pltpu.VMEM((planes * blocks, extent, LANES), F32),
            pltpu.VMEM((planes, extent, LANES), F32),
            pltpu.VMEM((2, wires, depth), BF16),
        ],
        compiler_params=params(),
        cost_estimate=cost(4e9, 2 * math.prod(table.shape)),
        name="signal",
    )(*parts, table)


def local(charge, intersection, ovl_block, ovl_count, diff_class, response, cotangent):
    total = charge.shape[1]
    owners = lax.axis_size("gz")
    slabs = lax.axis_size("drift")
    planes, wires, ticks = cotangent.shape
    wire_taps = response.shape[1]
    half = (wire_taps - 1) // 2
    bins = total // slabs

    currents, keep, give, local_currents = cut_pieces(
        ovl_block, ovl_count, charge, intersection, cotangent, owners, half
    )
    received = swap(give, "gz", 1)
    sums, edges = relay(keep.astype(F32), received) if owners > 2 else ((), ())
    beyond = [swap(block, "gz", 2 * j) for j, block in enumerate(edges, 1)]
    others = [swap(block, "gz", 2 * j) for j, block in enumerate(sums, 1)]

    levels, kinds = smeared_levels(
        diff_class, response, bins, slabs, sums[0] if sums else received
    )
    table = build_table(levels, kinds, planes, wire_taps, ticks)
    partial, crossing = backward(table, cotangent, received, beyond, wire_taps)
    distance = slabs // 2
    spread = [crossing] + [
        swap(partial if k == distance else crossing, "drift", k) for k in range(1, slabs)
    ]
    held, order = join(partial, spread[distance], 1), [0, distance]
    distance //= 2
    while distance > 1:
        held = join(held, swap(held, "drift", distance), len(order))
        order += [k ^ distance for k in order]
        distance //= 2
    ends = [held, swap(held, "drift", 1)]

    cuts = cut_slabs(
        currents, received, others, local_currents, bins, slabs, planes - 1, half, partial
    )
    windows, ready = [cuts[0]], cuts[0]
    for step, block in enumerate(cuts[1:]):
        if step:
            block = ready = pass_on(block, windows[1:], step, cuts[0].shape[0])
        windows.append(swap(block, "drift", 1 << step))

    count = planes - 1
    *cross, both = merge(spread, bins, total, ready)
    if owners == 4:
        across = [swap(block, "gz", 2) for block in cross]
        sources = [both, swap(both, "gz", 1), *across, *(swap(block, "gz", 1) for block in across)]
        places = [(0, None), (1, None)]
        places += [(2, p) for p in range(count)] + [(3, p) for p in range(count)]
    else:
        sources = [lax.all_gather(block, "gz", axis=0) for block in cross]
        places = [(None, p) for p in range(count)]
    signal = forward(windows, table, wires, wire_taps)
    charge_grad, signal = charge_gradient(
        ovl_block, ovl_count, sources, places, ends, order, intersection, owners, signal, bins, total
    )
    return signal, charge_grad


def solution(mesh):
    return jax.shard_map(
        local,
        mesh=mesh,
        in_specs=(
            P(("apa", "gz", "drift"), None),
            P(("apa", "gz", "drift"), None, None, None, None),
            P(("apa", "gz", "drift"), None, None),
            P(("apa", "gz", "drift"), None),
            P("apa"),
            P(),
            P("apa", "gz", "drift"),
        ),
        out_specs=(P("apa", "gz", "drift"), P(("apa", "gz", "drift"), None)),
        check_vma=False,
    )
```

```python
import functools
import math

import jax
import jax.numpy as jnp
from jax import lax
from jax.experimental import pallas as pl
from jax.experimental.pallas import tpu as pltpu
from jax.sharding import PartitionSpec as P

TPB = 8
HB = 2
CLASSES = 6
LANES = 128
EDGE = 16
GROUP = 8
WINDOW = 64
LEAD = HB * TPB - TPB // 2
VMEM_LIMIT = 24 * 1024 * 1024
WHOLE_VMEM = 61 * 1024 * 1024
BF16 = jnp.bfloat16
F32 = jnp.float32


def params(semantics=None, limit=VMEM_LIMIT):
    return pltpu.CompilerParams(vmem_limit_bytes=limit, dimension_semantics=semantics)


def vmem():
    return pl.BlockSpec(memory_space=pltpu.VMEM)


def smem():
    return pl.BlockSpec(memory_space=pltpu.SMEM)


def anywhere():
    return pl.BlockSpec(memory_space=pl.ANY)


def cost(flops, moved):
    return pl.CostEstimate(flops=int(flops), bytes_accessed=int(moved), transcendentals=0)


def swap(block, axis, distance):
    count = lax.axis_size(axis)
    return lax.ppermute(block, axis, [(i, i ^ distance) for i in range(count)])


def widths(number):
    spread = TPB * (0.2 + 0.15 * number)
    half = HB * TPB
    total = sum(math.exp(-((j + 0.5) ** 2) / (2.0 * spread * spread)) for j in range(-half, half))
    return 1.0 / (2.0 * spread * spread), 1.0 / total


def shared_lanes(left, right, shift, lane):
    if shift == 0:
        return left
    back = LANES - shift
    return jnp.where(lane < back, pltpu.roll(left, back, 1), pltpu.roll(right, back, 1))


def coded(rows, column):
    lane = lax.broadcasted_iota(jnp.int32, rows.shape, 1)
    level = jnp.broadcast_to(rows[:, column : column + 1].astype(BF16).astype(F32), rows.shape)
    return jnp.where(lane == 0, level, rows - level).astype(BF16)


def plain(rows, first):
    rows = rows.astype(F32)
    lane = lax.broadcasted_iota(jnp.int32, rows.shape, 1)
    level = jnp.broadcast_to(rows[:, :1], rows.shape)
    return jnp.where(lane == 0, level if first else jnp.zeros_like(rows), rows + level)


def levels_kernel(
    class_ref, response_ref, _, level_ref, kind_ref, flat_ref, *, bins, slabs, total
):
    planes, wire_taps, length = response_ref.shape
    rows = level_ref.shape[0] // planes
    groups = kind_ref.shape[0]
    slab = lax.axis_index("drift")
    lane = lax.broadcasted_iota(jnp.int32, (GROUP, LANES), 1)
    packed = class_ref[...].astype(F32)
    tiles = []
    for t in range(total // LANES):
        at = slice(t % 2 * LANES, (t % 2 + 1) * LANES)
        tiles.append(jnp.broadcast_to(packed[t // 2 : t // 2 + 1, at], (GROUP, LANES)))
    classes = tiles[0]
    none = jnp.zeros((GROUP, LANES), F32)
    numbers = none
    for source in range(slabs):
        at = source * bins - (WINDOW // 2 - HB)
        tile, shift = at // LANES, at % LANES
        pair = [tiles[t] if 0 <= t < len(tiles) else none for t in (tile, tile + 1)]
        numbers = jnp.where(slab == source, shared_lanes(pair[0], pair[1], shift, lane), numbers)
    x = slab * bins - (WINDOW // 2 - HB) + lane
    numbers = jnp.where((x >= 0) & (x < HB), (CLASSES + x).astype(F32), numbers)
    column = jnp.broadcast_to(numbers[:1], (LANES, LANES)).T.astype(jnp.int32)
    for m in range(groups):
        kind_ref[m] = column[m * GROUP : (m + 1) * GROUP]
    flat_ref[...] = jnp.zeros(flat_ref.shape, F32)
    for p in range(planes):
        flat_ref[p * rows : p * rows + wire_taps, :length] = response_ref[p].astype(F32)
    taps = flat_ref[...].astype(BF16)
    tap = lax.broadcasted_iota(jnp.int32, (LANES, 2 * LANES), 0)
    tick = lax.broadcasted_iota(jnp.int32, (LANES, 2 * LANES), 1)
    step = tick - tap - LEAD
    offset = step.astype(F32) - (TPB - 1) / 2.0
    squared = offset * offset
    inside = jnp.abs(offset) < HB * TPB
    for kind in range(CLASSES + HB):
        keep = inside
        if kind < CLASSES:
            narrow, scale = widths(kind)
        else:
            edge = kind - CLASSES
            narrow, scale = widths(0)
            for number in range(1, CLASSES):
                chosen = classes[:1, edge : edge + 1] == number
                narrow = jnp.where(chosen, widths(number)[0], narrow)
                scale = jnp.where(chosen, widths(number)[1], scale)
            keep = inside & (step >= -TPB * edge)
        smear = jnp.where(keep, jnp.exp(-(squared * narrow)) * scale, 0.0)
        high = smear.astype(BF16)
        low = (smear - high.astype(F32)).astype(BF16)
        near = jnp.dot(taps[:, :LANES], high, preferred_element_type=F32) + jnp.dot(
            taps[:, :LANES], low, preferred_element_type=F32
        )
        far = jnp.dot(taps[:, LANES:], high[:, :LANES], preferred_element_type=F32) + jnp.dot(
            taps[:, LANES:], low[:, :LANES], preferred_element_type=F32
        )
        level_ref[:, kind, :LANES] = near[:, :LANES]
        level_ref[:, kind, LANES:] = near[:, LANES:] + far


def smeared_levels(diff_class, response, bins, slabs, before):
    planes, wire_taps, _ = response.shape
    total = diff_class.shape[0]
    reach = 2 * LANES
    rows = -(-wire_taps // 8) * 8
    groups = (bins + WINDOW // 2) // GROUP
    classes = jnp.pad(diff_class.astype(BF16), (0, 8 * reach - total)).reshape(8, reach)
    return pl.pallas_call(
        functools.partial(levels_kernel, bins=bins, slabs=slabs, total=total),
        out_shape=(
            jax.ShapeDtypeStruct((planes * rows, CLASSES + HB, reach), F32),
            jax.ShapeDtypeStruct((groups, GROUP, LANES), jnp.int32),
        ),
        in_specs=[vmem(), vmem(), anywhere()],
        out_specs=(vmem(), vmem()),
        scratch_shapes=[pltpu.VMEM((planes * rows, reach), F32)],
        compiler_params=params(),
        cost_estimate=cost(1e8, 1e6),
        name="levels",
    )(classes, response, before)


def table_kernel(level_ref, kind_ref, table_ref, sum_ref, *, wire_taps):
    planes, blocks, depth, span = table_ref.shape
    rows = level_ref.shape[0] // planes
    groups = kind_ref.shape[0]
    tiles = span // LANES
    lane = lax.broadcasted_iota(jnp.int32, (GROUP, LANES), 1)
    row = lax.broadcasted_iota(jnp.int32, (GROUP, LANES), 0)
    starts = [LEAD_SHIFT + odd * (LANES // 2) + TPB * row for odd in range(2)]
    after = [lane >= start for start in starts]
    zero = jnp.zeros((GROUP, LANES), F32)
    empty = jnp.zeros((2 * GROUP, LANES), BF16)

    def body(a, plane):
        levels = level_ref[plane * rows + a]
        halves = [levels[:, :LANES], levels[:, LANES:]]
        pieces = []
        for m in range(groups):
            odd = m % 2
            parts = [
                pltpu.roll(
                    jnp.take_along_axis(half, kind_ref[m], axis=0),
                    LEAD_SHIFT + odd * (LANES // 2),
                    1,
                    stride=TPB,
                    stride_axis=0,
                )
                for half in halves
            ]
            pieces.append(
                (
                    jnp.where(after[odd], parts[0], zero),
                    jnp.where(after[odd], parts[1], parts[0]),
                    jnp.where(after[odd], zero, parts[1]),
                )
            )
        for block in range(blocks):
            for tile in range(tiles):
                here = slice(tile * LANES, (tile + 1) * LANES)
                total = zero
                for quarter in range(WINDOW // (2 * GROUP)):
                    m = 2 * (tiles * block + quarter)
                    at = a * WINDOW + quarter * 2 * GROUP
                    at = pl.ds(pl.multiple_of(at, 2 * GROUP), 2 * GROUP)
                    third = tile - quarter + 2
                    value = empty
                    if 0 <= third <= 2 and m + 1 < groups:
                        value = jnp.concatenate(
                            [pieces[m][third], pieces[m + 1][third]], axis=0
                        ).astype(BF16)
                        total = total + pieces[m][third] + pieces[m + 1][third]
                    table_ref[plane, block, at, here] = value
                sum_ref[a, block, :, here] = total
        return plane

    def whole_plane(plane, _):
        lax.fori_loop(0, wire_taps, body, plane, unroll=UNROLL)
        for block in range(blocks):
            total = jnp.sum(sum_ref[:, block], axis=1)
            high = total.astype(BF16).astype(F32)
            spare = jnp.zeros((depth - (WINDOW + 2) * wire_taps, span), F32)
            table_ref[plane, block, wire_taps * WINDOW :, :] = jnp.concatenate(
                [high, total - high, spare], axis=0
            ).astype(BF16)
        return 0

    lax.fori_loop(0, planes, whole_plane, 0)


UNROLL = 7
LEAD_SHIFT = (TPB * HB - LEAD) % LANES


def build_table(levels, kinds, planes, wire_taps, ticks_here):
    tiles = math.gcd(ticks_here, 2 * LANES) // LANES
    blocks = ticks_here // (tiles * LANES)
    shape = (planes, blocks, (wire_taps + 1) * WINDOW, tiles * LANES)
    return pl.pallas_call(
        functools.partial(table_kernel, wire_taps=wire_taps),
        out_shape=jax.ShapeDtypeStruct(shape, BF16),
        in_specs=[vmem(), vmem()],
        out_specs=vmem(),
        scratch_shapes=[pltpu.VMEM((wire_taps, blocks, GROUP, tiles * LANES), F32)],
        compiler_params=params(),
        cost_estimate=cost(4e9, 2 * math.prod(shape)),
        name="table",
    )(levels, kinds)


def back_kernel(table_ref, own_ref, received_ref, *refs, wire_taps):
    others, (out_ref, cross_ref, cot_ref, wide_ref) = refs[:-4], refs[-4:]
    planes, blocks, _, span = table_ref.shape
    _, wires, ticks = own_ref.shape
    total = received_ref.shape[1]
    half = (wire_taps - 1) // 2
    parts = ticks // total
    size = sixteens(planes * half)
    side = parts * size
    lows = received_ref.shape[0] - 2 * side
    even = lax.rem(lax.axis_index("gz"), 2) == 0
    lane = lax.broadcasted_iota(jnp.int32, (wires, LANES), 1)
    none = jnp.zeros((wires, LANES), F32)
    gap = jnp.zeros((EDGE - half, total), F32)
    step = span * 16 // LANES
    columns = (wire_taps + 1) // 2
    edges = []
    for part in range(parts):
        low = received_ref[lows + part * size : lows + (part + 1) * size].astype(F32)
        high = received_ref[lows + side + part * size : lows + side + (part + 1) * size].astype(F32)
        near = jnp.where(even, low, high)
        far = jnp.zeros((size, total), F32)
        for other in others:
            far += other[part * size : (part + 1) * size].astype(F32)
        edges.append((jnp.where(even, far, near), jnp.where(even, near, far)))
    for plane in range(planes):
        cot_ref[plane, EDGE : EDGE + wires] = own_ref[plane]
        for part in range(parts):
            here = slice(part * total, (part + 1) * total)
            before, after = [edge[plane * half : (plane + 1) * half] for edge in edges[part]]
            cot_ref[plane, :EDGE, here] = jnp.concatenate([gap, before], axis=0).astype(BF16)
            cot_ref[plane, EDGE + wires :, here] = jnp.concatenate([after, gap], axis=0).astype(BF16)
        result = none
        for block in range(blocks):
            i = (plane * blocks + block) % wide_ref.shape[0]
            wide = lax.dot_general(
                cot_ref[plane, :, block * span : (block + 1) * span],
                table_ref[plane, block, : columns * LANES],
                (((1,), (1,)), ((), ())),
                preferred_element_type=F32,
            )
            for column in range(columns):
                wide_ref[i, column] = wide[:, column * LANES : (column + 1) * LANES]
            left, right = none, none
            for column in range(columns):
                at = EDGE + half - 2 * column
                left += wide_ref[i, column, at : at + wires]
                if 2 * column + 1 < wire_taps:
                    right += wide_ref[i, column, at - 1 : at - 1 + wires]
            both = jnp.where(lane < WINDOW, left + pltpu.roll(right, WINDOW, 1), none)
            result += pltpu.roll(both, block * step, 1) if block else both
        out_ref[plane] = result.astype(BF16)
        if plane < planes - 1:
            cross_ref[plane] = result.astype(BF16)


def backward(table, cotangent, received, others, wire_taps):
    planes, _, _, _ = table.shape
    _, wires, ticks = cotangent.shape
    extent = wires + 2 * EDGE
    columns = (wire_taps + 1) // 2
    return pl.pallas_call(
        functools.partial(back_kernel, wire_taps=wire_taps),
        out_shape=(
            jax.ShapeDtypeStruct((planes, wires, LANES), BF16),
            jax.ShapeDtypeStruct((planes - 1, wires, LANES), BF16),
        ),
        in_specs=[vmem()] * (3 + len(others)),
        out_specs=(vmem(), vmem()),
        scratch_shapes=[
            pltpu.VMEM((planes, extent, ticks), BF16),
            pltpu.VMEM((2, columns, extent, LANES), F32),
        ],
        compiler_params=params(),
        cost_estimate=cost(4e9, 2 * math.prod(table.shape)),
        name="bin_gradients",
    )(table, cotangent, received, *others)


def join_kernel(first_ref, second_ref, out_ref):
    count = out_ref.shape[0] // 2
    out_ref[:count] = first_ref[first_ref.shape[0] - count :]
    out_ref[count:] = second_ref[second_ref.shape[0] - count :]


def join(first, second, count):
    shape = (2 * count,) + first.shape[1:]
    return pl.pallas_call(
        join_kernel,
        out_shape=jax.ShapeDtypeStruct(shape, BF16),
        in_specs=[vmem()] * 2,
        out_specs=vmem(),
        compiler_params=params(),
        cost_estimate=cost(1e6, 4 * math.prod(shape)),
        name="join",
    )(first, second)


def added(slab_ref, p, bins, lead, total):
    slabs, _, wires, _ = slab_ref.shape
    lane = lax.broadcasted_iota(jnp.int32, (wires, LANES), 1)
    none = jnp.zeros((wires, LANES), F32)
    tiles = [none] * (total // LANES)
    for source in range(slabs):
        values = slab_ref[source, p].astype(F32)
        tile, shift = (source * bins - lead) // LANES, (source * bins - lead) % LANES
        if shift:
            values = pltpu.roll(values, shift, 1)
        for t, inside in ((tile, lane >= shift), (tile + 1, lane < shift)):
            if 0 <= t < len(tiles):
                tiles[t] += jnp.where(inside, values, none)
    return [values.astype(BF16) for values in tiles]


def merge_kernel(*refs, bins, lead, planes):
    outs, slab_ref = refs[-planes - 2 : -1], refs[-1]
    total = outs[0].shape[1]
    slab = lax.axis_index("drift")
    for k in range(slab_ref.shape[0]):
        slab_ref[slab ^ k] = refs[k][:planes]
    for p in range(planes):
        for t, values in enumerate(added(slab_ref, p, bins, lead, total)):
            here = slice(t * LANES, (t + 1) * LANES)
            outs[p][:, here] = values
            outs[planes][p, :, here] = values


def merge(arrays, bins, total, before):
    planes, wires, _ = arrays[0].shape
    return pl.pallas_call(
        functools.partial(merge_kernel, bins=bins, lead=WINDOW // 2 - HB, planes=planes),
        out_shape=(jax.ShapeDtypeStruct((wires, total), BF16),) * planes
        + (jax.ShapeDtypeStruct((planes, wires, total), BF16),),
        in_specs=[vmem()] * len(arrays) + [anywhere()],
        out_specs=(vmem(),) * (planes + 1),
        scratch_shapes=[pltpu.VMEM((len(arrays), planes, wires, LANES), BF16)],
        compiler_params=params(),
        cost_estimate=cost(1e8, 4 * planes * wires * total),
        name="merge_bins",
    )(*arrays, before)


def charge_kernel(block_ref, count_ref, *refs, places, order, bins, lead):
    sources, refs = refs[:-12], refs[-12:]
    held_ref, brought_ref, share_ref, signal_ref, out_hbm, signal_hbm = refs[:6]
    all_ref, chosen_ref, out_ref, slab_ref, local_ref, sems = refs[6:]
    cells, planes, entries, wire_block, width = share_ref.shape
    owners, _, wires, total = all_ref.shape
    per_owner = wires // wire_block
    z = lax.axis_index("gz")
    slab = lax.axis_index("drift")
    for i, k in enumerate(order):
        slab_ref[slab ^ k, 0] = held_ref[i]
        slab_ref[slab ^ k ^ 1, 0] = brought_ref[i]
    for t, values in enumerate(added(slab_ref, 0, bins, lead, total)):
        local_ref[:, t * LANES : (t + 1) * LANES] = values
    for (k, p), source in zip(places, sources, strict=True):
        if k is None:
            all_ref[:, p] = source[...]
        elif p is None:
            all_ref[z ^ k] = source[...]
        else:
            all_ref[z ^ k, p] = source[...]
    empty = jnp.zeros((wire_block, total), BF16)
    stores = [pltpu.make_async_copy(signal_ref, signal_hbm, sems.at[cells])]
    stores[0].start()
    for b in range(cells):
        for p in range(planes):
            for k in range(entries):
                name = block_ref[p, k, b]
                if p < planes - 1:
                    name = jnp.clip(name, 0, owners * per_owner - 1)
                    owner = name // per_owner
                    start = pl.multiple_of((name - owner * per_owner) * wire_block, wire_block)
                    rows = all_ref[owner, p, pl.ds(start, wire_block), :]
                else:
                    name = jnp.clip(name - z * per_owner, 0, per_owner - 1)
                    start = pl.multiple_of(name * wire_block, wire_block)
                    rows = local_ref[pl.ds(start, wire_block), :]
                at = (p * entries + k) * wire_block
                chosen_ref[b, at : at + wire_block] = jnp.where(k < count_ref[b, p], rows, empty)
        here = slice(b * width, (b + 1) * width)
        out_ref[here] = lax.dot_general(
            share_ref[b].reshape(planes * entries * wire_block, width),
            chosen_ref[b],
            (((0,), (0,)), ((), ())),
            preferred_element_type=F32,
        ).astype(BF16)
        store = pltpu.make_async_copy(out_ref.at[here], out_hbm.at[here], sems.at[b])
        store.start()
        stores.append(store)
    for store in stores:
        store.wait()


def charge_gradient(
    ovl_block, ovl_count, sources, places, ends, order, intersection, owners, signal, bins, total
):
    cells, planes, entries, wire_block, width = intersection.shape
    wires = ends[0].shape[1]
    shape = (owners, planes - 1, wires, total)
    return pl.pallas_call(
        functools.partial(
            charge_kernel, places=places, order=order, bins=bins, lead=WINDOW // 2 - HB
        ),
        out_shape=(
            jax.ShapeDtypeStruct((cells * width, total), BF16),
            jax.ShapeDtypeStruct(signal.shape, BF16),
        ),
        in_specs=[smem(), smem()] + [vmem()] * (len(sources) + 4),
        out_specs=(anywhere(), anywhere()),
        scratch_shapes=[
            pltpu.VMEM(shape, BF16),
            pltpu.VMEM((cells, planes * entries * wire_block, total), BF16),
            pltpu.VMEM((cells * width, total), BF16),
            pltpu.VMEM((2 * len(order), 1, wires, LANES), BF16),
            pltpu.VMEM((wires, total), BF16),
            pltpu.SemaphoreType.DMA((cells + 1,)),
        ],
        compiler_params=params(),
        cost_estimate=cost(1e8, 2 * math.prod(shape)),
        name="charge_gradient",
    )(jnp.transpose(ovl_block, (1, 2, 0)), ovl_count, *sources, *ends, intersection, signal)


def pieces_kernel(
    block_hbm, count_hbm, charge_hbm, share_hbm, cot_hbm, own_hbm, keep_hbm, give_hbm, local_hbm,
    block_ref, count_ref, charge_ref, share_ref, edge_ref, cross_ref, own_ref, keep_ref, give_ref, local_ref,
    sems, out_sems, *, half,
):
    cells, planes, entries, wire_block, width = share_ref.shape
    wires, total = local_ref.shape
    ticks = edge_ref.shape[3]
    per_owner = wires // wire_block
    cut = own_ref.shape[0]
    halves = 1 + keep_ref.shape[0]
    owners = 2 * halves
    z = lax.axis_index("gz")
    loads = [
        pltpu.make_async_copy(source, target, sems.at[i])
        for i, (source, target) in enumerate(
            (
                (block_hbm, block_ref),
                (count_hbm, count_ref),
                (charge_hbm, charge_ref),
                (share_hbm, share_ref),
                (cot_hbm.at[:, :EDGE], edge_ref.at[0]),
                (cot_hbm.at[:, wires - EDGE :], edge_ref.at[1]),
            )
        )
    ]
    for load in loads:
        load.start()
    cross_ref[...] = jnp.zeros(cross_ref.shape, F32)
    local_ref[...] = jnp.zeros(local_ref.shape, F32)
    for load in loads[:4]:
        load.wait()
    for b in range(cells):
        pieces = (
            jnp.dot(
                share_ref[b].reshape(planes * entries * wire_block, width),
                charge_ref[b * width : (b + 1) * width],
                preferred_element_type=F32,
            )
            .astype(BF16)
            .astype(F32)
        )
        for p in range(planes):
            for k in range(entries):
                at = (p * entries + k) * wire_block
                piece = pieces[at : at + wire_block]
                piece = jnp.where(k < count_ref[b, p], piece, jnp.zeros_like(piece))
                name = block_ref[p, k, b]
                if p < planes - 1:
                    name = jnp.clip(name, 0, owners * per_owner - 1)
                    start = pl.multiple_of(EDGE + name * wire_block, EDGE)
                    cross_ref[p, pl.ds(start, wire_block)] += piece
                else:
                    name = jnp.clip(name - z * per_owner, 0, per_owner - 1)
                    start = pl.multiple_of(name * wire_block, wire_block)
                    local_ref[pl.ds(start, wire_block)] += piece
    for load in loads[4:]:
        load.wait()
    at = halves * cut
    gap = jnp.zeros((sixteens(planes * half) - planes * half, ticks), F32)
    for side, first in ((0, 0), (1, EDGE - half)):
        rows = [edge_ref[side, p].astype(F32)[first : first + half] for p in range(planes)]
        rows = jnp.concatenate(rows + [gap], axis=0).astype(BF16)
        for part in range(ticks // total):
            give_ref[at : at + rows.shape[0]] = rows[:, part * total : (part + 1) * total]
            at += rows.shape[0]
    extent = wires + 2 * EDGE
    none = jnp.zeros((half, total), F32)
    stores = [
        pltpu.make_async_copy(source, target, out_sems.at[i])
        for i, (source, target) in enumerate(
            (
                (give_ref, give_hbm),
                (keep_ref, keep_hbm),
                (own_ref, own_hbm),
                (local_ref, local_hbm),
            )
        )
    ]
    stores[3].start()
    for k in [*range(1, owners, 2), *range(2, owners, 2), 0]:
        to = z ^ k
        blocks = []
        for p in range(planes - 1):
            rows = cross_ref[p, pl.ds(pl.multiple_of(to * wires, EDGE), extent)]
            blocks.append(rows[EDGE - half : extent - EDGE + half])
        blocks.append(jnp.where(to == z + 1, local_ref[wires - half :], none))
        blocks.append(jnp.where(to == z - 1, local_ref[:half], none))
        rows = padded(blocks)
        if k % 2:
            give_ref[k // 2 * cut : (k // 2 + 1) * cut] = coded(rows, 0)
        elif k:
            keep_ref[k // 2 - 1] = coded(rows, 0)
        else:
            own_ref[...] = rows
        if k == owners - 1:
            stores[0].start()
        if k == owners - 2 and k:
            stores[1].start()
    if owners == 2:
        stores[1].start()
    stores[2].start()
    for store in stores:
        store.wait()


def sixteens(rows):
    return -(-rows // 16) * 16


def padded(blocks):
    count = sum(block.shape[0] for block in blocks)
    if count % 16:
        blocks = blocks + [jnp.zeros((sixteens(count) - count, blocks[0].shape[1]), F32)]
    return jnp.concatenate(blocks, axis=0)


def cut_pieces(ovl_block, ovl_count, charge, intersection, cotangent, owners, half):
    cells, planes, entries, wire_block, width = intersection.shape
    total = charge.shape[1]
    _, wires, ticks = cotangent.shape
    rows = sixteens((planes - 1) * (wires + 2 * half) + 2 * half)
    edges = 2 * sixteens(planes * half) * ticks // total
    hbm = pl.BlockSpec(memory_space=pltpu.HBM)
    blocks = jnp.transpose(ovl_block, (1, 2, 0))
    outs = (
        jax.ShapeDtypeStruct((rows, total), F32),
        jax.ShapeDtypeStruct((owners // 2 - 1, rows, total), BF16),
        jax.ShapeDtypeStruct((owners // 2 * rows + edges, total), BF16),
        jax.ShapeDtypeStruct((wires, total), F32),
    )
    return pl.pallas_call(
        functools.partial(pieces_kernel, half=half),
        out_shape=outs,
        in_specs=[hbm] * 5,
        out_specs=(hbm,) * 4,
        scratch_shapes=[
            pltpu.SMEM(blocks.shape, jnp.int32),
            pltpu.SMEM(ovl_count.shape, jnp.int32),
            pltpu.VMEM(charge.shape, BF16),
            pltpu.VMEM(intersection.shape, BF16),
            pltpu.VMEM((2, planes, EDGE, ticks), BF16),
            pltpu.VMEM((planes - 1, owners * wires + 2 * EDGE, total), F32),
            *[pltpu.VMEM(out.shape, out.dtype) for out in outs],
            pltpu.SemaphoreType.DMA((6,)),
            pltpu.SemaphoreType.DMA((4,)),
        ],
        compiler_params=params(limit=WHOLE_VMEM),
        cost_estimate=cost(1e8, 4 * owners * rows * total),
        name="pieces",
    )(blocks, ovl_count, charge, intersection, cotangent)


def relay_kernel(keep_ref, received_ref, *outs):
    others, rows, _ = keep_ref.shape
    edges = (received_ref.shape[0] - (others + 1) * rows) // 2
    z = lax.axis_index("gz")
    even = lax.rem(z, 2) == 0
    low = received_ref[(others + 1) * rows : (others + 1) * rows + edges]
    high = received_ref[(others + 1) * rows + edges :]
    for j in range(others):
        to = z ^ (2 * (j + 1))
        summed = plain(keep_ref[j], True)
        summed += plain(received_ref[(j + 1) * rows : (j + 2) * rows], True)
        outs[j][...] = coded(summed, 0)
        upward, downward = even & (to == z + 2), jnp.logical_not(even) & (to == z - 2)
        outs[others + j][...] = jnp.where(
            upward, high, jnp.where(downward, low, jnp.zeros_like(low))
        )


def relay(keep, received):
    others, rows, total = keep.shape
    edges = (received.shape[0] - (others + 1) * rows) // 2
    outs = pl.pallas_call(
        relay_kernel,
        out_shape=(jax.ShapeDtypeStruct((rows, total), BF16),) * others
        + (jax.ShapeDtypeStruct((edges, total), BF16),) * others,
        in_specs=[vmem(), vmem()],
        out_specs=(vmem(),) * (2 * others),
        compiler_params=params(),
        cost_estimate=cost(1e7, 6 * others * rows * total),
        name="relay",
    )(keep, received)
    return outs[:others], outs[others:]


def slabs_kernel(*refs, bins, lead, slabs, cross, half):
    count = len(refs) - slabs.bit_length() - 1
    keep_ref, received_ref, others, local_ref = refs[0], refs[1], refs[2 : count - 2], refs[count - 2]
    outs, cut_ref = refs[count:-1], refs[-1]
    total = local_ref.shape[1]
    cut = keep_ref.shape[0]
    summed = keep_ref[...] + plain(received_ref[:cut], True)
    for other in others:
        summed += plain(other[...], True)
    wires = local_ref.shape[0]
    edge = cross * (wires + 2 * half)
    rows = padded([summed[: edge + half], local_ref[...], summed[edge + half : edge + 2 * half]])
    none = jnp.zeros((rows.shape[0], LANES), F32)
    lane = lax.broadcasted_iota(jnp.int32, none.shape, 1)
    level = jnp.broadcast_to(rows[:, :1].astype(BF16).astype(F32), none.shape)
    tiles = [rows[:, t * LANES : (t + 1) * LANES] - level for t in range(total // LANES)]
    for to in range(slabs):
        at = to * bins - lead
        tile, shift = at // LANES, at % LANES
        pair = [tiles[t] if 0 <= t < len(tiles) else -level for t in (tile, tile + 1)]
        value = shared_lanes(pair[0], pair[1], shift, lane)
        cut_ref[to] = jnp.where(lane == 0, level, value).astype(BF16)
    slab = lax.axis_index("drift")
    outs[0][...] = cut_ref[slab]
    size = rows.shape[0]
    for s, out in enumerate(outs[1:]):
        for i in range(slabs >> (s + 1)):
            out[i * size : (i + 1) * size] = cut_ref[slab ^ ((2 * i + 1) << s)]


def cut_slabs(keep, received, others, local, bins, slabs, cross, half, before):
    wires, total = local.shape
    rows = sixteens((cross + 1) * (wires + 2 * half))
    steps = slabs.bit_length() - 1
    counts = [1] + [slabs >> (s + 1) for s in range(steps)]
    return pl.pallas_call(
        functools.partial(
            slabs_kernel, bins=bins, lead=WINDOW // 2 - HB, slabs=slabs, cross=cross, half=half
        ),
        out_shape=tuple(jax.ShapeDtypeStruct((n * rows, LANES), BF16) for n in counts),
        in_specs=[vmem()] * (3 + len(others)) + [anywhere()],
        out_specs=(vmem(),) * len(counts),
        scratch_shapes=[pltpu.VMEM((slabs, rows, LANES), BF16)],
        compiler_params=params(),
        cost_estimate=cost(1e8, 4 * rows * total),
        name="slab_currents",
    )(keep, received, *others, local, before)


def pass_kernel(*refs, step, size):
    own_ref, arrived, out_ref = refs[0], refs[1:-1], refs[-1]
    for i in range(own_ref.shape[0] // size):
        here = slice(i * size, (i + 1) * size)
        total = plain(own_ref[here], False)
        for r, other in enumerate(arrived):
            at = ((2 * i + 1) << step) >> (r + 1)
            total += plain(other[at * size : (at + 1) * size], False)
        out_ref[here] = coded(total, WINDOW // 2)


def pass_on(own, arrived, step, size):
    return pl.pallas_call(
        functools.partial(pass_kernel, step=step, size=size),
        out_shape=jax.ShapeDtypeStruct(own.shape, BF16),
        in_specs=[vmem()] * (1 + len(arrived)),
        out_specs=vmem(),
        compiler_params=params(),
        cost_estimate=cost(1e6, 4 * math.prod(own.shape)),
        name="pass_on",
    )(own, *arrived)


def signal_kernel(*refs, wire_taps):
    parts, (table_ref, out_ref, even_ref, odd_ref, level_ref, lines_ref) = refs[:-6], refs[-6:]
    planes, blocks, _, span = table_ref.shape
    _, wires, _ = out_ref.shape
    half = (wire_taps - 1) // 2
    extent = wires + 2 * half
    step = span * 16 // LANES
    middle = WINDOW // 2
    lane = lax.broadcasted_iota(jnp.int32, (wires, LANES), 1)
    size = parts[0].shape[0]
    summed = plain(parts[0][...], False)
    for part in parts[1:]:
        summed += plain(part[:size], False)
    for p in range(planes):
        currents = summed[p * extent : (p + 1) * extent]
        level = currents[:, middle : middle + 1].astype(BF16).astype(F32)
        level = jnp.broadcast_to(level, currents.shape)
        level_ref[p] = level
        currents = currents - level
        levels = jnp.zeros((wires, LANES), F32)
        for a in range(wire_taps):
            at = a
            both = (lane == WINDOW + a) | (lane == WINDOW + wire_taps + a)
            levels = jnp.where(both, level_ref[p, at : at + wires], levels)
        turned = {}
        for block in range(blocks):
            i = p * blocks + block
            turns = [(-step * block) % LANES, (WINDOW - step * block) % LANES]
            for turn in turns:
                if turn not in turned:
                    turned[turn] = (i, len(turned) % 2)
                    target = odd_ref if turned[turn][1] else even_ref
                    target[i] = pltpu.roll(currents, turn, 1) if turn else currents
            (left_at, left_odd), (right_at, right_odd) = turned[turns[0]], turned[turns[1]]
            left_ref = (odd_ref if left_odd else even_ref).at[left_at]
            right_ref = (odd_ref if right_odd else even_ref).at[right_at]
            for pair in range((wire_taps + 1) // 2):
                at = 2 * pair
                right = levels
                if 2 * pair + 1 < wire_taps:
                    right = right_ref[at + 1 : at + 1 + wires]
                line = jnp.where(lane < WINDOW, left_ref[at : at + wires], right)
                lines_ref[i % 2, :, pair * LANES : (pair + 1) * LANES] = line.astype(BF16)
            out_ref[p, :, block * span : (block + 1) * span] = jnp.dot(
                lines_ref[i % 2], table_ref[p, block], preferred_element_type=F32
            ).astype(BF16)


def forward(parts, table, wires, wire_taps):
    planes, blocks, depth, span = table.shape
    extent = wires + wire_taps - 1
    shape = (planes, wires, blocks * span)
    return pl.pallas_call(
        functools.partial(signal_kernel, wire_taps=wire_taps),
        out_shape=jax.ShapeDtypeStruct(shape, BF16),
        in_specs=[vmem()] * (len(parts) + 1),
        out_specs=vmem(),
        scratch_shapes=[
            pltpu.VMEM((planes * blocks, extent, LANES), F32),
            pltpu.VMEM((planes * blocks, extent, LANES), F32),
            pltpu.VMEM((planes, extent, LANES), F32),
            pltpu.VMEM((2, wires, depth), BF16),
        ],
        compiler_params=params(),
        cost_estimate=cost(4e9, 2 * math.prod(table.shape)),
        name="signal",
    )(*parts, table)


def local(charge, intersection, ovl_block, ovl_count, diff_class, response, cotangent):
    total = charge.shape[1]
    owners = lax.axis_size("gz")
    slabs = lax.axis_size("drift")
    planes, wires, ticks = cotangent.shape
    wire_taps = response.shape[1]
    half = (wire_taps - 1) // 2
    bins = total // slabs

    currents, keep, give, local_currents = cut_pieces(
        ovl_block, ovl_count, charge, intersection, cotangent, owners, half
    )
    received = swap(give, "gz", 1)
    sums, edges = relay(keep.astype(F32), received) if owners > 2 else ((), ())
    beyond = [swap(block, "gz", 2 * j) for j, block in enumerate(edges, 1)]
    others = [swap(block, "gz", 2 * j) for j, block in enumerate(sums, 1)]

    levels, kinds = smeared_levels(
        diff_class, response, bins, slabs, sums[0] if sums else received
    )
    table = build_table(levels, kinds, planes, wire_taps, ticks)
    partial, crossing = backward(table, cotangent, received, beyond, wire_taps)
    distance = slabs // 2
    spread = [crossing] + [
        swap(partial if k == distance else crossing, "drift", k) for k in range(1, slabs)
    ]
    held, order = join(partial, spread[distance], 1), [0, distance]
    distance //= 2
    while distance > 1:
        held = join(held, swap(held, "drift", distance), len(order))
        order += [k ^ distance for k in order]
        distance //= 2
    ends = [held, swap(held, "drift", 1)]

    cuts = cut_slabs(
        currents, received, others, local_currents, bins, slabs, planes - 1, half, partial
    )
    windows = [cuts[0]]
    for step, block in enumerate(cuts[1:]):
        if step:
            block = pass_on(block, windows[1:], step, cuts[0].shape[0])
        windows.append(swap(block, "drift", 1 << step))

    count = planes - 1
    *cross, both = merge(spread, bins, total, cuts[0])
    if owners == 4:
        across = [swap(block, "gz", 2) for block in cross]
        sources = [both, swap(both, "gz", 1), *across, *(swap(block, "gz", 1) for block in across)]
        places = [(0, None), (1, None)]
        places += [(2, p) for p in range(count)] + [(3, p) for p in range(count)]
    else:
        sources = [lax.all_gather(block, "gz", axis=0) for block in cross]
        places = [(None, p) for p in range(count)]
    signal = forward(windows, table, wires, wire_taps)
    charge_grad, signal = charge_gradient(
        ovl_block, ovl_count, sources, places, ends, order, intersection, owners, signal, bins, total
    )
    return signal, charge_grad


def solution(mesh):
    return jax.shard_map(
        local,
        mesh=mesh,
        in_specs=(
            P(("apa", "gz", "drift"), None),
            P(("apa", "gz", "drift"), None, None, None, None),
            P(("apa", "gz", "drift"), None, None),
            P(("apa", "gz", "drift"), None),
            P("apa"),
            P(),
            P("apa", "gz", "drift"),
        ),
        out_specs=(P("apa", "gz", "drift"), P(("apa", "gz", "drift"), None)),
        check_vma=False,
    )
```

```python
import functools
import math

import jax
import jax.numpy as jnp
from jax import lax
from jax.experimental import pallas as pl
from jax.experimental.pallas import tpu as pltpu
from jax.sharding import PartitionSpec as P

TPB = 8
HB = 2
CLASSES = 6
LANES = 128
EDGE = 16
GROUP = 8
WINDOW = 64
LEAD = HB * TPB - TPB // 2
VMEM_LIMIT = 24 * 1024 * 1024
WHOLE_VMEM = 61 * 1024 * 1024
BF16 = jnp.bfloat16
F32 = jnp.float32


def params(semantics=None, limit=VMEM_LIMIT):
    return pltpu.CompilerParams(vmem_limit_bytes=limit, dimension_semantics=semantics)


def vmem():
    return pl.BlockSpec(memory_space=pltpu.VMEM)


def smem():
    return pl.BlockSpec(memory_space=pltpu.SMEM)


def anywhere():
    return pl.BlockSpec(memory_space=pl.ANY)


def cost(flops, moved):
    return pl.CostEstimate(flops=int(flops), bytes_accessed=int(moved), transcendentals=0)


def swap(block, axis, distance):
    count = lax.axis_size(axis)
    return lax.ppermute(block, axis, [(i, i ^ distance) for i in range(count)])


def widths(number):
    spread = TPB * (0.2 + 0.15 * number)
    half = HB * TPB
    total = sum(math.exp(-((j + 0.5) ** 2) / (2.0 * spread * spread)) for j in range(-half, half))
    return 1.0 / (2.0 * spread * spread), 1.0 / total


def shared_lanes(left, right, shift, lane):
    if shift == 0:
        return left
    back = LANES - shift
    return jnp.where(lane < back, pltpu.roll(left, back, 1), pltpu.roll(right, back, 1))


def coded(rows, column):
    lane = lax.broadcasted_iota(jnp.int32, rows.shape, 1)
    level = jnp.broadcast_to(rows[:, column : column + 1].astype(BF16).astype(F32), rows.shape)
    return jnp.where(lane == 0, level, rows - level).astype(BF16)


def plain(rows, first):
    rows = rows.astype(F32)
    lane = lax.broadcasted_iota(jnp.int32, rows.shape, 1)
    level = jnp.broadcast_to(rows[:, :1], rows.shape)
    return jnp.where(lane == 0, level if first else jnp.zeros_like(rows), rows + level)


def levels_kernel(
    class_ref, response_ref, _, level_ref, kind_ref, flat_ref, *, bins, slabs, total
):
    planes, wire_taps, length = response_ref.shape
    rows = level_ref.shape[0] // planes
    groups = kind_ref.shape[0]
    slab = lax.axis_index("drift")
    lane = lax.broadcasted_iota(jnp.int32, (GROUP, LANES), 1)
    packed = class_ref[...].astype(F32)
    tiles = []
    for t in range(total // LANES):
        at = slice(t % 2 * LANES, (t % 2 + 1) * LANES)
        tiles.append(jnp.broadcast_to(packed[t // 2 : t // 2 + 1, at], (GROUP, LANES)))
    classes = tiles[0]
    none = jnp.zeros((GROUP, LANES), F32)
    numbers = none
    for source in range(slabs):
        at = source * bins - (WINDOW // 2 - HB)
        tile, shift = at // LANES, at % LANES
        pair = [tiles[t] if 0 <= t < len(tiles) else none for t in (tile, tile + 1)]
        numbers = jnp.where(slab == source, shared_lanes(pair[0], pair[1], shift, lane), numbers)
    x = slab * bins - (WINDOW // 2 - HB) + lane
    numbers = jnp.where((x >= 0) & (x < HB), (CLASSES + x).astype(F32), numbers)
    column = jnp.broadcast_to(numbers[:1], (LANES, LANES)).T.astype(jnp.int32)
    for m in range(groups):
        kind_ref[m] = column[m * GROUP : (m + 1) * GROUP]
    flat_ref[...] = jnp.zeros(flat_ref.shape, F32)
    for p in range(planes):
        flat_ref[p * rows : p * rows + wire_taps, :length] = response_ref[p].astype(F32)
    taps = flat_ref[...].astype(BF16)
    tap = lax.broadcasted_iota(jnp.int32, (LANES, 2 * LANES), 0)
    tick = lax.broadcasted_iota(jnp.int32, (LANES, 2 * LANES), 1)
    step = tick - tap - LEAD
    offset = step.astype(F32) - (TPB - 1) / 2.0
    squared = offset * offset
    inside = jnp.abs(offset) < HB * TPB
    for kind in range(CLASSES + HB):
        keep = inside
        if kind < CLASSES:
            narrow, scale = widths(kind)
        else:
            edge = kind - CLASSES
            narrow, scale = widths(0)
            for number in range(1, CLASSES):
                chosen = classes[:1, edge : edge + 1] == number
                narrow = jnp.where(chosen, widths(number)[0], narrow)
                scale = jnp.where(chosen, widths(number)[1], scale)
            keep = inside & (step >= -TPB * edge)
        smear = jnp.where(keep, jnp.exp(-(squared * narrow)) * scale, 0.0)
        high = smear.astype(BF16)
        low = (smear - high.astype(F32)).astype(BF16)
        near = jnp.dot(taps[:, :LANES], high, preferred_element_type=F32) + jnp.dot(
            taps[:, :LANES], low, preferred_element_type=F32
        )
        far = jnp.dot(taps[:, LANES:], high[:, :LANES], preferred_element_type=F32) + jnp.dot(
            taps[:, LANES:], low[:, :LANES], preferred_element_type=F32
        )
        level_ref[:, kind, :LANES] = near[:, :LANES]
        level_ref[:, kind, LANES:] = near[:, LANES:] + far


def smeared_levels(diff_class, response, bins, slabs, before):
    planes, wire_taps, _ = response.shape
    total = diff_class.shape[0]
    reach = 2 * LANES
    rows = -(-wire_taps // 8) * 8
    groups = (bins + WINDOW // 2) // GROUP
    classes = jnp.pad(diff_class.astype(BF16), (0, 8 * reach - total)).reshape(8, reach)
    return pl.pallas_call(
        functools.partial(levels_kernel, bins=bins, slabs=slabs, total=total),
        out_shape=(
            jax.ShapeDtypeStruct((planes * rows, CLASSES + HB, reach), F32),
            jax.ShapeDtypeStruct((groups, GROUP, LANES), jnp.int32),
        ),
        in_specs=[vmem(), vmem(), anywhere()],
        out_specs=(vmem(), vmem()),
        scratch_shapes=[pltpu.VMEM((planes * rows, reach), F32)],
        compiler_params=params(),
        cost_estimate=cost(1e8, 1e6),
        name="levels",
    )(classes, response, before)


def table_kernel(level_ref, kind_ref, table_ref, sum_ref, *, wire_taps):
    planes, blocks, depth, span = table_ref.shape
    rows = level_ref.shape[0] // planes
    groups = kind_ref.shape[0]
    tiles = span // LANES
    lane = lax.broadcasted_iota(jnp.int32, (GROUP, LANES), 1)
    row = lax.broadcasted_iota(jnp.int32, (GROUP, LANES), 0)
    starts = [LEAD_SHIFT + odd * (LANES // 2) + TPB * row for odd in range(2)]
    after = [lane >= start for start in starts]
    zero = jnp.zeros((GROUP, LANES), F32)
    empty = jnp.zeros((2 * GROUP, LANES), BF16)

    def body(a, plane):
        levels = level_ref[plane * rows + a]
        halves = [levels[:, :LANES], levels[:, LANES:]]
        pieces = []
        for m in range(groups):
            odd = m % 2
            parts = [
                pltpu.roll(
                    jnp.take_along_axis(half, kind_ref[m], axis=0),
                    LEAD_SHIFT + odd * (LANES // 2),
                    1,
                    stride=TPB,
                    stride_axis=0,
                )
                for half in halves
            ]
            pieces.append(
                (
                    jnp.where(after[odd], parts[0], zero),
                    jnp.where(after[odd], parts[1], parts[0]),
                    jnp.where(after[odd], zero, parts[1]),
                )
            )
        for block in range(blocks):
            for tile in range(tiles):
                here = slice(tile * LANES, (tile + 1) * LANES)
                total = zero
                for quarter in range(WINDOW // (2 * GROUP)):
                    m = 2 * (tiles * block + quarter)
                    at = a * WINDOW + quarter * 2 * GROUP
                    at = pl.ds(pl.multiple_of(at, 2 * GROUP), 2 * GROUP)
                    third = tile - quarter + 2
                    value = empty
                    if 0 <= third <= 2 and m + 1 < groups:
                        value = jnp.concatenate(
                            [pieces[m][third], pieces[m + 1][third]], axis=0
                        ).astype(BF16)
                        total = total + pieces[m][third] + pieces[m + 1][third]
                    table_ref[plane, block, at, here] = value
                sum_ref[a, block, :, here] = total
        return plane

    def whole_plane(plane, _):
        lax.fori_loop(0, wire_taps, body, plane, unroll=UNROLL)
        for block in range(blocks):
            total = jnp.sum(sum_ref[:, block], axis=1)
            high = total.astype(BF16).astype(F32)
            spare = jnp.zeros((depth - (WINDOW + 2) * wire_taps, span), F32)
            table_ref[plane, block, wire_taps * WINDOW :, :] = jnp.concatenate(
                [high, total - high, spare], axis=0
            ).astype(BF16)
        return 0

    lax.fori_loop(0, planes, whole_plane, 0)


UNROLL = 21
LEAD_SHIFT = (TPB * HB - LEAD) % LANES


def build_table(levels, kinds, planes, wire_taps, ticks_here):
    tiles = math.gcd(ticks_here, 2 * LANES) // LANES
    blocks = ticks_here // (tiles * LANES)
    shape = (planes, blocks, (wire_taps + 1) * WINDOW, tiles * LANES)
    return pl.pallas_call(
        functools.partial(table_kernel, wire_taps=wire_taps),
        out_shape=jax.ShapeDtypeStruct(shape, BF16),
        in_specs=[vmem(), vmem()],
        out_specs=vmem(),
        scratch_shapes=[pltpu.VMEM((wire_taps, blocks, GROUP, tiles * LANES), F32)],
        compiler_params=params(),
        cost_estimate=cost(4e9, 2 * math.prod(shape)),
        name="table",
    )(levels, kinds)


def back_kernel(table_ref, own_ref, received_ref, *refs, wire_taps):
    others, (out_ref, cross_ref, cot_ref, wide_ref) = refs[:-4], refs[-4:]
    planes, blocks, _, span = table_ref.shape
    _, wires, ticks = own_ref.shape
    total = received_ref.shape[1]
    half = (wire_taps - 1) // 2
    parts = ticks // total
    size = sixteens(planes * half)
    side = parts * size
    lows = received_ref.shape[0] - 2 * side
    even = lax.rem(lax.axis_index("gz"), 2) == 0
    lane = lax.broadcasted_iota(jnp.int32, (wires, LANES), 1)
    none = jnp.zeros((wires, LANES), F32)
    gap = jnp.zeros((EDGE - half, total), F32)
    step = span * 16 // LANES
    columns = (wire_taps + 1) // 2
    edges = []
    for part in range(parts):
        low = received_ref[lows + part * size : lows + (part + 1) * size].astype(F32)
        high = received_ref[lows + side + part * size : lows + side + (part + 1) * size].astype(F32)
        near = jnp.where(even, low, high)
        far = jnp.zeros((size, total), F32)
        for other in others:
            far += other[part * size : (part + 1) * size].astype(F32)
        edges.append((jnp.where(even, far, near), jnp.where(even, near, far)))
    for plane in range(planes):
        cot_ref[plane, EDGE : EDGE + wires] = own_ref[plane]
        for part in range(parts):
            here = slice(part * total, (part + 1) * total)
            before, after = [edge[plane * half : (plane + 1) * half] for edge in edges[part]]
            cot_ref[plane, :EDGE, here] = jnp.concatenate([gap, before], axis=0).astype(BF16)
            cot_ref[plane, EDGE + wires :, here] = jnp.concatenate([after, gap], axis=0).astype(BF16)
        result = none
        for block in range(blocks):
            i = (plane * blocks + block) % wide_ref.shape[0]
            wide = lax.dot_general(
                cot_ref[plane, :, block * span : (block + 1) * span],
                table_ref[plane, block, : columns * LANES],
                (((1,), (1,)), ((), ())),
                preferred_element_type=F32,
            )
            for column in range(columns):
                wide_ref[i, column] = wide[:, column * LANES : (column + 1) * LANES]
            left, right = none, none
            for column in range(columns):
                at = EDGE + half - 2 * column
                left += wide_ref[i, column, at : at + wires]
                if 2 * column + 1 < wire_taps:
                    right += wide_ref[i, column, at - 1 : at - 1 + wires]
            both = jnp.where(lane < WINDOW, left + pltpu.roll(right, WINDOW, 1), none)
            result += pltpu.roll(both, block * step, 1) if block else both
        out_ref[plane] = result.astype(BF16)
        if plane < planes - 1:
            cross_ref[plane] = result.astype(BF16)


def backward(table, cotangent, received, others, wire_taps):
    planes, _, _, _ = table.shape
    _, wires, ticks = cotangent.shape
    extent = wires + 2 * EDGE
    columns = (wire_taps + 1) // 2
    return pl.pallas_call(
        functools.partial(back_kernel, wire_taps=wire_taps),
        out_shape=(
            jax.ShapeDtypeStruct((planes, wires, LANES), BF16),
            jax.ShapeDtypeStruct((planes - 1, wires, LANES), BF16),
        ),
        in_specs=[vmem()] * (3 + len(others)),
        out_specs=(vmem(), vmem()),
        scratch_shapes=[
            pltpu.VMEM((planes, extent, ticks), BF16),
            pltpu.VMEM((2, columns, extent, LANES), F32),
        ],
        compiler_params=params(),
        cost_estimate=cost(4e9, 2 * math.prod(table.shape)),
        name="bin_gradients",
    )(table, cotangent, received, *others)


def join_kernel(first_ref, second_ref, out_ref):
    count = out_ref.shape[0] // 2
    out_ref[:count] = first_ref[first_ref.shape[0] - count :]
    out_ref[count:] = second_ref[second_ref.shape[0] - count :]


def join(first, second, count):
    shape = (2 * count,) + first.shape[1:]
    return pl.pallas_call(
        join_kernel,
        out_shape=jax.ShapeDtypeStruct(shape, BF16),
        in_specs=[vmem()] * 2,
        out_specs=vmem(),
        compiler_params=params(),
        cost_estimate=cost(1e6, 4 * math.prod(shape)),
        name="join",
    )(first, second)


def added(slab_ref, p, bins, lead, total):
    slabs, _, wires, _ = slab_ref.shape
    lane = lax.broadcasted_iota(jnp.int32, (wires, LANES), 1)
    none = jnp.zeros((wires, LANES), F32)
    tiles = [none] * (total // LANES)
    for source in range(slabs):
        values = slab_ref[source, p].astype(F32)
        tile, shift = (source * bins - lead) // LANES, (source * bins - lead) % LANES
        if shift:
            values = pltpu.roll(values, shift, 1)
        for t, inside in ((tile, lane >= shift), (tile + 1, lane < shift)):
            if 0 <= t < len(tiles):
                tiles[t] += jnp.where(inside, values, none)
    return [values.astype(BF16) for values in tiles]


def merge_kernel(*refs, bins, lead, planes):
    outs, slab_ref = refs[-planes - 2 : -1], refs[-1]
    total = outs[0].shape[1]
    slab = lax.axis_index("drift")
    for k in range(slab_ref.shape[0]):
        slab_ref[slab ^ k] = refs[k][:planes]
    for p in range(planes):
        for t, values in enumerate(added(slab_ref, p, bins, lead, total)):
            here = slice(t * LANES, (t + 1) * LANES)
            outs[p][:, here] = values
            outs[planes][p, :, here] = values


def merge(arrays, bins, total, before):
    planes, wires, _ = arrays[0].shape
    return pl.pallas_call(
        functools.partial(merge_kernel, bins=bins, lead=WINDOW // 2 - HB, planes=planes),
        out_shape=(jax.ShapeDtypeStruct((wires, total), BF16),) * planes
        + (jax.ShapeDtypeStruct((planes, wires, total), BF16),),
        in_specs=[vmem()] * len(arrays) + [anywhere()],
        out_specs=(vmem(),) * (planes + 1),
        scratch_shapes=[pltpu.VMEM((len(arrays), planes, wires, LANES), BF16)],
        compiler_params=params(),
        cost_estimate=cost(1e8, 4 * planes * wires * total),
        name="merge_bins",
    )(*arrays, before)


def charge_kernel(block_ref, count_ref, *refs, places, order, bins, lead):
    sources, refs = refs[:-12], refs[-12:]
    held_ref, brought_ref, share_ref, signal_ref, out_hbm, signal_hbm = refs[:6]
    all_ref, chosen_ref, out_ref, slab_ref, local_ref, sems = refs[6:]
    cells, planes, entries, wire_block, width = share_ref.shape
    owners, _, wires, total = all_ref.shape
    per_owner = wires // wire_block
    z = lax.axis_index("gz")
    slab = lax.axis_index("drift")
    for i, k in enumerate(order):
        slab_ref[slab ^ k, 0] = held_ref[i]
        slab_ref[slab ^ k ^ 1, 0] = brought_ref[i]
    for t, values in enumerate(added(slab_ref, 0, bins, lead, total)):
        local_ref[:, t * LANES : (t + 1) * LANES] = values
    for (k, p), source in zip(places, sources, strict=True):
        if k is None:
            all_ref[:, p] = source[...]
        elif p is None:
            all_ref[z ^ k] = source[...]
        else:
            all_ref[z ^ k, p] = source[...]
    empty = jnp.zeros((wire_block, total), BF16)
    stores = [pltpu.make_async_copy(signal_ref, signal_hbm, sems.at[cells])]
    stores[0].start()
    for b in range(cells):
        for p in range(planes):
            for k in range(entries):
                name = block_ref[p, k, b]
                if p < planes - 1:
                    name = jnp.clip(name, 0, owners * per_owner - 1)
                    owner = name // per_owner
                    start = pl.multiple_of((name - owner * per_owner) * wire_block, wire_block)
                    rows = all_ref[owner, p, pl.ds(start, wire_block), :]
                else:
                    name = jnp.clip(name - z * per_owner, 0, per_owner - 1)
                    start = pl.multiple_of(name * wire_block, wire_block)
                    rows = local_ref[pl.ds(start, wire_block), :]
                at = (p * entries + k) * wire_block
                chosen_ref[b, at : at + wire_block] = jnp.where(k < count_ref[b, p], rows, empty)
        here = slice(b * width, (b + 1) * width)
        out_ref[here] = lax.dot_general(
            share_ref[b].reshape(planes * entries * wire_block, width),
            chosen_ref[b],
            (((0,), (0,)), ((), ())),
            preferred_element_type=F32,
        ).astype(BF16)
        store = pltpu.make_async_copy(out_ref.at[here], out_hbm.at[here], sems.at[b])
        store.start()
        stores.append(store)
    for store in stores:
        store.wait()


def charge_gradient(
    ovl_block, ovl_count, sources, places, ends, order, intersection, owners, signal, bins, total
):
    cells, planes, entries, wire_block, width = intersection.shape
    wires = ends[0].shape[1]
    shape = (owners, planes - 1, wires, total)
    return pl.pallas_call(
        functools.partial(
            charge_kernel, places=places, order=order, bins=bins, lead=WINDOW // 2 - HB
        ),
        out_shape=(
            jax.ShapeDtypeStruct((cells * width, total), BF16),
            jax.ShapeDtypeStruct(signal.shape, BF16),
        ),
        in_specs=[smem(), smem()] + [vmem()] * (len(sources) + 4),
        out_specs=(anywhere(), anywhere()),
        scratch_shapes=[
            pltpu.VMEM(shape, BF16),
            pltpu.VMEM((cells, planes * entries * wire_block, total), BF16),
            pltpu.VMEM((cells * width, total), BF16),
            pltpu.VMEM((2 * len(order), 1, wires, LANES), BF16),
            pltpu.VMEM((wires, total), BF16),
            pltpu.SemaphoreType.DMA((cells + 1,)),
        ],
        compiler_params=params(),
        cost_estimate=cost(1e8, 2 * math.prod(shape)),
        name="charge_gradient",
    )(jnp.transpose(ovl_block, (1, 2, 0)), ovl_count, *sources, *ends, intersection, signal)


def pieces_kernel(
    block_hbm, count_hbm, charge_hbm, share_hbm, cot_hbm, own_hbm, keep_hbm, give_hbm, local_hbm,
    block_ref, count_ref, charge_ref, share_ref, edge_ref, cross_ref, own_ref, keep_ref, give_ref, local_ref,
    sems, out_sems, *, half,
):
    cells, planes, entries, wire_block, width = share_ref.shape
    wires, total = local_ref.shape
    ticks = edge_ref.shape[3]
    per_owner = wires // wire_block
    cut = own_ref.shape[0]
    halves = 1 + keep_ref.shape[0]
    owners = 2 * halves
    z = lax.axis_index("gz")
    loads = [
        pltpu.make_async_copy(source, target, sems.at[i])
        for i, (source, target) in enumerate(
            (
                (block_hbm, block_ref),
                (count_hbm, count_ref),
                (charge_hbm, charge_ref),
                (share_hbm, share_ref),
                (cot_hbm.at[:, :EDGE], edge_ref.at[0]),
                (cot_hbm.at[:, wires - EDGE :], edge_ref.at[1]),
            )
        )
    ]
    for load in loads:
        load.start()
    cross_ref[...] = jnp.zeros(cross_ref.shape, F32)
    local_ref[...] = jnp.zeros(local_ref.shape, F32)
    for load in loads[:4]:
        load.wait()
    for b in range(cells):
        pieces = (
            jnp.dot(
                share_ref[b].reshape(planes * entries * wire_block, width),
                charge_ref[b * width : (b + 1) * width],
                preferred_element_type=F32,
            )
            .astype(BF16)
            .astype(F32)
        )
        for p in range(planes):
            for k in range(entries):
                at = (p * entries + k) * wire_block
                piece = pieces[at : at + wire_block]
                piece = jnp.where(k < count_ref[b, p], piece, jnp.zeros_like(piece))
                name = block_ref[p, k, b]
                if p < planes - 1:
                    name = jnp.clip(name, 0, owners * per_owner - 1)
                    start = pl.multiple_of(EDGE + name * wire_block, EDGE)
                    cross_ref[p, pl.ds(start, wire_block)] += piece
                else:
                    name = jnp.clip(name - z * per_owner, 0, per_owner - 1)
                    start = pl.multiple_of(name * wire_block, wire_block)
                    local_ref[pl.ds(start, wire_block)] += piece
    for load in loads[4:]:
        load.wait()
    at = halves * cut
    gap = jnp.zeros((sixteens(planes * half) - planes * half, ticks), F32)
    for side, first in ((0, 0), (1, EDGE - half)):
        rows = [edge_ref[side, p].astype(F32)[first : first + half] for p in range(planes)]
        rows = jnp.concatenate(rows + [gap], axis=0).astype(BF16)
        for part in range(ticks // total):
            give_ref[at : at + rows.shape[0]] = rows[:, part * total : (part + 1) * total]
            at += rows.shape[0]
    extent = wires + 2 * EDGE
    none = jnp.zeros((half, total), F32)
    stores = [
        pltpu.make_async_copy(source, target, out_sems.at[i])
        for i, (source, target) in enumerate(
            (
                (give_ref, give_hbm),
                (keep_ref, keep_hbm),
                (own_ref, own_hbm),
                (local_ref, local_hbm),
            )
        )
    ]
    stores[3].start()
    for k in [*range(1, owners, 2), *range(2, owners, 2), 0]:
        to = z ^ k
        blocks = []
        for p in range(planes - 1):
            rows = cross_ref[p, pl.ds(pl.multiple_of(to * wires, EDGE), extent)]
            blocks.append(rows[EDGE - half : extent - EDGE + half])
        blocks.append(jnp.where(to == z + 1, local_ref[wires - half :], none))
        blocks.append(jnp.where(to == z - 1, local_ref[:half], none))
        rows = padded(blocks)
        if k % 2:
            give_ref[k // 2 * cut : (k // 2 + 1) * cut] = coded(rows, 0)
        elif k:
            keep_ref[k // 2 - 1] = coded(rows, 0)
        else:
            own_ref[...] = rows
        if k == owners - 1:
            stores[0].start()
        if k == owners - 2 and k:
            stores[1].start()
    if owners == 2:
        stores[1].start()
    stores[2].start()
    for store in stores:
        store.wait()


def sixteens(rows):
    return -(-rows // 16) * 16


def padded(blocks):
    count = sum(block.shape[0] for block in blocks)
    if count % 16:
        blocks = blocks + [jnp.zeros((sixteens(count) - count, blocks[0].shape[1]), F32)]
    return jnp.concatenate(blocks, axis=0)


def cut_pieces(ovl_block, ovl_count, charge, intersection, cotangent, owners, half):
    cells, planes, entries, wire_block, width = intersection.shape
    total = charge.shape[1]
    _, wires, ticks = cotangent.shape
    rows = sixteens((planes - 1) * (wires + 2 * half) + 2 * half)
    edges = 2 * sixteens(planes * half) * ticks // total
    hbm = pl.BlockSpec(memory_space=pltpu.HBM)
    blocks = jnp.transpose(ovl_block, (1, 2, 0))
    outs = (
        jax.ShapeDtypeStruct((rows, total), F32),
        jax.ShapeDtypeStruct((owners // 2 - 1, rows, total), BF16),
        jax.ShapeDtypeStruct((owners // 2 * rows + edges, total), BF16),
        jax.ShapeDtypeStruct((wires, total), F32),
    )
    return pl.pallas_call(
        functools.partial(pieces_kernel, half=half),
        out_shape=outs,
        in_specs=[hbm] * 5,
        out_specs=(hbm,) * 4,
        scratch_shapes=[
            pltpu.SMEM(blocks.shape, jnp.int32),
            pltpu.SMEM(ovl_count.shape, jnp.int32),
            pltpu.VMEM(charge.shape, BF16),
            pltpu.VMEM(intersection.shape, BF16),
            pltpu.VMEM((2, planes, EDGE, ticks), BF16),
            pltpu.VMEM((planes - 1, owners * wires + 2 * EDGE, total), F32),
            *[pltpu.VMEM(out.shape, out.dtype) for out in outs],
            pltpu.SemaphoreType.DMA((6,)),
            pltpu.SemaphoreType.DMA((4,)),
        ],
        compiler_params=params(limit=WHOLE_VMEM),
        cost_estimate=cost(1e8, 4 * owners * rows * total),
        name="pieces",
    )(blocks, ovl_count, charge, intersection, cotangent)


def relay_kernel(keep_ref, received_ref, *outs):
    others, rows, _ = keep_ref.shape
    edges = (received_ref.shape[0] - (others + 1) * rows) // 2
    z = lax.axis_index("gz")
    even = lax.rem(z, 2) == 0
    low = received_ref[(others + 1) * rows : (others + 1) * rows + edges]
    high = received_ref[(others + 1) * rows + edges :]
    for j in range(others):
        to = z ^ (2 * (j + 1))
        summed = plain(keep_ref[j], True)
        summed += plain(received_ref[(j + 1) * rows : (j + 2) * rows], True)
        outs[j][...] = coded(summed, 0)
        upward, downward = even & (to == z + 2), jnp.logical_not(even) & (to == z - 2)
        outs[others + j][...] = jnp.where(
            upward, high, jnp.where(downward, low, jnp.zeros_like(low))
        )


def relay(keep, received):
    others, rows, total = keep.shape
    edges = (received.shape[0] - (others + 1) * rows) // 2
    outs = pl.pallas_call(
        relay_kernel,
        out_shape=(jax.ShapeDtypeStruct((rows, total), BF16),) * others
        + (jax.ShapeDtypeStruct((edges, total), BF16),) * others,
        in_specs=[vmem(), vmem()],
        out_specs=(vmem(),) * (2 * others),
        compiler_params=params(),
        cost_estimate=cost(1e7, 6 * others * rows * total),
        name="relay",
    )(keep, received)
    return outs[:others], outs[others:]


def slabs_kernel(*refs, bins, lead, slabs, cross, half):
    count = len(refs) - slabs.bit_length() - 1
    keep_ref, received_ref, others, local_ref = refs[0], refs[1], refs[2 : count - 2], refs[count - 2]
    outs, cut_ref = refs[count:-1], refs[-1]
    total = local_ref.shape[1]
    cut = keep_ref.shape[0]
    summed = keep_ref[...] + plain(received_ref[:cut], True)
    for other in others:
        summed += plain(other[...], True)
    wires = local_ref.shape[0]
    edge = cross * (wires + 2 * half)
    rows = padded([summed[: edge + half], local_ref[...], summed[edge + half : edge + 2 * half]])
    none = jnp.zeros((rows.shape[0], LANES), F32)
    lane = lax.broadcasted_iota(jnp.int32, none.shape, 1)
    level = jnp.broadcast_to(rows[:, :1].astype(BF16).astype(F32), none.shape)
    tiles = [rows[:, t * LANES : (t + 1) * LANES] - level for t in range(total // LANES)]
    for to in range(slabs):
        at = to * bins - lead
        tile, shift = at // LANES, at % LANES
        pair = [tiles[t] if 0 <= t < len(tiles) else -level for t in (tile, tile + 1)]
        value = shared_lanes(pair[0], pair[1], shift, lane)
        cut_ref[to] = jnp.where(lane == 0, level, value).astype(BF16)
    slab = lax.axis_index("drift")
    outs[0][...] = cut_ref[slab]
    size = rows.shape[0]
    for s, out in enumerate(outs[1:]):
        for i in range(slabs >> (s + 1)):
            out[i * size : (i + 1) * size] = cut_ref[slab ^ ((2 * i + 1) << s)]


def cut_slabs(keep, received, others, local, bins, slabs, cross, half, before):
    wires, total = local.shape
    rows = sixteens((cross + 1) * (wires + 2 * half))
    steps = slabs.bit_length() - 1
    counts = [1] + [slabs >> (s + 1) for s in range(steps)]
    return pl.pallas_call(
        functools.partial(
            slabs_kernel, bins=bins, lead=WINDOW // 2 - HB, slabs=slabs, cross=cross, half=half
        ),
        out_shape=tuple(jax.ShapeDtypeStruct((n * rows, LANES), BF16) for n in counts),
        in_specs=[vmem()] * (3 + len(others)) + [anywhere()],
        out_specs=(vmem(),) * len(counts),
        scratch_shapes=[pltpu.VMEM((slabs, rows, LANES), BF16)],
        compiler_params=params(),
        cost_estimate=cost(1e8, 4 * rows * total),
        name="slab_currents",
    )(keep, received, *others, local, before)


def pass_kernel(*refs, step, size):
    own_ref, arrived, out_ref = refs[0], refs[1:-1], refs[-1]
    for i in range(own_ref.shape[0] // size):
        here = slice(i * size, (i + 1) * size)
        total = plain(own_ref[here], False)
        for r, other in enumerate(arrived):
            at = ((2 * i + 1) << step) >> (r + 1)
            total += plain(other[at * size : (at + 1) * size], False)
        out_ref[here] = coded(total, WINDOW // 2)


def pass_on(own, arrived, step, size):
    return pl.pallas_call(
        functools.partial(pass_kernel, step=step, size=size),
        out_shape=jax.ShapeDtypeStruct(own.shape, BF16),
        in_specs=[vmem()] * (1 + len(arrived)),
        out_specs=vmem(),
        compiler_params=params(),
        cost_estimate=cost(1e6, 4 * math.prod(own.shape)),
        name="pass_on",
    )(own, *arrived)


def signal_kernel(*refs, wire_taps):
    parts, (table_ref, out_ref, even_ref, odd_ref, level_ref, lines_ref) = refs[:-6], refs[-6:]
    planes, blocks, _, span = table_ref.shape
    _, wires, _ = out_ref.shape
    half = (wire_taps - 1) // 2
    extent = wires + 2 * half
    step = span * 16 // LANES
    middle = WINDOW // 2
    lane = lax.broadcasted_iota(jnp.int32, (wires, LANES), 1)
    size = parts[0].shape[0]
    summed = plain(parts[0][...], False)
    for part in parts[1:]:
        summed += plain(part[:size], False)
    for p in range(planes):
        currents = summed[p * extent : (p + 1) * extent]
        level = currents[:, middle : middle + 1].astype(BF16).astype(F32)
        level = jnp.broadcast_to(level, currents.shape)
        level_ref[p] = level
        currents = currents - level
        levels = jnp.zeros((wires, LANES), F32)
        for a in range(wire_taps):
            at = a
            both = (lane == WINDOW + a) | (lane == WINDOW + wire_taps + a)
            levels = jnp.where(both, level_ref[p, at : at + wires], levels)
        turned = {}
        for block in range(blocks):
            i = p * blocks + block
            turns = [(-step * block) % LANES, (WINDOW - step * block) % LANES]
            for turn in turns:
                if turn not in turned:
                    turned[turn] = (i, len(turned) % 2)
                    target = odd_ref if turned[turn][1] else even_ref
                    target[i] = pltpu.roll(currents, turn, 1) if turn else currents
            (left_at, left_odd), (right_at, right_odd) = turned[turns[0]], turned[turns[1]]
            left_ref = (odd_ref if left_odd else even_ref).at[left_at]
            right_ref = (odd_ref if right_odd else even_ref).at[right_at]
            for pair in range((wire_taps + 1) // 2):
                at = 2 * pair
                right = levels
                if 2 * pair + 1 < wire_taps:
                    right = right_ref[at + 1 : at + 1 + wires]
                line = jnp.where(lane < WINDOW, left_ref[at : at + wires], right)
                lines_ref[i % 2, :, pair * LANES : (pair + 1) * LANES] = line.astype(BF16)
            out_ref[p, :, block * span : (block + 1) * span] = jnp.dot(
                lines_ref[i % 2], table_ref[p, block], preferred_element_type=F32
            ).astype(BF16)


def forward(parts, table, wires, wire_taps):
    planes, blocks, depth, span = table.shape
    extent = wires + wire_taps - 1
    shape = (planes, wires, blocks * span)
    return pl.pallas_call(
        functools.partial(signal_kernel, wire_taps=wire_taps),
        out_shape=jax.ShapeDtypeStruct(shape, BF16),
        in_specs=[vmem()] * (len(parts) + 1),
        out_specs=vmem(),
        scratch_shapes=[
            pltpu.VMEM((planes * blocks, extent, LANES), F32),
            pltpu.VMEM((planes * blocks, extent, LANES), F32),
            pltpu.VMEM((planes, extent, LANES), F32),
            pltpu.VMEM((2, wires, depth), BF16),
        ],
        compiler_params=params(),
        cost_estimate=cost(4e9, 2 * math.prod(table.shape)),
        name="signal",
    )(*parts, table)


def local(charge, intersection, ovl_block, ovl_count, diff_class, response, cotangent):
    total = charge.shape[1]
    owners = lax.axis_size("gz")
    slabs = lax.axis_size("drift")
    planes, wires, ticks = cotangent.shape
    wire_taps = response.shape[1]
    half = (wire_taps - 1) // 2
    bins = total // slabs

    currents, keep, give, local_currents = cut_pieces(
        ovl_block, ovl_count, charge, intersection, cotangent, owners, half
    )
    received = swap(give, "gz", 1)
    sums, edges = relay(keep.astype(F32), received) if owners > 2 else ((), ())
    beyond = [swap(block, "gz", 2 * j) for j, block in enumerate(edges, 1)]
    others = [swap(block, "gz", 2 * j) for j, block in enumerate(sums, 1)]

    levels, kinds = smeared_levels(
        diff_class, response, bins, slabs, sums[0] if sums else received
    )
    table = build_table(levels, kinds, planes, wire_taps, ticks)
    partial, crossing = backward(table, cotangent, received, beyond, wire_taps)
    distance = slabs // 2
    spread = [crossing] + [
        swap(partial if k == distance else crossing, "drift", k) for k in range(1, slabs)
    ]
    held, order = join(partial, spread[distance], 1), [0, distance]
    distance //= 2
    while distance > 1:
        held = join(held, swap(held, "drift", distance), len(order))
        order += [k ^ distance for k in order]
        distance //= 2
    ends = [held, swap(held, "drift", 1)]

    cuts = cut_slabs(
        currents, received, others, local_currents, bins, slabs, planes - 1, half, partial
    )
    windows = [cuts[0]]
    for step, block in enumerate(cuts[1:]):
        if step:
            block = pass_on(block, windows[1:], step, cuts[0].shape[0])
        windows.append(swap(block, "drift", 1 << step))

    count = planes - 1
    *cross, both = merge(spread, bins, total, cuts[0])
    if owners == 4:
        across = [swap(block, "gz", 2) for block in cross]
        sources = [both, swap(both, "gz", 1), *across, *(swap(block, "gz", 1) for block in across)]
        places = [(0, None), (1, None)]
        places += [(2, p) for p in range(count)] + [(3, p) for p in range(count)]
    else:
        sources = [lax.all_gather(block, "gz", axis=0) for block in cross]
        places = [(None, p) for p in range(count)]
    signal = forward(windows, table, wires, wire_taps)
    charge_grad, signal = charge_gradient(
        ovl_block, ovl_count, sources, places, ends, order, intersection, owners, signal, bins, total
    )
    return signal, charge_grad


def solution(mesh):
    return jax.shard_map(
        local,
        mesh=mesh,
        in_specs=(
            P(("apa", "gz", "drift"), None),
            P(("apa", "gz", "drift"), None, None, None, None),
            P(("apa", "gz", "drift"), None, None),
            P(("apa", "gz", "drift"), None),
            P("apa"),
            P(),
            P("apa", "gz", "drift"),
        ),
        out_specs=(P("apa", "gz", "drift"), P(("apa", "gz", "drift"), None)),
        check_vma=False,
    )
```
